32 devices in a mesh: cons: 4 (over y, core), ty: 2 (over x), tx: 4 (over z).
Axes of the slice: x: 2, y: 2, z: 4, core: 2. Of those that a mesh axis runs over, the one named last changes fastest.
Arguments:
- elevation: float32 [8, 2, 288, 2048], P('cons', None, 'ty', 'tx'), may hold values from -6 to 6
- equilibrium: float32 [8, 2, 288, 2048], P('cons', None, 'ty', 'tx'), may hold values from -5 to 5
- depth: float32 [288, 2048], P('ty', 'tx'), may hold values from 0.1 to 1
- land_mask: int32 [288, 2048], P('ty', 'tx'), may hold values 0 or 1
- friction_prev: float32 [288, 2048], P('ty', 'tx'), may hold values from 0.3 to 3
Outputs:
- elevation_out: float32 [8, 2, 288, 2048], P('cons', None, 'ty', 'tx')
- friction: float32 [288, 2048], P('ty', 'tx')
The draws below stay inside these ranges and needn't reach their ends.
All inputs are finite; a program needn't handle non-finite values. No bound on the sum of `land_mask` on one device may be relied on, other than what follows from the above.
Results may differ from the reference program's by a relative error of at most 0.00002.
Values sent between devices are 32-bit elements; how exact they have to be, the bound alone decides.
No kernel may reach another device: no remote copies, remote signals or barrier semaphores. Data moves between devices by JAX's collectives and lax.ppermute only.
A program may use at most 64 MiB of HBM per device.

```python
import math
import jax
import jax.numpy as jnp
from jax import lax

CONS = 8
NY = 288
NX = 2048


def with_ends(values, key, least, high):
    index_at = [jax.random.randint(jax.random.fold_in(key, axis), (), 0, length) for axis, length in enumerate(values.shape)]
    widest = values.shape.index(max(values.shape))
    next_to = index_at[:widest] + [(index_at[widest] + 1) % values.shape[widest]] + index_at[widest + 1:]
    return values.at[tuple(index_at)].set(least).at[tuple(next_to)].set(high)


def block_scale(own_key, dims, cuts, smallest, high):
    def one(position, blocks):
        heights = jax.random.uniform(jax.random.fold_in(jax.random.fold_in(own_key, 6), position), (blocks,), jnp.float32, smallest / len(cuts), high / len(cuts))
        return jnp.repeat(jnp.exp(heights), dims[position] // blocks).reshape((-1,) + (1,) * (len(dims) - position - 1))

    level = one(*cuts[0])
    for cut in cuts[1:]:
        level = level * one(*cut)
    return level


def noise(key, shape, spread, most, pieces=(), held_as=jnp.bfloat16):
    drawn = jax.random.normal(key, shape, jnp.float32) * spread
    if len(pieces) > 0:
        drawn = block_scale(key, shape, pieces, -0.22, 0.18) * drawn
    return jnp.clip(drawn, min=-most, max=most).astype(held_as)


def setup_inputs(seed: int = 0) -> dict:
    key_of = jax.random.split(jax.random.key(seed), 6)
    elevation = noise(key_of[0], (CONS, 2, NY, NX), 1.0, 6.0, ((0, 4), (2, 2), (3, 4)), jnp.float32)
    equilibrium = noise(key_of[1], (CONS, 2, NY, NX), 0.7, 5.0, ((0, 4), (2, 2), (3, 4)), jnp.float32)
    depth = jnp.clip(jnp.exp(math.log(1.0) - 2.3025851 * jax.random.uniform(key_of[2], (NY, NX), jnp.float32) ** block_scale(key_of[2], (NY, NX), ((0, 2), (1, 4)), -0.2, 0.2)), 0.1, 1.0)
    land_mask = with_ends((jax.random.randint(key_of[3], (NY, NX), 0, 5) < 4).astype(jnp.int32), jax.random.fold_in(key_of[3], 1), 0, 1)
    friction_prev = jnp.clip(jnp.exp(math.log(3.0) - 2.3025851 * jax.random.uniform(key_of[4], (NY, NX), jnp.float32) ** block_scale(key_of[4], (NY, NX), ((0, 2), (1, 4)), -0.2, 0.2)), 0.3, 3.0)
    return dict(elevation=elevation, equilibrium=equilibrium, depth=depth, land_mask=land_mask, friction_prev=friction_prev)


OMEGA_TABLE = (1.0, 1.0351, 0.9582, 1.0379, 0.5181, 0.4816, 0.5164, 0.4454)
AY_SCALE = 0.5
THETA = 0.05
DRAG = 0.5
BACKGROUND = 0.01

def east_of(field):
    return jnp.roll(field, -1, axis=-1)

def west_of(field):
    return jnp.roll(field, 1, axis=-1)

def north_of(field):
    return jnp.concatenate([field[..., 1:, :], jnp.zeros_like(field[..., :1, :])], axis=-2)

def south_of(field):
    return jnp.concatenate([jnp.zeros_like(field[..., :1, :]), field[..., :-1, :]], axis=-2)

def latitude_factor(rows, total):
    lat = (-60.0 + 120.0 * (rows.astype(jnp.float32) + 0.5) / total) * (math.pi / 180.0)
    return 0.5 / jnp.cos(lat)

def momentum(num_re, num_im, fric, omega, face_mask):
    denom = fric * fric + omega * omega
    return (face_mask * (num_re * fric + num_im * omega) / denom, face_mask * (num_im * fric - num_re * omega) / denom)

def one_sweep(eta, equil, omega, fric, statics):
    ax_rows, maskf, mu_face, mv_face, hu_face, hv_face, depth = statics
    zeta = eta - equil
    grad_x = ax_rows * (east_of(zeta) - zeta)
    grad_y = AY_SCALE * (north_of(zeta) - zeta)
    fric_u = 0.5 * (fric + east_of(fric))
    fric_v = 0.5 * (fric + north_of(fric))
    u_re, u_im = momentum(-hu_face * grad_x[0], -hu_face * grad_x[1], fric_u, omega, mu_face)
    v_re, v_im = momentum(-hv_face * grad_y[0], -hv_face * grad_y[1], fric_v, omega, mv_face)
    trans_u = jnp.stack([u_re, u_im])
    trans_v = jnp.stack([v_re, v_im])
    west_u = west_of(trans_u)
    south_v = south_of(trans_v)
    div = ax_rows * (trans_u - west_u) + AY_SCALE * (trans_v - south_v)
    res = jnp.stack([-omega * eta[1] + div[0], omega * eta[0] + div[1]])
    eta_new = maskf * (eta - THETA * res)
    cu = 0.5 * (trans_u + west_u)
    cv = 0.5 * (trans_v + south_v)
    term = 0.5 * (cu[0] * cu[0] + cu[1] * cu[1] + cv[0] * cv[0] + cv[1] * cv[1]) / (depth * depth)
    return (eta_new, term)

def reference(elevation, equilibrium, depth, land_mask, friction_prev):
    rows = jnp.arange(NY, dtype=jnp.int32)
    ax_rows = latitude_factor(rows, NY)[:, None]
    maskf = land_mask.astype(jnp.float32)
    mu_face = maskf * east_of(maskf)
    mv_face = maskf * north_of(maskf)
    hu_face = 0.5 * (depth + east_of(depth))
    hv_face = 0.5 * (depth + north_of(depth))
    statics = (ax_rows, maskf, mu_face, mv_face, hu_face, hv_face, depth)
    omegas = jnp.array(OMEGA_TABLE, dtype=jnp.float32)

    def first(carry, item):
        eta, equil, omega = item
        eta_new, term = one_sweep(eta, equil, omega, friction_prev, statics)
        return (carry + term, eta_new)
    variance, eta_one = lax.scan(first, jnp.zeros((NY, NX), jnp.float32), (elevation, equilibrium, omegas))
    friction = DRAG * jnp.sqrt(variance + BACKGROUND) / depth

    def second(carry, item):
        eta, equil, omega = item
        eta_new, term = one_sweep(eta, equil, omega, friction, statics)
        return (carry, eta_new)
    unused, eta_two = lax.scan(second, jnp.zeros((), jnp.float32), (eta_one, equilibrium, omegas))
    return (eta_two, friction)
```

```python
import functools
import math

import jax
import jax.numpy as jnp
from jax import lax
from jax.experimental import pallas as pl
from jax.experimental.pallas import tpu as pltpu
from jax.sharding import PartitionSpec as P

OMEGA_TABLE = (1.0, 1.0351, 0.9582, 1.0379, 0.5181, 0.4816, 0.5164, 0.4454)
AY = 0.5
THETA = 0.05
DRAG = 0.5
BACKGROUND = 0.01
F32 = jnp.float32
LANES = 128
FIELDS = 6
MSG = 4 * FIELDS
TINY_DEPTH = 1e-6
PARAMS = pltpu.CompilerParams(vmem_limit_bytes=16 * 1024 * 1024)


def vmem(x):
    return pltpu.with_memory_space_constraint(x, pltpu.VMEM)


def recip(x):
    return 1.0 / x


def metric(rows, total):
    lat = (rows + 0.5) * (120.0 / total * math.pi / 180.0) - math.pi / 3.0
    s = lat * lat
    acc = jnp.full_like(s, 1.0 / math.factorial(16))
    for n in (14, 12, 10, 8, 6, 4, 2, 0):
        acc = ((-1.0) ** (n // 2)) / math.factorial(n) + s * acc
    return 0.5 / acc


def omegas(kdev):
    index = lax.axis_index("cons")
    out = []
    for c in range(kdev):
        w = jnp.float32(OMEGA_TABLE[c])
        for i in range(1, len(OMEGA_TABLE) // kdev):
            w = jnp.where(index == i, jnp.float32(OMEGA_TABLE[i * kdev + c]), w)
        out.append(w)
    return out


def rolled(x, shift, axis):
    return pltpu.roll(x, shift % x.shape[axis], axis)


def face(zr, zi, zr_next, zi_next, r2, coef, w2):
    g = coef * recip(r2 * r2 + w2 * w2)
    a = g * r2
    b = g * w2
    dr = zr - zr_next
    di = zi - zi_next
    return a * dr + b * di, a * di - b * dr


def pack_kernel(e, q, d, m, r, m1, m2, mn, ms, ec, qc, dc, mc, rc, er, qr, dr, mr, rr, cols, sems):
    _, _, rows, width = e.shape
    copies = []

    def fetch(src, dst):
        copy = pltpu.make_async_copy(src, dst, sems.at[len(copies)])
        copy.start()
        copies.append(copy)

    sides = (slice(0, LANES), slice(width - LANES, width))
    ends = (slice(0, 8), slice(rows - 8, rows))
    for s in range(2):
        for src, dst in ((e, ec), (q, qc)):
            fetch(src.at[:, :, :, sides[s]], dst.at[s])
        for src, dst in ((d, dc), (m, mc), (r, rc)):
            fetch(src.at[:, sides[s]], dst.at[s])
    for s in range(2):
        for src, dst in ((e, er), (q, qr)):
            fetch(src.at[:, :, ends[s], :], dst.at[s])
        for src, dst in ((d, dr), (m, mr), (r, rr)):
            fetch(src.at[ends[s], :], dst.at[s])
    for copy in copies:
        copy.wait()

    lane = lax.broadcasted_iota(jnp.int32, (rows, LANES), 1)
    both = jnp.zeros((rows, LANES), F32)
    for s in range(2):
        planes = [ec[s, c, p] - qc[s, c, p] for p in range(2) for c in range(2)]
        planes += [rc[s], dc[s], mc[s].astype(F32)]
        planes += [ec[s, c, p] for p in range(2) for c in range(2)]
        for k, plane in enumerate(planes):
            at = 32 * s + 2 * k
            shift = at if s == 0 else at - (LANES - 2)
            both = jnp.where((lane == at) | (lane == at + 1), rolled(plane, shift, 1), both)
    pad = -(-rows // LANES) * LANES
    turned = jnp.concatenate([both, jnp.zeros((pad - rows, LANES), F32)], axis=0).T
    for s in range(2):
        at = 32 * s
        near = 0 if s == 0 else 1
        for g in range(2):
            for line in range(2):
                for c in range(2):
                    row = at + 4 * g + 2 * c + line
                    cols[s, 4 * g + 2 * line + c, :] = turned[row, :]
        for g in range(2, 5):
            for line in range(2):
                for c in range(2):
                    cols[s, 4 * g + 2 * line + c, :] = turned[at + 2 * (g + 2) + line, :]
        for c in range(4):
            cols[s, 20 + c, :] = turned[at + 2 * (7 + c) + near, :]
    odd = lax.rem(lax.axis_index("tx"), 2)
    m1[...] = cols[1 - odd]
    m2[...] = cols[odd]

    for s, out in enumerate((ms, mn)):
        base = 0 if s == 0 else 6
        near = 0 if s == 0 else 7
        out[:, width:] = jnp.zeros((MSG, LANES), F32)
        for p in range(2):
            for c in range(2):
                z = er[s, c, p] - qr[s, c, p]
                for line in range(2):
                    out[4 * p + 2 * line + c, :width] = z[base + line, :]
                out[20 + 2 * p + c, :width] = er[s, c, p, near, :]
        for g, plane in ((2, rr[s]), (3, dr[s]), (4, mr[s].astype(F32))):
            for line in range(2):
                for c in range(2):
                    out[4 * g + 2 * line + c, :width] = plane[base + line, :]


def pack(elevation, equilibrium, depth, land_mask, friction):
    kdev, _, rows, width = elevation.shape
    pad = -(-rows // LANES) * LANES
    col = pltpu.VMEM((MSG, pad), F32)
    row = pltpu.VMEM((MSG, width + LANES), F32)
    cut = pltpu.VMEM((2, kdev, 2, rows, LANES), F32)
    cut8 = pltpu.VMEM((2, kdev, 2, 8, width), F32)
    return pl.pallas_call(
        pack_kernel,
        out_shape=(col, col, row, row),
        in_specs=[pl.BlockSpec(memory_space=pltpu.HBM)] * 5,
        out_specs=[pl.BlockSpec(memory_space=pltpu.VMEM)] * 4,
        scratch_shapes=[
            cut,
            cut,
            pltpu.VMEM((2, rows, LANES), F32),
            pltpu.VMEM((2, rows, LANES), jnp.int32),
            pltpu.VMEM((2, rows, LANES), F32),
            cut8,
            cut8,
            pltpu.VMEM((2, 8, width), F32),
            pltpu.VMEM((2, 8, width), jnp.int32),
            pltpu.VMEM((2, 8, width), F32),
            pltpu.VMEM((2, MSG, pad), F32),
            pltpu.SemaphoreType.DMA((20,)),
        ],
        compiler_params=PARAMS,
        name="pack",
    )(elevation, equilibrium, depth, land_mask, friction)


def tile_rows(ref, at, size, nxt):
    here = ref[at : at + size, :]
    after = ref[nxt : nxt + 8, :]
    return here, jnp.concatenate([here[1:], after[0:1]], axis=0)


def east(x):
    return rolled(x, -1, 1)


def row_metric(at, size, width, rows):
    first = lax.axis_index("ty") * rows
    index = lax.broadcasted_iota(jnp.int32, (size, LANES), 0) + (first + at)
    ax = metric(index.astype(F32), rows * lax.axis_size("ty"))
    return ax, jnp.concatenate([ax] * (width // LANES), axis=1)


def first_kernel(e, q, d, m, r, e1, send, keep, var):
    kdev, _, rows, width = e.shape
    size = 16
    ws = omegas(kdev)
    last_v = [jnp.zeros((1, width), F32)] * (2 * kdev)
    for at in range(0, rows, size):
        nxt = min(at + size, rows - 8)
        _, ax = row_metric(at, size, width, rows)
        md, mn = tile_rows(m, at, size, nxt)
        md, mn = md.astype(F32), mn.astype(F32)
        dd, dn = tile_rows(d, at, size, nxt)
        rd, rn = tile_rows(r, at, size, nxt)
        coef_u = (THETA * ax * ax) * (md * east(md) * (dd + east(dd)))
        coef_v = (THETA * AY * AY) * (md * mn * (dd + dn))
        r2u = rd + east(rd)
        r2v = rd + rn
        sum_u = sum_v = None
        for c in range(kdev):
            w2 = 2.0 * ws[c]
            wt = THETA * ws[c]
            er, ern = tile_rows(e.at[c, 0], at, size, nxt)
            ei, ein = tile_rows(e.at[c, 1], at, size, nxt)
            qr, qrn = tile_rows(q.at[c, 0], at, size, nxt)
            qi, qin = tile_rows(q.at[c, 1], at, size, nxt)
            zr, zi = er - qr, ei - qi
            ur, ui = face(zr, zi, east(zr), east(zi), r2u, coef_u, w2)
            vr, vi = face(zr, zi, ern - qrn, ein - qin, r2v, coef_v, w2)
            uwr, uwi = rolled(ur, 1, 1), rolled(ui, 1, 1)
            vsr = jnp.concatenate([last_v[2 * c], vr[:-1]], axis=0)
            vsi = jnp.concatenate([last_v[2 * c + 1], vi[:-1]], axis=0)
            last_v[2 * c], last_v[2 * c + 1] = vr[-1:], vi[-1:]
            e1[c, 0, at : at + size, :] = md * (er + wt * ei - (ur - uwr) - (vr - vsr))
            e1[c, 1, at : at + size, :] = md * (ei - wt * er - (ui - uwi) - (vi - vsi))
            su = (ur + uwr) * (ur + uwr) + (ui + uwi) * (ui + uwi)
            sv = (vr + vsr) * (vr + vsr) + (vi + vsi) * (vi + vsi)
            sum_u = su if sum_u is None else sum_u + su
            sum_v = sv if sum_v is None else sum_v + sv
        inv = recip(dd)
        ia = recip(THETA * ax)
        total = (0.125 * ia * ia) * sum_u + (0.125 / (THETA * AY) ** 2) * sum_v
        var[at : at + size, :] = total * (inv * inv)
    half = rows // 2
    core = lax.rem(lax.axis_index("cons"), 2)
    send[...] = var[pl.ds(pl.multiple_of((1 - core) * half, 8), half), :]
    keep[...] = var[pl.ds(pl.multiple_of(core * half, 8), half), :]


def first_sweep(e, q, d, m, r):
    kdev, _, rows, width = e.shape
    half = pltpu.VMEM((rows // 2, width), F32)
    return pl.pallas_call(
        first_kernel,
        out_shape=(pltpu.VMEM(e.shape, F32), half, half),
        in_specs=[pl.BlockSpec(memory_space=pltpu.VMEM)] * 5,
        out_specs=[pl.BlockSpec(memory_space=pltpu.VMEM)] * 3,
        scratch_shapes=[pltpu.VMEM((rows, width), F32)],
        compiler_params=PARAMS,
        name="first_sweep",
    )(vmem(e), vmem(q), vmem(d), vmem(m), vmem(r))


def roles(a, b):
    even = lax.rem(lax.axis_index("tx"), 2) == 0
    return jnp.where(even, b, a), jnp.where(even, a, b)


def merge_kernel(rows, f1, f2, mn, ms, mn_out, ms_out, my_out):
    width = mn.shape[1] - LANES
    fw, fe = roles(f1[...], f2[...])
    block = (rows - 1) // LANES * LANES
    lane = lax.broadcasted_iota(jnp.int32, (MSG, LANES), 1)
    in_block = rows - 1 - block
    fe_last = rolled(rolled(fe[:, block : block + LANES], -in_block, 1), 2, 0)
    fw_last = rolled(fw[:, block : block + LANES], LANES - 1 - in_block, 1)
    fe_first = fe[:, :LANES]
    fw_first = rolled(rolled(fw[:, :LANES], LANES - 1, 1), -2, 0)
    n_end = jnp.where(lane == 0, fe_last, jnp.where(lane == LANES - 1, fw_last, 0.0))
    s_end = jnp.where(lane == 0, fe_first, jnp.where(lane == LANES - 1, fw_first, 0.0))
    mn_out[:, :width] = mn[:, :width]
    ms_out[:, :width] = ms[:, :width]
    mn_out[:, width:] = n_end
    ms_out[:, width:] = s_end
    low = lax.axis_index("ty") == 0
    my_out[...] = jnp.where(low, mn_out[...], ms_out[...])


def merge(rows, f1, f2, mn, ms):
    out = pltpu.VMEM(mn.shape, F32)
    return pl.pallas_call(
        functools.partial(merge_kernel, rows),
        out_shape=(out, out, out),
        in_specs=[pl.BlockSpec(memory_space=pltpu.VMEM)] * 4,
        out_specs=[pl.BlockSpec(memory_space=pltpu.VMEM)] * 3,
        compiler_params=PARAMS,
        name="merge",
    )(*map(vmem, (f1, f2, mn, ms)))


def strip_omega(shape, ws):
    odd = lax.rem(lax.broadcasted_iota(jnp.int32, shape, 0), 2)
    return jnp.where(odd == 0, ws[0], ws[1])


def strip_sweep(low, high, ws, g_across, g_along):
    field = [jnp.concatenate([low[4 * g : 4 * g + 4], high[4 * g : 4 * g + 4]], axis=0) for g in range(5)]
    zr, zi, r, d, m = field
    none = jnp.zeros((2, low.shape[1]), F32)
    er = jnp.concatenate([none, low[20:22], high[20:22], none], axis=0)
    ei = jnp.concatenate([none, low[22:24], high[22:24], none], axis=0)
    w = strip_omega(zr.shape, ws)
    w2 = 2.0 * w
    wt = THETA * w
    up = lambda x: rolled(x, -2, 0)
    nx = lambda x: rolled(x, -1, 1)
    coef_a = (THETA * g_across * g_across) * (m * up(m) * (d + up(d)))
    coef_l = (THETA * g_along * g_along) * (m * nx(m) * (d + nx(d)))
    ar, ai = face(zr, zi, up(zr), up(zi), r + up(r), coef_a, w2)
    lr, li = face(zr, zi, nx(zr), nx(zi), r + nx(r), coef_l, w2)
    abr, abi = rolled(ar, 2, 0), rolled(ai, 2, 0)
    lbr, lbi = rolled(lr, 1, 1), rolled(li, 1, 1)
    e1r = m * (er + wt * ei - (ar - abr) - (lr - lbr))
    e1i = m * (ei - wt * er - (ai - abi) - (li - lbi))
    sa = (ar + abr) * (ar + abr) + (ai + abi) * (ai + abi)
    sl = (lr + lbr) * (lr + lbr) + (li + lbi) * (li + lbi)
    inv = recip(jnp.maximum(d, TINY_DEPTH))
    ia = recip(THETA * g_across)
    il = recip(THETA * g_along)
    var = 0.125 * (ia * ia * sa + il * il * sl) * (inv * inv)
    var = var + rolled(var, -1, 0)
    z1r = e1r - (er - zr)
    z1i = e1i - (ei - zi)
    return (z1r, z1i, d, coef_a, e1r, e1i), var


def rim_kernel(rows, m1, m2, f1, f2, mn, ms, fn_ref, fs_ref, recv, keep, s_out, n_out, w_out, e_out, sums):
    kdev = 2
    width = mn.shape[1] - LANES
    pad = m1.shape[1]
    ws = omegas(kdev)
    ty, count = lax.axis_index("ty"), lax.axis_size("ty")
    first = (ty * rows).astype(F32)
    total = rows * count
    fn = jnp.where(ty < count - 1, fn_ref[...], 0.0)
    fs = jnp.where(ty > 0, fs_ref[...], 0.0)
    half = keep.shape[0]
    sums[:half, :] = recv[...] + keep[...]

    ay = jnp.float32(AY)
    line = lax.broadcasted_iota(jnp.int32, (8, LANES), 0) // 2
    for low, high, start, out, at in ((fs, ms[...], -2, s_out, 0), (mn[...], fn, rows - 2, n_out, 2)):
        ax = metric((line + start).astype(F32) + first, total)
        ax = jnp.concatenate([ax] * (low.shape[1] // LANES), axis=1)
        held, var = strip_sweep(low, high, ws, ay, ax)
        for k, x in enumerate(held):
            out[8 * k : 8 * k + 8, :] = x
        for p in range(2):
            sums[half + at + p, :] = var[2 + 2 * p, :width]

    mw, me = roles(m1[...], m2[...])
    fw, fe = roles(f1[...], f2[...])
    mw, me, fw, fe = mw, me, fw, fe
    hi = rows - (pad - LANES)
    lane = lax.broadcasted_iota(jnp.int32, (MSG, LANES), 1)
    fn_end, fn_lo, fn_hi = fn[:, width:], fn[:, :LANES], fn[:, width - LANES : width]
    fs_end, fs_lo, fs_hi = fs[:, width:], fs[:, :LANES], fs[:, width - LANES : width]
    down = lambda x: rolled(x, 2, 0)
    up = lambda x: rolled(x, -2, 0)

    def ended(msg, north, north_lane, south, south_lane):
        block = msg[:, pad - LANES :]
        block = jnp.where(lane == hi, rolled(north, hi - north_lane, 1), block)
        block = jnp.where(lane == LANES - 1, rolled(south, LANES - 1 - south_lane, 1), block)
        return jnp.concatenate([msg[:, : pad - LANES], block], axis=1)

    last = LANES - 1
    low_w = ended(fw, down(fn_end), last, fs_end, last)
    high_w = ended(mw, fn_lo, 0, up(fs_lo), 0)
    low_e = ended(me, down(fn_hi), last, fs_hi, last)
    high_e = ended(fe, fn_end, 0, up(fs_end), 0)
    row = lax.broadcasted_iota(jnp.int32, (8, pad), 1).astype(F32) + first
    ax = metric(jnp.minimum(row, first + rows), total)
    for low, high, out, at in ((low_w, high_w, w_out, 4), (low_e, high_e, e_out, 5)):
        held, var = strip_sweep(low, high, ws, ax, ay)
        for k, x in enumerate(held):
            out[8 * k : 8 * k + 8, :] = x
        for p in range(2):
            sums[half + at, p * pad : (p + 1) * pad] = var[2 + 2 * p, :]
    sums[half + 6 :, :] = jnp.zeros((2, width), F32)


def rim(rows, m1, m2, f1, f2, mn, ms, fn, fs, recv, keep):
    row = pltpu.VMEM((48, mn.shape[1]), F32)
    col = pltpu.VMEM((48, m1.shape[1]), F32)
    sums = pltpu.VMEM((keep.shape[0] + 8, keep.shape[1]), F32)
    return pl.pallas_call(
        functools.partial(rim_kernel, rows),
        out_shape=(row, row, col, col, sums),
        in_specs=[pl.BlockSpec(memory_space=pltpu.VMEM)] * 10,
        out_specs=[pl.BlockSpec(memory_space=pltpu.VMEM)] * 5,
        compiler_params=PARAMS,
        name="rim",
    )(*map(vmem, (m1, m2, f1, f2, mn, ms, fn, fs, recv, keep)))


def rate(var, d):
    return DRAG * jnp.sqrt(var + BACKGROUND) / d


def second_kernel(e1, q, d, m, mine, other, ss, sn, sw, se, eta, fric, cols):
    kdev, _, rows, width = e1.shape
    pad = sw.shape[1]
    size = 16
    ws = omegas(kdev)
    half = rows // 2
    core = lax.rem(lax.axis_index("cons"), 2)
    fric[pl.ds(pl.multiple_of(core * half, 8), half), :] = mine[:half, :]
    fric[pl.ds(pl.multiple_of((1 - core) * half, 8), half), :] = other[:half, :]
    rims = mine[half:, :] + other[half:, :]

    def edge(strip, var_a, var_b):
        zr, zi, dep, coef = (strip[8 * k : 8 * k + 8, :] for k in range(4))
        var = jnp.concatenate([var_a, var_a, var_a, var_a, var_b, var_b, var_b, var_b], axis=0)
        f = rate(var, jnp.maximum(dep, TINY_DEPTH))
        up = lambda x: rolled(x, -2, 0)
        w2 = 2.0 * strip_omega(zr.shape, ws)
        return face(zr, zi, up(zr), up(zi), f + up(f), coef, w2)

    none = jnp.zeros((1, LANES), F32)
    wide = lambda x: jnp.concatenate([x, none], axis=1)
    south = edge(ss, wide(rims[0:1]), wide(rims[1:2]))
    north = edge(sn, wide(rims[2:3]), wide(rims[3:4]))
    west = edge(sw, rims[4:5, :pad], rims[4:5, pad : 2 * pad])
    east_ = edge(se, rims[5:6, :pad], rims[5:6, pad : 2 * pad])

    for p in range(2):
        cols[2 * p : 2 * p + 2, :] = west[p][2:4]
        cols[4 + 2 * p : 6 + 2 * p, :] = east_[p][2:4]
        cols[8 + 2 * p : 10 + 2 * p, :] = sw[8 * (4 + p) + 4 : 8 * (4 + p) + 6, :]
        cols[12 + 2 * p : 14 + 2 * p, :] = se[8 * (4 + p) + 2 : 8 * (4 + p) + 4, :]
    cols[16:17, :] = rims[4:5, pad : 2 * pad]
    cols[17:18, :] = rims[5:6, :pad]
    turned = cols[...].T

    lane = lax.broadcasted_iota(jnp.int32, (rows, LANES), 1)

    def patched(block, k, at):
        return jnp.where(lane == at, rolled(turned[:rows], at - k, 1), block)

    left, right = slice(0, LANES), slice(width - LANES, width)
    last = LANES - 1
    for p in range(2):
        for c in range(kdev):
            e1[c, p, 0:1, :] = ss[8 * (4 + p) + 4 + c : 8 * (4 + p) + 5 + c, :width]
            e1[c, p, rows - 1 : rows, :] = sn[8 * (4 + p) + 2 + c : 8 * (4 + p) + 3 + c, :width]
            e1[c, p, :, left] = patched(e1[c, p, :, left], 8 + 2 * p + c, 0)
            e1[c, p, :, right] = patched(e1[c, p, :, right], 12 + 2 * p + c, last)
    fric[0:1, :] = rims[1:2]
    fric[rows - 1 : rows, :] = rims[2:3]
    fric[:, left] = patched(fric[:, left], 16, 0)
    fric[:, right] = patched(fric[:, right], 17, last)
    for at in range(0, rows, size):
        fric[at : at + size, :] = rate(fric[at : at + size, :], d[at : at + size, :])

    lane = lax.broadcasted_iota(jnp.int32, (size, LANES), 1)
    last_v = [None] * (2 * kdev)
    for c in range(kdev):
        for p in range(2):
            last_v[2 * c + p] = south[p][2 + c : 3 + c, :width]
    for at in range(0, rows, size):
        nxt = min(at + size, rows - 8)
        _, ax = row_metric(at, size, width, rows)
        edges = turned[at : at + size]
        md, mn = tile_rows(m, at, size, nxt)
        md, mn = md.astype(F32), mn.astype(F32)
        dd, dn = tile_rows(d, at, size, nxt)
        rd, rn = tile_rows(fric, at, size, nxt)
        coef_u = (THETA * ax * ax) * (md * east(md) * (dd + east(dd)))
        coef_v = (THETA * AY * AY) * (md * mn * (dd + dn))
        r2u = rd + east(rd)
        r2v = rd + rn

        def with_east(u, k):
            block = jnp.where(lane == last, rolled(edges, last - k, 1), u[:, right])
            return jnp.concatenate([u[:, : width - LANES], block], axis=1)

        def from_west(u, k):
            u = rolled(u, 1, 1)
            block = jnp.where(lane == 0, rolled(edges, -k, 1), u[:, left])
            return jnp.concatenate([block, u[:, LANES:]], axis=1)

        for c in range(kdev):
            w2 = 2.0 * ws[c]
            wt = THETA * ws[c]
            er, ern = tile_rows(e1.at[c, 0], at, size, nxt)
            ei, ein = tile_rows(e1.at[c, 1], at, size, nxt)
            qr, qrn = tile_rows(q.at[c, 0], at, size, nxt)
            qi, qin = tile_rows(q.at[c, 1], at, size, nxt)
            zr, zi = er - qr, ei - qi
            ur, ui = face(zr, zi, east(zr), east(zi), r2u, coef_u, w2)
            vr, vi = face(zr, zi, ern - qrn, ein - qin, r2v, coef_v, w2)
            ur, ui = with_east(ur, 4 + c), with_east(ui, 6 + c)
            if at + size == rows:
                vr = jnp.concatenate([vr[:-1], north[0][2 + c : 3 + c, :width]], axis=0)
                vi = jnp.concatenate([vi[:-1], north[1][2 + c : 3 + c, :width]], axis=0)
            uwr, uwi = from_west(ur, c), from_west(ui, 2 + c)
            vsr = jnp.concatenate([last_v[2 * c], vr[:-1]], axis=0)
            vsi = jnp.concatenate([last_v[2 * c + 1], vi[:-1]], axis=0)
            last_v[2 * c], last_v[2 * c + 1] = vr[-1:], vi[-1:]
            eta[c, 0, at : at + size, :] = md * (er + wt * ei - (ur - uwr) - (vr - vsr))
            eta[c, 1, at : at + size, :] = md * (ei - wt * er - (ui - uwi) - (vi - vsi))


def second_kernel_copy(e1_in, q, d, m, mine, other, ss, sn, sw, se, eta, fric, e1, cols):
    e1[...] = e1_in[...]
    second_kernel(e1, q, d, m, mine, other, ss, sn, sw, se, eta, fric, cols)


def second_sweep(e1, q, d, m, mine, other, ss, sn, sw, se):
    kdev, _, rows, width = e1.shape
    return pl.pallas_call(
        second_kernel_copy,
        out_shape=(jax.ShapeDtypeStruct(e1.shape, F32), jax.ShapeDtypeStruct(d.shape, F32)),
        in_specs=[pl.BlockSpec(memory_space=pltpu.VMEM)] * 10,
        out_specs=[pl.BlockSpec(memory_space=pltpu.VMEM)] * 2,
        scratch_shapes=[pltpu.VMEM(e1.shape, F32), pltpu.VMEM((LANES, sw.shape[1]), F32)],
        compiler_params=PARAMS,
        name="second_sweep",
    )(*map(vmem, (e1, q, d, m, mine, other, ss, sn, sw, se)))


def swapped(x, axis, bit):
    return lax.ppermute(x, axis, [(i, i ^ bit) for i in range(lax.axis_size(axis))])


def body(elevation, equilibrium, depth, land_mask, friction_prev):
    rows = depth.shape[0]
    ntx, nty, ncons = (lax.axis_size(a) for a in ("tx", "ty", "cons"))
    m1, m2, mn, ms = pack(elevation, equilibrium, depth, land_mask, friction_prev)
    f2 = lax.ppermute(m2, "tx", [(i, (i - 1 if i % 2 == 0 else i + 1) % ntx) for i in range(ntx)])
    f1 = swapped(m1, "tx", 1)
    e1, send, keep = first_sweep(elevation, equilibrium, depth, land_mask, friction_prev)
    recv = swapped(send, "cons", 1)
    mn, ms, my = merge(rows, f1, f2, mn, ms)
    if nty == 2:
        fn = fs = swapped(my, "ty", 1)
    else:
        fn = lax.ppermute(ms, "ty", [(i, i - 1) for i in range(1, nty)])
        fs = lax.ppermute(mn, "ty", [(i, i + 1) for i in range(nty - 1)])
    ss, sn, sw, se, sums = rim(rows, m1, m2, f1, f2, mn, ms, fn, fs, recv, keep)
    bit = 2
    while bit < ncons:
        sums = sums + swapped(sums, "cons", bit)
        bit *= 2
    other = swapped(sums, "cons", 1)
    return second_sweep(e1, equilibrium, depth, land_mask, sums, other, ss, sn, sw, se)


def solution(mesh):
    return jax.shard_map(
        body,
        mesh=mesh,
        in_specs=(
            P("cons", None, "ty", "tx"),
            P("cons", None, "ty", "tx"),
            P("ty", "tx"),
            P("ty", "tx"),
            P("ty", "tx"),
        ),
        out_specs=(P("cons", None, "ty", "tx"), P("ty", "tx")),
        check_vma=False,
    )
```

```python
import functools
import math

import jax
import jax.numpy as jnp
from jax import lax
from jax.experimental import pallas as pl
from jax.experimental.pallas import tpu as pltpu
from jax.sharding import PartitionSpec as P

OMEGA_TABLE = (1.0, 1.0351, 0.9582, 1.0379, 0.5181, 0.4816, 0.5164, 0.4454)
AY = 0.5
THETA = 0.05
DRAG = 0.5
BACKGROUND = 0.01
F32 = jnp.float32
LANES = 128
FIELDS = 6
MSG = 4 * FIELDS
TINY_DEPTH = 1e-6
PARAMS = pltpu.CompilerParams(vmem_limit_bytes=16 * 1024 * 1024)


def vmem(x):
    return pltpu.with_memory_space_constraint(x, pltpu.VMEM)


def hbm(x):
    return pltpu.with_memory_space_constraint(x, pltpu.HBM)


def recip(x):
    return pl.reciprocal(x, approx=True) if jnp.ndim(x) else 1.0 / x


def metric(rows, total):
    lat = (rows + 0.5) * (120.0 / total * math.pi / 180.0) - math.pi / 3.0
    s = lat * lat
    acc = jnp.full_like(s, 1.0 / math.factorial(16))
    for n in (14, 12, 10, 8, 6, 4, 2, 0):
        acc = ((-1.0) ** (n // 2)) / math.factorial(n) + s * acc
    return 0.5 / acc


def omegas(kdev):
    index = lax.axis_index("cons")
    out = []
    for c in range(kdev):
        w = jnp.float32(OMEGA_TABLE[c])
        for i in range(1, len(OMEGA_TABLE) // kdev):
            w = jnp.where(index == i, jnp.float32(OMEGA_TABLE[i * kdev + c]), w)
        out.append(w)
    return out


def rolled(x, shift, axis):
    return pltpu.roll(x, shift % x.shape[axis], axis)


def face(zr, zi, zr_next, zi_next, r2, coef, w2):
    g = coef * recip(r2 * r2 + w2 * w2)
    a = g * r2
    b = g * w2
    dr = zr - zr_next
    di = zi - zi_next
    return a * dr + b * di, a * di - b * dr


def flux(dr, di, g, a, w2):
    b = g * w2
    return a * dr + b * di, a * di - b * dr


def pack_kernel(e_in, q_in, d_in, m_in, r_in, e, q, d, m, r, m2, m1, mn, ms, ints, cols, sems):
    kdev, _, rows, width = e.shape
    copies = []

    def fetch(src, dst):
        copy = pltpu.make_async_copy(src, dst, sems.at[len(copies)])
        copy.start()
        copies.append(copy)

    for src, dst in ((d_in, d), (m_in, ints), (r_in, r)):
        fetch(src, dst)
    for c in range(kdev):
        for p in range(2):
            fetch(e_in.at[c, p], e.at[c, p])
            fetch(q_in.at[c, p], q.at[c, p])
    for copy in copies[:3]:
        copy.wait()
    m[...] = ints[...].astype(F32)
    for copy in copies[3:]:
        copy.wait()
    sides = (slice(0, LANES), slice(width - LANES, width))
    ends = (slice(0, 8), slice(rows - 8, rows))

    lane = lax.broadcasted_iota(jnp.int32, (rows, LANES), 1)
    both = jnp.zeros((rows, LANES), F32)
    for s in range(2):
        side = sides[s]
        planes = [e[c, p, :, side] - q[c, p, :, side] for p in range(2) for c in range(2)]
        planes += [r[:, side], d[:, side], m[:, side]]
        planes += [e[c, p, :, side] for p in range(2) for c in range(2)]
        for k, plane in enumerate(planes):
            at = 32 * s + 2 * k
            shift = at if s == 0 else at - (LANES - 2)
            both = jnp.where((lane == at) | (lane == at + 1), rolled(plane, shift, 1), both)
    pad = -(-rows // LANES) * LANES
    turned = jnp.concatenate([both, jnp.zeros((pad - rows, LANES), F32)], axis=0).T
    for s in range(2):
        at = 32 * s
        near = 0 if s == 0 else 1
        for g in range(2):
            for line in range(2):
                for c in range(2):
                    row = at + 4 * g + 2 * c + line
                    cols[s, 4 * g + 2 * line + c, :] = turned[row, :]
        for g in range(2, 5):
            for line in range(2):
                for c in range(2):
                    cols[s, 4 * g + 2 * line + c, :] = turned[at + 2 * (g + 2) + line, :]
        for c in range(4):
            cols[s, 20 + c, :] = turned[at + 2 * (7 + c) + near, :]
    odd = lax.rem(lax.axis_index("tx"), 2)
    m1[...] = cols[1 - odd]
    m2[:MSG, :] = cols[odd]
    m2[MSG:, :] = jnp.zeros((m2.shape[0] - MSG, m2.shape[1]), F32)

    for s, out in enumerate((ms, mn)):
        base = 0 if s == 0 else 6
        near = 0 if s == 0 else 7
        out[:, width:] = jnp.zeros((MSG, LANES), F32)
        for p in range(2):
            for c in range(2):
                line8 = e[c, p, ends[s], :]
                z = line8 - q[c, p, ends[s], :]
                for line in range(2):
                    out[4 * p + 2 * line + c, :width] = z[base + line, :]
                out[20 + 2 * p + c, :width] = line8[near, :]
        for g, plane in ((2, r[ends[s], :]), (3, d[ends[s], :]), (4, m[ends[s], :])):
            for line in range(2):
                for c in range(2):
                    out[4 * g + 2 * line + c, :width] = plane[base + line, :]


def pack(elevation, equilibrium, depth, land_mask, friction):
    kdev, _, rows, width = elevation.shape
    pad = -(-rows // LANES) * LANES
    field, plane = pltpu.VMEM(elevation.shape, F32), pltpu.VMEM(depth.shape, F32)
    row = pltpu.VMEM((MSG, width + LANES), F32)
    return pl.pallas_call(
        pack_kernel,
        out_shape=(field, field, plane, plane, plane, pltpu.VMEM((MSG + 8, pad), F32), pltpu.VMEM((MSG, pad), F32), row, row),
        in_specs=[pl.BlockSpec(memory_space=pltpu.HBM)] * 5,
        out_specs=[pl.BlockSpec(memory_space=pltpu.VMEM)] * 9,
        scratch_shapes=[
            pltpu.VMEM(depth.shape, jnp.int32),
            pltpu.VMEM((2, MSG, pad), F32),
            pltpu.SemaphoreType.DMA((3 + 4 * kdev,)),
        ],
        compiler_params=PARAMS,
        name="pack",
    )(*map(hbm, (elevation, equilibrium, depth, land_mask, friction)))


def tile_rows(ref, at, size, nxt):
    here = ref[at : at + size, :]
    after = ref[nxt : nxt + 8, :]
    return here, jnp.concatenate([here[1:], after[0:1]], axis=0)


def east(x):
    return rolled(x, -1, 1)


def row_metric(at, size, width, rows):
    first = lax.axis_index("ty") * rows
    index = lax.broadcasted_iota(jnp.int32, (size, LANES), 0) + (first + at)
    ax = metric(index.astype(F32), rows * lax.axis_size("ty"))
    return ax, jnp.concatenate([ax] * (width // LANES), axis=1)


def first_kernel(e, q, d, mask, r, after, e1, send, keep, var):
    del after
    kdev, _, rows, width = e.shape
    size = 16
    ws = omegas(kdev)
    last_v = [jnp.zeros((1, width), F32)] * (2 * kdev)
    for at in range(0, rows, size):
        nxt = min(at + size, rows - 8)
        _, ax = row_metric(at, size, width, rows)
        md, mn = tile_rows(mask, at, size, nxt)
        dd, dn = tile_rows(d, at, size, nxt)
        rd, rn = tile_rows(r, at, size, nxt)
        coef_u = (THETA * ax * ax) * (md * east(md) * (dd + east(dd)))
        coef_v = (THETA * AY * AY) * (md * mn * (dd + dn))
        r2u = rd + east(rd)
        r2v = rd + rn
        squ, sqv = r2u * r2u, r2v * r2v
        sum_u = sum_v = None
        for c in range(kdev):
            w2 = 2.0 * ws[c]
            wt = THETA * ws[c]
            er, ern = tile_rows(e.at[c, 0], at, size, nxt)
            ei, ein = tile_rows(e.at[c, 1], at, size, nxt)
            qr, qrn = tile_rows(q.at[c, 0], at, size, nxt)
            qi, qin = tile_rows(q.at[c, 1], at, size, nxt)
            zr, zi = er - qr, ei - qi
            gu = coef_u * recip(squ + w2 * w2)
            gv = coef_v * recip(sqv + w2 * w2)
            ur, ui = flux(zr - east(zr), zi - east(zi), gu, gu * r2u, w2)
            vr, vi = flux(zr - (ern - qrn), zi - (ein - qin), gv, gv * r2v, w2)
            uwr, uwi = rolled(ur, 1, 1), rolled(ui, 1, 1)
            vsr = jnp.concatenate([last_v[2 * c], vr[:-1]], axis=0)
            vsi = jnp.concatenate([last_v[2 * c + 1], vi[:-1]], axis=0)
            last_v[2 * c], last_v[2 * c + 1] = vr[-1:], vi[-1:]
            e1[c, 0, at : at + size, :] = md * (er + wt * ei - (ur - uwr) - (vr - vsr))
            e1[c, 1, at : at + size, :] = md * (ei - wt * er - (ui - uwi) - (vi - vsi))
            su = (ur + uwr) * (ur + uwr) + (ui + uwi) * (ui + uwi)
            sv = (vr + vsr) * (vr + vsr) + (vi + vsi) * (vi + vsi)
            sum_u = su if sum_u is None else sum_u + su
            sum_v = sv if sum_v is None else sum_v + sv
        inv = recip(dd)
        ia = recip(THETA * ax)
        total = (0.125 * ia * ia) * sum_u + (0.125 / (THETA * AY) ** 2) * sum_v
        var[at : at + size, :] = total * (inv * inv)
    half = rows // 2
    core = lax.rem(lax.axis_index("cons"), 2)
    send[...] = var[pl.ds(pl.multiple_of((1 - core) * half, 8), half), :]
    keep[...] = var[pl.ds(pl.multiple_of(core * half, 8), half), :]


def first_sweep(e, q, d, m, r, after):
    kdev, _, rows, width = e.shape
    half = pltpu.VMEM((rows // 2, width), F32)
    return pl.pallas_call(
        first_kernel,
        out_shape=(pltpu.VMEM(e.shape, F32), half, half),
        in_specs=[pl.BlockSpec(memory_space=pltpu.VMEM)] * 6,
        out_specs=[pl.BlockSpec(memory_space=pltpu.VMEM)] * 3,
        scratch_shapes=[pltpu.VMEM(d.shape, F32)],
        compiler_params=PARAMS,
        cost_estimate=pl.CostEstimate(flops=80 * e.size, bytes_accessed=160 * e.size, transcendentals=0),
        name="first_sweep",
    )(*map(vmem, (e, q, d, m, r, after)))


def add_kernel(a, b, *refs):
    refs[-1][...] = a[...] + b[...]


def added(a, b, *after):
    return pl.pallas_call(
        add_kernel,
        out_shape=pltpu.VMEM(a.shape, F32),
        in_specs=[pl.BlockSpec(memory_space=pltpu.VMEM)] * (2 + len(after)),
        out_specs=pl.BlockSpec(memory_space=pltpu.VMEM),
        compiler_params=PARAMS,
        name="added",
    )(vmem(a), vmem(b), *map(vmem, after))


def halves_kernel(a, b, after, left, right):
    del after
    cut = left.shape[1]
    left[...] = a[:, :cut] + b[:, :cut]
    right[...] = a[:, cut:] + b[:, cut:]


def halves(a, b, after):
    part = pltpu.VMEM((a.shape[0], a.shape[1] // 2), F32)
    return pl.pallas_call(
        halves_kernel,
        out_shape=(part, part),
        in_specs=[pl.BlockSpec(memory_space=pltpu.VMEM)] * 3,
        out_specs=[pl.BlockSpec(memory_space=pltpu.VMEM)] * 2,
        compiler_params=PARAMS,
        name="halves",
    )(vmem(a), vmem(b), vmem(after))


def join_kernel(after, *refs):
    del after
    out = refs[-1]
    rows, cut = refs[0].shape
    for k, at in enumerate((slice(0, cut), slice(cut, 2 * cut))):
        out[:rows, at] = functools.reduce(jnp.add, [ref[...] for ref in refs[k:-1:3]])
    out[rows:, :] = functools.reduce(jnp.add, [ref[...] for ref in refs[2:-1:3]])


def joined(parts, after):
    (rows, cut), rims = parts[0][0].shape, parts[0][2].shape[0]
    flat = [x for part in parts for x in part]
    return pl.pallas_call(
        join_kernel,
        out_shape=pltpu.VMEM((rows + rims, 2 * cut), F32),
        in_specs=[pl.BlockSpec(memory_space=pltpu.VMEM)] * (1 + len(flat)),
        out_specs=pl.BlockSpec(memory_space=pltpu.VMEM),
        compiler_params=PARAMS,
        name="joined",
    )(*map(vmem, (after, *flat)))


def roles(a, b):
    even = lax.rem(lax.axis_index("tx"), 2) == 0
    return jnp.where(even, b, a), jnp.where(even, a, b)


def merge_kernel(rows, f2, f1, mn, ms, send, mn_out, ms_out, my_out, send_out):
    width = mn.shape[1] - LANES
    fw, fe = roles(f1[...], f2[:MSG, :])
    block = (rows - 1) // LANES * LANES
    lane = lax.broadcasted_iota(jnp.int32, (MSG, LANES), 1)
    in_block = rows - 1 - block
    fe_last = rolled(rolled(fe[:, block : block + LANES], -in_block, 1), 2, 0)
    fw_last = rolled(fw[:, block : block + LANES], LANES - 1 - in_block, 1)
    fe_first = fe[:, :LANES]
    fw_first = rolled(rolled(fw[:, :LANES], LANES - 1, 1), -2, 0)
    n_end = jnp.where(lane == 0, fe_last, jnp.where(lane == LANES - 1, fw_last, 0.0))
    s_end = jnp.where(lane == 0, fe_first, jnp.where(lane == LANES - 1, fw_first, 0.0))
    mn_out[:, :width] = mn[:, :width]
    ms_out[:, :width] = ms[:, :width]
    mn_out[:, width:] = n_end
    ms_out[:, width:] = s_end
    low = lax.axis_index("ty") == 0
    my_out[:MSG, :] = jnp.where(low, mn_out[...], ms_out[...])
    my_out[MSG:, :] = jnp.zeros((my_out.shape[0] - MSG, my_out.shape[1]), F32)
    send_out[...] = send[...]


def merge(rows, f1, f2, mn, ms, send):
    out = pltpu.VMEM(mn.shape, F32)
    return pl.pallas_call(
        functools.partial(merge_kernel, rows),
        out_shape=(out, out, pltpu.VMEM((MSG + 8, mn.shape[1]), F32), pltpu.VMEM(send.shape, F32)),
        in_specs=[pl.BlockSpec(memory_space=pltpu.VMEM)] * 5,
        out_specs=[pl.BlockSpec(memory_space=pltpu.VMEM)] * 4,
        compiler_params=PARAMS,
        name="merge",
    )(*map(vmem, (f2, f1, mn, ms, send)))


def strip_omega(shape, ws):
    odd = lax.rem(lax.broadcasted_iota(jnp.int32, shape, 0), 2)
    return jnp.where(odd == 0, ws[0], ws[1])


def strip_sweep(low, high, ws, g_across, g_along):
    field = [jnp.concatenate([low[4 * g : 4 * g + 4], high[4 * g : 4 * g + 4]], axis=0) for g in range(5)]
    zr, zi, r, d, m = field
    none = jnp.zeros((2, low.shape[1]), F32)
    er = jnp.concatenate([none, low[20:22], high[20:22], none], axis=0)
    ei = jnp.concatenate([none, low[22:24], high[22:24], none], axis=0)
    w = strip_omega(zr.shape, ws)
    w2 = 2.0 * w
    wt = THETA * w
    up = lambda x: rolled(x, -2, 0)
    nx = lambda x: rolled(x, -1, 1)
    coef_a = (THETA * g_across * g_across) * (m * up(m) * (d + up(d)))
    coef_l = (THETA * g_along * g_along) * (m * nx(m) * (d + nx(d)))
    ar, ai = face(zr, zi, up(zr), up(zi), r + up(r), coef_a, w2)
    lr, li = face(zr, zi, nx(zr), nx(zi), r + nx(r), coef_l, w2)
    abr, abi = rolled(ar, 2, 0), rolled(ai, 2, 0)
    lbr, lbi = rolled(lr, 1, 1), rolled(li, 1, 1)
    e1r = m * (er + wt * ei - (ar - abr) - (lr - lbr))
    e1i = m * (ei - wt * er - (ai - abi) - (li - lbi))
    sa = (ar + abr) * (ar + abr) + (ai + abi) * (ai + abi)
    sl = (lr + lbr) * (lr + lbr) + (li + lbi) * (li + lbi)
    inv = recip(jnp.maximum(d, TINY_DEPTH))
    ia = recip(THETA * g_across)
    il = recip(THETA * g_along)
    var = 0.125 * (ia * ia * sa + il * il * sl) * (inv * inv)
    var = var + rolled(var, -1, 0)
    z1r = e1r - (er - zr)
    z1i = e1i - (ei - zi)
    return (z1r, z1i, d, coef_a, e1r, e1i), var


def rim_kernel(rows, after, m2, m1, f2, f1, mn, ms, fn_ref, fs_ref, s_out, n_out, w_out, e_out, sums):
    kdev = 2
    width = mn.shape[1] - LANES
    pad = m1.shape[1]
    ws = omegas(kdev)
    ty, count = lax.axis_index("ty"), lax.axis_size("ty")
    first = (ty * rows).astype(F32)
    total = rows * count
    fn = jnp.where(ty < count - 1, fn_ref[:MSG, :], 0.0)
    fs = jnp.where(ty > 0, fs_ref[:MSG, :], 0.0)

    ay = AY
    line = lax.broadcasted_iota(jnp.int32, (8, LANES), 0) // 2
    for low, high, start, out, at in ((fs, ms[...], -2, s_out, 0), (mn[...], fn, rows - 2, n_out, 2)):
        ax = metric((line + start).astype(F32) + first, total)
        ax = jnp.concatenate([ax] * (low.shape[1] // LANES), axis=1)
        held, var = strip_sweep(low, high, ws, ay, ax)
        for k, x in enumerate(held):
            out[8 * k : 8 * k + 8, :] = x
        for p in range(2):
            sums[at + p, :] = var[2 + 2 * p, :width]

    mw, me = roles(m1[...], m2[:MSG, :])
    fw, fe = roles(f1[...], f2[:MSG, :])
    mw, me, fw, fe = mw, me, fw, fe
    hi = rows - (pad - LANES)
    lane = lax.broadcasted_iota(jnp.int32, (MSG, LANES), 1)
    fn_end, fn_lo, fn_hi = fn[:, width:], fn[:, :LANES], fn[:, width - LANES : width]
    fs_end, fs_lo, fs_hi = fs[:, width:], fs[:, :LANES], fs[:, width - LANES : width]
    down = lambda x: rolled(x, 2, 0)
    up = lambda x: rolled(x, -2, 0)

    def ended(msg, north, north_lane, south, south_lane):
        block = msg[:, pad - LANES :]
        block = jnp.where(lane == hi, rolled(north, hi - north_lane, 1), block)
        block = jnp.where(lane == LANES - 1, rolled(south, LANES - 1 - south_lane, 1), block)
        return jnp.concatenate([msg[:, : pad - LANES], block], axis=1)

    last = LANES - 1
    low_w = ended(fw, down(fn_end), last, fs_end, last)
    high_w = ended(mw, fn_lo, 0, up(fs_lo), 0)
    low_e = ended(me, down(fn_hi), last, fs_hi, last)
    high_e = ended(fe, fn_end, 0, up(fs_end), 0)
    row = lax.broadcasted_iota(jnp.int32, (8, pad), 1).astype(F32) + first
    ax = metric(jnp.minimum(row, first + rows), total)
    for low, high, out, at in ((low_w, high_w, w_out, 4), (low_e, high_e, e_out, 5)):
        held, var = strip_sweep(low, high, ws, ax, ay)
        for k, x in enumerate(held):
            out[8 * k : 8 * k + 8, :] = x
        for p in range(2):
            sums[at, p * pad : (p + 1) * pad] = var[2 + 2 * p, :]
    sums[6:, :] = jnp.zeros((2, width), F32)


def rim(rows, m1, m2, f1, f2, mn, ms, fn, fs, after):
    row = pltpu.VMEM((48, mn.shape[1]), F32)
    col = pltpu.VMEM((48, m1.shape[1]), F32)
    sums = pltpu.VMEM((8, mn.shape[1] - LANES), F32)
    return pl.pallas_call(
        functools.partial(rim_kernel, rows),
        out_shape=(row, row, col, col, sums),
        in_specs=[pl.BlockSpec(memory_space=pltpu.VMEM)] * 9,
        out_specs=[pl.BlockSpec(memory_space=pltpu.VMEM)] * 5,
        compiler_params=PARAMS,
        name="rim",
    )(*map(vmem, (after, m2, m1, f2, f1, mn, ms, fn, fs)))


def prepare_kernel(e1_in, q, d, m, ss, sn, sw, se, du, dv, base, coef, e1, cols):
    kdev, _, rows, width = e1_in.shape
    size = 16
    ws = omegas(kdev)
    e1[...] = e1_in[...]
    for p in range(2):
        cols[2 * p : 2 * p + 2, :] = sw[8 * (4 + p) + 4 : 8 * (4 + p) + 6, :]
        cols[4 + 2 * p : 6 + 2 * p, :] = se[8 * (4 + p) + 2 : 8 * (4 + p) + 4, :]
    turned = cols[...].T
    lane = lax.broadcasted_iota(jnp.int32, (rows, LANES), 1)
    left, right = slice(0, LANES), slice(width - LANES, width)
    last = LANES - 1
    for p in range(2):
        for c in range(kdev):
            e1[c, p, 0:1, :] = ss[8 * (4 + p) + 4 + c : 8 * (4 + p) + 5 + c, :width]
            e1[c, p, rows - 1 : rows, :] = sn[8 * (4 + p) + 2 + c : 8 * (4 + p) + 3 + c, :width]
            k = 2 * p + c
            e1[c, p, :, left] = jnp.where(lane == 0, rolled(turned[:rows], -k, 1), e1[c, p, :, left])
            k = 4 + 2 * p + c
            e1[c, p, :, right] = jnp.where(lane == last, rolled(turned[:rows], last - k, 1), e1[c, p, :, right])
    for at in range(0, rows, size):
        nxt = min(at + size, rows - 8)
        here = slice(at, at + size)
        _, ax = row_metric(at, size, width, rows)
        md, mn = tile_rows(m, at, size, nxt)
        dd, dn = tile_rows(d, at, size, nxt)
        coef[0, here, :] = (THETA * ax * ax) * (md * east(md) * (dd + east(dd)))
        coef[1, here, :] = (THETA * AY * AY) * (md * mn * (dd + dn))
        for c in range(kdev):
            wt = THETA * ws[c]
            er, ern = tile_rows(e1.at[c, 0], at, size, nxt)
            ei, ein = tile_rows(e1.at[c, 1], at, size, nxt)
            qr, qrn = tile_rows(q.at[c, 0], at, size, nxt)
            qi, qin = tile_rows(q.at[c, 1], at, size, nxt)
            zr, zi = er - qr, ei - qi
            du[c, 0, here, :] = zr - east(zr)
            du[c, 1, here, :] = zi - east(zi)
            dv[c, 0, here, :] = zr - (ern - qrn)
            dv[c, 1, here, :] = zi - (ein - qin)
            base[c, 0, here, :] = md * (er + wt * ei)
            base[c, 1, here, :] = md * (ei - wt * er)


def prepare(e1, q, d, m, ss, sn, sw, se):
    plane = pltpu.VMEM(e1.shape, F32)
    return pl.pallas_call(
        prepare_kernel,
        out_shape=(plane, plane, plane, pltpu.VMEM((2, *d.shape), F32)),
        in_specs=[pl.BlockSpec(memory_space=pltpu.VMEM)] * 8,
        out_specs=[pl.BlockSpec(memory_space=pltpu.VMEM)] * 4,
        scratch_shapes=[pltpu.VMEM(e1.shape, F32), pltpu.VMEM((LANES, sw.shape[1]), F32)],
        compiler_params=PARAMS,
        cost_estimate=pl.CostEstimate(flops=40 * e1.size, bytes_accessed=160 * e1.size, transcendentals=0),
        name="prepare",
    )(*map(vmem, (e1, q, d, m, ss, sn, sw, se)))


def rate(var, d):
    s = var + BACKGROUND
    return (DRAG * (s * lax.rsqrt(s))) * recip(d)


def second_kernel(
    du, dv, base, coef, d, m, mine, other, ss, sn, sw, se, eta_out, fric_out, eta, fric, cols, sems
):
    kdev, _, rows, width = eta.shape
    pad = sw.shape[1]
    size = 16
    ws = omegas(kdev)
    half = rows // 2
    core = lax.rem(lax.axis_index("cons"), 2)
    fric[pl.ds(pl.multiple_of(core * half, 8), half), :] = mine[:half, :]
    fric[pl.ds(pl.multiple_of((1 - core) * half, 8), half), :] = other[:half, :]
    rims = mine[half:, :] + other[half:, :]

    def edge(strip, var_a, var_b):
        zr, zi, dep, ca = (strip[8 * k : 8 * k + 8, :] for k in range(4))
        var = jnp.concatenate([var_a, var_a, var_a, var_a, var_b, var_b, var_b, var_b], axis=0)
        f = rate(var, jnp.maximum(dep, TINY_DEPTH))
        up = lambda x: rolled(x, -2, 0)
        w2 = 2.0 * strip_omega(zr.shape, ws)
        return face(zr, zi, up(zr), up(zi), f + up(f), ca, w2)

    none = jnp.zeros((1, LANES), F32)
    wide = lambda x: jnp.concatenate([x, none], axis=1)
    south = edge(ss, wide(rims[0:1]), wide(rims[1:2]))
    north = edge(sn, wide(rims[2:3]), wide(rims[3:4]))
    west = edge(sw, rims[4:5, :pad], rims[4:5, pad : 2 * pad])
    east_ = edge(se, rims[5:6, :pad], rims[5:6, pad : 2 * pad])

    for p in range(2):
        cols[2 * p : 2 * p + 2, :] = west[p][2:4]
        cols[4 + 2 * p : 6 + 2 * p, :] = east_[p][2:4]
    cols[8:9, :] = rims[4:5, pad : 2 * pad]
    cols[9:10, :] = rims[5:6, :pad]
    turned = cols[...].T

    lane = lax.broadcasted_iota(jnp.int32, (rows, LANES), 1)
    left, right = slice(0, LANES), slice(width - LANES, width)
    last = LANES - 1
    fric[0:1, :] = rims[1:2]
    fric[rows - 1 : rows, :] = rims[2:3]
    fric[:, left] = jnp.where(lane == 0, rolled(turned[:rows], -8, 1), fric[:, left])
    fric[:, right] = jnp.where(lane == last, rolled(turned[:rows], last - 9, 1), fric[:, right])
    for at in range(0, rows, size):
        fric[at : at + size, :] = rate(fric[at : at + size, :], d[at : at + size, :])
    copies = [pltpu.make_async_copy(fric, fric_out, sems.at[0])]
    copies[0].start()

    lane = lax.broadcasted_iota(jnp.int32, (size, LANES), 1)
    last_v = [None] * (2 * kdev)
    for c in range(kdev):
        for p in range(2):
            last_v[2 * c + p] = south[p][2 + c : 3 + c, :width]
    for at in range(0, rows, size):
        nxt = min(at + size, rows - 8)
        here = slice(at, at + size)
        edges = turned[here]
        md = m[here, :]
        rd, rn = tile_rows(fric, at, size, nxt)
        coef_u, coef_v = coef[0, here, :], coef[1, here, :]
        r2u = rd + east(rd)
        r2v = rd + rn
        squ, sqv = r2u * r2u, r2v * r2v

        def with_east(u, k):
            block = jnp.where(lane == last, rolled(edges, last - k, 1), u[:, right])
            return jnp.concatenate([u[:, : width - LANES], block], axis=1)

        def from_west(u, k):
            u = rolled(u, 1, 1)
            block = jnp.where(lane == 0, rolled(edges, -k, 1), u[:, left])
            return jnp.concatenate([block, u[:, LANES:]], axis=1)

        for c in range(kdev):
            w2 = 2.0 * ws[c]
            gu = coef_u * recip(squ + w2 * w2)
            gv = coef_v * recip(sqv + w2 * w2)
            ur, ui = flux(du[c, 0, here, :], du[c, 1, here, :], gu, gu * r2u, w2)
            vr, vi = flux(dv[c, 0, here, :], dv[c, 1, here, :], gv, gv * r2v, w2)
            ur, ui = with_east(ur, 4 + c), with_east(ui, 6 + c)
            if at + size == rows:
                vr = jnp.concatenate([vr[:-1], north[0][2 + c : 3 + c, :width]], axis=0)
                vi = jnp.concatenate([vi[:-1], north[1][2 + c : 3 + c, :width]], axis=0)
            uwr, uwi = from_west(ur, c), from_west(ui, 2 + c)
            vsr = jnp.concatenate([last_v[2 * c], vr[:-1]], axis=0)
            vsi = jnp.concatenate([last_v[2 * c + 1], vi[:-1]], axis=0)
            last_v[2 * c], last_v[2 * c + 1] = vr[-1:], vi[-1:]
            eta[c, 0, here, :] = base[c, 0, here, :] - md * ((ur - uwr) + (vr - vsr))
            eta[c, 1, here, :] = base[c, 1, here, :] - md * ((ui - uwi) + (vi - vsi))
        copies.append(
            pltpu.make_async_copy(eta.at[:, :, here, :], eta_out.at[:, :, here, :], sems.at[len(copies)])
        )
        copies[-1].start()
    for copy in copies:
        copy.wait()


def second_sweep(du, dv, base, coef, d, m, mine, other, ss, sn, sw, se):
    args = (du, dv, base, coef, d, m, mine, other, ss, sn, sw, se)
    return pl.pallas_call(
        second_kernel,
        out_shape=(jax.ShapeDtypeStruct(du.shape, F32), jax.ShapeDtypeStruct(d.shape, F32)),
        in_specs=[pl.BlockSpec(memory_space=pltpu.VMEM)] * len(args),
        out_specs=[pl.BlockSpec(memory_space=pltpu.HBM)] * 2,
        scratch_shapes=[
            pltpu.VMEM(du.shape, F32),
            pltpu.VMEM(d.shape, F32),
            pltpu.VMEM((LANES, sw.shape[1]), F32),
            pltpu.SemaphoreType.DMA((1 + d.shape[0] // 16,)),
        ],
        compiler_params=PARAMS,
        name="second_sweep",
    )(*map(vmem, args))


def swapped(x, axis, bit):
    return lax.ppermute(x, axis, [(i, i ^ bit) for i in range(lax.axis_size(axis))])


def body(elevation, equilibrium, depth, land_mask, friction_prev):
    rows = depth.shape[0]
    ntx, nty, ncons = (lax.axis_size(a) for a in ("tx", "ty", "cons"))
    elev, equil, depth, mask, fric, m2, m1, mn, ms = pack(
        elevation, equilibrium, depth, land_mask, friction_prev
    )
    f2 = lax.ppermute(m2, "tx", [(i, (i - 1 if i % 2 == 0 else i + 1) % ntx) for i in range(ntx)])
    f1 = swapped(m1, "tx", 1)
    e1, send, keep = first_sweep(elev, equil, depth, mask, fric, m1)
    mn, ms, my, send = merge(rows, f1, f2, mn, ms, send)
    recv = swapped(send, "cons", 1)
    if nty == 2:
        fn = fs = swapped(my, "ty", 1)
    else:
        fn = lax.ppermute(ms, "ty", [(i, i - 1) for i in range(1, nty)])
        fs = lax.ppermute(mn, "ty", [(i, i + 1) for i in range(nty - 1)])
    left, right = halves(recv, keep, my)
    ss, sn, sw, se, rims = rim(rows, m1, m2, f1, f2, mn, ms, fn, fs, left)
    prepared = prepare(e1, equil, depth, mask, ss, sn, sw, se)
    parts, bit = [(left, right, rims)], 2
    if bit < ncons:
        parts.append(tuple(swapped(x, "cons", bit) for x in parts[0]))
        bit *= 2
    sums = joined(parts, prepared[2])
    while bit < ncons:
        sums = added(sums, swapped(sums, "cons", bit))
        bit *= 2
    return second_sweep(*prepared, depth, mask, sums, swapped(sums, "cons", 1), ss, sn, sw, se)


def solution(mesh):
    return jax.shard_map(
        body,
        mesh=mesh,
        in_specs=(
            P("cons", None, "ty", "tx"),
            P("cons", None, "ty", "tx"),
            P("ty", "tx"),
            P("ty", "tx"),
            P("ty", "tx"),
        ),
        out_specs=(P("cons", None, "ty", "tx"), P("ty", "tx")),
        check_vma=False,
    )
```

```python
import functools
import math

import jax
import jax.numpy as jnp
from jax import lax
from jax.experimental import pallas as pl
from jax.experimental.pallas import tpu as pltpu
from jax.sharding import PartitionSpec as P

OMEGA_TABLE = (1.0, 1.0351, 0.9582, 1.0379, 0.5181, 0.4816, 0.5164, 0.4454)
AY = 0.5
THETA = 0.05
DRAG = 0.5
BACKGROUND = 0.01
F32 = jnp.float32
LANES = 128
FIELDS = 6
MSG = 4 * FIELDS
TINY_DEPTH = 1e-6
PARAMS = pltpu.CompilerParams(vmem_limit_bytes=16 * 1024 * 1024)


def vmem(x):
    return pltpu.with_memory_space_constraint(x, pltpu.VMEM)


def hbm(x):
    return pltpu.with_memory_space_constraint(x, pltpu.HBM)


def recip(x):
    return pl.reciprocal(x, approx=True) if jnp.ndim(x) else 1.0 / x


def metric(rows, total):
    lat = (rows + 0.5) * (120.0 / total * math.pi / 180.0) - math.pi / 3.0
    s = lat * lat
    acc = jnp.full_like(s, 1.0 / math.factorial(16))
    for n in (14, 12, 10, 8, 6, 4, 2, 0):
        acc = ((-1.0) ** (n // 2)) / math.factorial(n) + s * acc
    return 0.5 / acc


def omegas(kdev):
    index = lax.axis_index("cons")
    out = []
    for c in range(kdev):
        w = jnp.float32(OMEGA_TABLE[c])
        for i in range(1, len(OMEGA_TABLE) // kdev):
            w = jnp.where(index == i, jnp.float32(OMEGA_TABLE[i * kdev + c]), w)
        out.append(w)
    return out


def rolled(x, shift, axis):
    return pltpu.roll(x, shift % x.shape[axis], axis)


def face(zr, zi, zr_next, zi_next, r2, coef, w2):
    g = coef * recip(r2 * r2 + w2 * w2)
    a = g * r2
    b = g * w2
    dr = zr - zr_next
    di = zi - zi_next
    return a * dr + b * di, a * di - b * dr


def flux(dr, di, g, a, w2):
    b = g * w2
    return a * dr + b * di, a * di - b * dr


def pack_columns_kernel(e_in, q_in, d_in, m_in, r_in, m2, m1, e, q, d, m, r, turned, sems):
    rows, width = d_in.shape
    copies = []
    for s, side in enumerate((slice(0, LANES), slice(width - LANES, width))):
        for src, dst in ((e_in, e), (q_in, q)):
            copies.append((src.at[:, :, :, side], dst.at[s]))
        for src, dst in ((d_in, d), (m_in, m), (r_in, r)):
            copies.append((src.at[:, side], dst.at[s]))
    copies = [pltpu.make_async_copy(src, dst, sems.at[k]) for k, (src, dst) in enumerate(copies)]
    for copy in copies:
        copy.start()
    for copy in copies:
        copy.wait()
    lane = lax.broadcasted_iota(jnp.int32, (rows, LANES), 1)

    def edges(plane):
        return jnp.where(lane < LANES // 2, plane(0), plane(1))

    elev = [edges(lambda s: e[s, c, p]) for p in range(2) for c in range(2)]
    equil = [edges(lambda s: q[s, c, p]) for p in range(2) for c in range(2)]
    planes = [x - y for x, y in zip(elev, equil)]
    planes += [edges(lambda s: r[s]), edges(lambda s: d[s]), edges(lambda s: m[s]).astype(F32)]
    both = jnp.zeros((rows, LANES), F32)
    for k, plane in enumerate(planes + elev):
        both = jnp.where((lane >= 4 * k) & (lane < 4 * k + 4), rolled(plane, 4 * k + 2, 1), both)
    pad = turned.shape[1]
    turned[...] = jnp.concatenate([both, jnp.zeros((pad - rows, LANES), F32)], axis=0).T
    odd = lax.rem(lax.axis_index("tx"), 2) == 1

    def put(row, k, east_, west):
        x, y = turned[4 * k + east_ : 4 * k + east_ + 1, :], turned[4 * k + west : 4 * k + west + 1, :]
        m1[row : row + 1, :] = jnp.where(odd, y, x)
        m2[row : row + 1, :] = jnp.where(odd, x, y)

    for g in range(5):
        for n in range(2):
            for c in range(2):
                put(4 * g + 2 * n + c, 2 * g + c if g < 2 else g + 2, n, 2 + n)
    for c in range(4):
        put(20 + c, 7 + c, 1, 2)
    m2[MSG:, :] = jnp.zeros((m2.shape[0] - MSG, pad), F32)


def pack_columns(elevation, equilibrium, depth, land_mask, friction):
    kdev, _, rows, width = elevation.shape
    pad = -(-rows // LANES) * LANES
    cut, plane = pltpu.VMEM((2, kdev, 2, rows, LANES), F32), pltpu.VMEM((2, rows, LANES), F32)
    return pl.pallas_call(
        pack_columns_kernel,
        out_shape=(pltpu.VMEM((MSG + 8, pad), F32), pltpu.VMEM((MSG, pad), F32)),
        in_specs=[pl.BlockSpec(memory_space=pltpu.HBM)] * 5,
        out_specs=[pl.BlockSpec(memory_space=pltpu.VMEM)] * 2,
        scratch_shapes=[
            cut,
            cut,
            plane,
            pltpu.VMEM((2, rows, LANES), jnp.int32),
            plane,
            pltpu.VMEM((LANES, pad), F32),
            pltpu.SemaphoreType.DMA((10,)),
        ],
        compiler_params=PARAMS,
        name="pack_columns",
    )(*map(hbm, (elevation, equilibrium, depth, land_mask, friction)))


def pack_kernel(e_in, q_in, d_in, m_in, r_in, after, e, q, d, m, r, mn, ms, ints, sems):
    del after
    kdev, _, rows, width = e.shape
    copies = []

    def fetch(src, dst):
        copy = pltpu.make_async_copy(src, dst, sems.at[len(copies)])
        copy.start()
        copies.append(copy)

    for src, dst in ((d_in, d), (m_in, ints), (r_in, r)):
        fetch(src, dst)
    for c in range(kdev):
        for p in range(2):
            fetch(e_in.at[c, p], e.at[c, p])
            fetch(q_in.at[c, p], q.at[c, p])
    for copy in copies[:3]:
        copy.wait()
    m[...] = ints[...].astype(F32)
    for copy in copies[3:]:
        copy.wait()

    ends = (slice(0, 8), slice(rows - 8, rows))
    for s, out in enumerate((ms, mn)):
        base = 0 if s == 0 else 6
        near = 0 if s == 0 else 7
        out[:, width:] = jnp.zeros((MSG, LANES), F32)
        for p in range(2):
            for c in range(2):
                line8 = e[c, p, ends[s], :]
                z = line8 - q[c, p, ends[s], :]
                for line in range(2):
                    out[4 * p + 2 * line + c, :width] = z[base + line, :]
                out[20 + 2 * p + c, :width] = line8[near, :]
        for g, plane in ((2, r[ends[s], :]), (3, d[ends[s], :]), (4, m[ends[s], :])):
            for line in range(2):
                for c in range(2):
                    out[4 * g + 2 * line + c, :width] = plane[base + line, :]


def pack(elevation, equilibrium, depth, land_mask, friction, after):
    kdev, _, rows, width = elevation.shape
    field, plane = pltpu.VMEM(elevation.shape, F32), pltpu.VMEM(depth.shape, F32)
    row = pltpu.VMEM((MSG, width + LANES), F32)
    return pl.pallas_call(
        pack_kernel,
        out_shape=(field, field, plane, plane, plane, row, row),
        in_specs=[pl.BlockSpec(memory_space=pltpu.HBM)] * 5 + [pl.BlockSpec(memory_space=pltpu.VMEM)],
        out_specs=[pl.BlockSpec(memory_space=pltpu.VMEM)] * 7,
        scratch_shapes=[
            pltpu.VMEM(depth.shape, jnp.int32),
            pltpu.SemaphoreType.DMA((3 + 4 * kdev,)),
        ],
        compiler_params=PARAMS,
        cost_estimate=pl.CostEstimate(flops=0, bytes_accessed=160 * elevation.size, transcendentals=0),
        name="pack",
    )(*map(hbm, (elevation, equilibrium, depth, land_mask, friction)), vmem(after))


def tile_rows(ref, at, size, nxt):
    here = ref[at : at + size, :]
    after = ref[nxt : nxt + 8, :]
    return here, jnp.concatenate([here[1:], after[0:1]], axis=0)


def east(x):
    return rolled(x, -1, 1)


def row_metric(at, size, width, rows):
    first = lax.axis_index("ty") * rows
    index = lax.broadcasted_iota(jnp.int32, (size, LANES), 0) + (first + at)
    ax = metric(index.astype(F32), rows * lax.axis_size("ty"))
    return ax, jnp.concatenate([ax] * (width // LANES), axis=1)


def first_kernel(e, q, d, mask, r, after, e1, send, keep, var):
    del after
    kdev, _, rows, width = e.shape
    size = 16
    ws = omegas(kdev)
    last_v = [jnp.zeros((1, width), F32)] * (2 * kdev)
    for at in range(0, rows, size):
        nxt = min(at + size, rows - 8)
        _, ax = row_metric(at, size, width, rows)
        md, mn = tile_rows(mask, at, size, nxt)
        dd, dn = tile_rows(d, at, size, nxt)
        rd, rn = tile_rows(r, at, size, nxt)
        coef_u = (THETA * ax * ax) * (md * east(md) * (dd + east(dd)))
        coef_v = (THETA * AY * AY) * (md * mn * (dd + dn))
        r2u = rd + east(rd)
        r2v = rd + rn
        squ, sqv = r2u * r2u, r2v * r2v
        sum_u = sum_v = None
        for c in range(kdev):
            w2 = 2.0 * ws[c]
            wt = THETA * ws[c]
            er, ern = tile_rows(e.at[c, 0], at, size, nxt)
            ei, ein = tile_rows(e.at[c, 1], at, size, nxt)
            qr, qrn = tile_rows(q.at[c, 0], at, size, nxt)
            qi, qin = tile_rows(q.at[c, 1], at, size, nxt)
            zr, zi = er - qr, ei - qi
            gu = coef_u * recip(squ + w2 * w2)
            gv = coef_v * recip(sqv + w2 * w2)
            ur, ui = flux(zr - east(zr), zi - east(zi), gu, gu * r2u, w2)
            vr, vi = flux(zr - (ern - qrn), zi - (ein - qin), gv, gv * r2v, w2)
            uwr, uwi = rolled(ur, 1, 1), rolled(ui, 1, 1)
            vsr = jnp.concatenate([last_v[2 * c], vr[:-1]], axis=0)
            vsi = jnp.concatenate([last_v[2 * c + 1], vi[:-1]], axis=0)
            last_v[2 * c], last_v[2 * c + 1] = vr[-1:], vi[-1:]
            e1[c, 0, at : at + size, :] = md * (er + wt * ei - (ur - uwr) - (vr - vsr))
            e1[c, 1, at : at + size, :] = md * (ei - wt * er - (ui - uwi) - (vi - vsi))
            su = (ur + uwr) * (ur + uwr) + (ui + uwi) * (ui + uwi)
            sv = (vr + vsr) * (vr + vsr) + (vi + vsi) * (vi + vsi)
            sum_u = su if sum_u is None else sum_u + su
            sum_v = sv if sum_v is None else sum_v + sv
        inv = recip(dd)
        ia = recip(THETA * ax)
        total = (0.125 * ia * ia) * sum_u + (0.125 / (THETA * AY) ** 2) * sum_v
        var[at : at + size, :] = total * (inv * inv)
    half = rows // 2
    core = lax.rem(lax.axis_index("cons"), 2)
    send[...] = var[pl.ds(pl.multiple_of((1 - core) * half, 8), half), :]
    keep[...] = var[pl.ds(pl.multiple_of(core * half, 8), half), :]


def first_sweep(e, q, d, m, r, after):
    kdev, _, rows, width = e.shape
    half = pltpu.VMEM((rows // 2, width), F32)
    return pl.pallas_call(
        first_kernel,
        out_shape=(pltpu.VMEM(e.shape, F32), half, half),
        in_specs=[pl.BlockSpec(memory_space=pltpu.VMEM)] * 6,
        out_specs=[pl.BlockSpec(memory_space=pltpu.VMEM)] * 3,
        scratch_shapes=[pltpu.VMEM(d.shape, F32)],
        compiler_params=PARAMS,
        cost_estimate=pl.CostEstimate(flops=80 * e.size, bytes_accessed=160 * e.size, transcendentals=0),
        name="first_sweep",
    )(*map(vmem, (e, q, d, m, r, after)))


def add_kernel(a, b, *refs):
    refs[-1][...] = a[...] + b[...]


def added(a, b, *after):
    return pl.pallas_call(
        add_kernel,
        out_shape=pltpu.VMEM(a.shape, F32),
        in_specs=[pl.BlockSpec(memory_space=pltpu.VMEM)] * (2 + len(after)),
        out_specs=pl.BlockSpec(memory_space=pltpu.VMEM),
        compiler_params=PARAMS,
        name="added",
    )(vmem(a), vmem(b), *map(vmem, after))


def halves_kernel(a, b, after, left, right):
    del after
    cut = left.shape[1]
    left[...] = a[:, :cut] + b[:, :cut]
    right[...] = a[:, cut:] + b[:, cut:]


def halves(a, b, after):
    part = pltpu.VMEM((a.shape[0], a.shape[1] // 2), F32)
    return pl.pallas_call(
        halves_kernel,
        out_shape=(part, part),
        in_specs=[pl.BlockSpec(memory_space=pltpu.VMEM)] * 3,
        out_specs=[pl.BlockSpec(memory_space=pltpu.VMEM)] * 2,
        compiler_params=PARAMS,
        name="halves",
    )(vmem(a), vmem(b), vmem(after))


def join_kernel(after, *refs):
    del after
    out = refs[-1]
    rows, cut = refs[0].shape
    for k, at in enumerate((slice(0, cut), slice(cut, 2 * cut))):
        out[:rows, at] = functools.reduce(jnp.add, [ref[...] for ref in refs[k:-1:3]])
    out[rows:, :] = functools.reduce(jnp.add, [ref[...] for ref in refs[2:-1:3]])


def joined(parts, after):
    (rows, cut), rims = parts[0][0].shape, parts[0][2].shape[0]
    flat = [x for part in parts for x in part]
    return pl.pallas_call(
        join_kernel,
        out_shape=pltpu.VMEM((rows + rims, 2 * cut), F32),
        in_specs=[pl.BlockSpec(memory_space=pltpu.VMEM)] * (1 + len(flat)),
        out_specs=pl.BlockSpec(memory_space=pltpu.VMEM),
        compiler_params=PARAMS,
        name="joined",
    )(*map(vmem, (after, *flat)))


def roles(a, b):
    even = lax.rem(lax.axis_index("tx"), 2) == 0
    return jnp.where(even, b, a), jnp.where(even, a, b)


def merge_kernel(rows, f2, f1, mn, ms, send, mn_out, ms_out, my_out, send_out):
    width = mn.shape[1] - LANES
    fw, fe = roles(f1[...], f2[:MSG, :])
    block = (rows - 1) // LANES * LANES
    lane = lax.broadcasted_iota(jnp.int32, (MSG, LANES), 1)
    in_block = rows - 1 - block
    fe_last = rolled(rolled(fe[:, block : block + LANES], -in_block, 1), 2, 0)
    fw_last = rolled(fw[:, block : block + LANES], LANES - 1 - in_block, 1)
    fe_first = fe[:, :LANES]
    fw_first = rolled(rolled(fw[:, :LANES], LANES - 1, 1), -2, 0)
    n_end = jnp.where(lane == 0, fe_last, jnp.where(lane == LANES - 1, fw_last, 0.0))
    s_end = jnp.where(lane == 0, fe_first, jnp.where(lane == LANES - 1, fw_first, 0.0))
    mn_out[:, :width] = mn[:, :width]
    ms_out[:, :width] = ms[:, :width]
    mn_out[:, width:] = n_end
    ms_out[:, width:] = s_end
    low = lax.axis_index("ty") == 0
    my_out[:MSG, :] = jnp.where(low, mn_out[...], ms_out[...])
    my_out[MSG:, :] = jnp.zeros((my_out.shape[0] - MSG, my_out.shape[1]), F32)
    send_out[...] = send[...]


def merge(rows, f1, f2, mn, ms, send):
    out = pltpu.VMEM(mn.shape, F32)
    return pl.pallas_call(
        functools.partial(merge_kernel, rows),
        out_shape=(out, out, pltpu.VMEM((MSG + 8, mn.shape[1]), F32), pltpu.VMEM(send.shape, F32)),
        in_specs=[pl.BlockSpec(memory_space=pltpu.VMEM)] * 5,
        out_specs=[pl.BlockSpec(memory_space=pltpu.VMEM)] * 4,
        compiler_params=PARAMS,
        name="merge",
    )(*map(vmem, (f2, f1, mn, ms, send)))


def strip_omega(shape, ws):
    odd = lax.rem(lax.broadcasted_iota(jnp.int32, shape, 0), 2)
    return jnp.where(odd == 0, ws[0], ws[1])


def strip_sweep(low, high, ws, g_across, g_along):
    field = [jnp.concatenate([low[4 * g : 4 * g + 4], high[4 * g : 4 * g + 4]], axis=0) for g in range(5)]
    zr, zi, r, d, m = field
    none = jnp.zeros((2, low.shape[1]), F32)
    er = jnp.concatenate([none, low[20:22], high[20:22], none], axis=0)
    ei = jnp.concatenate([none, low[22:24], high[22:24], none], axis=0)
    w = strip_omega(zr.shape, ws)
    w2 = 2.0 * w
    wt = THETA * w
    up = lambda x: rolled(x, -2, 0)
    nx = lambda x: rolled(x, -1, 1)
    coef_a = (THETA * g_across * g_across) * (m * up(m) * (d + up(d)))
    coef_l = (THETA * g_along * g_along) * (m * nx(m) * (d + nx(d)))
    ar, ai = face(zr, zi, up(zr), up(zi), r + up(r), coef_a, w2)
    lr, li = face(zr, zi, nx(zr), nx(zi), r + nx(r), coef_l, w2)
    abr, abi = rolled(ar, 2, 0), rolled(ai, 2, 0)
    lbr, lbi = rolled(lr, 1, 1), rolled(li, 1, 1)
    e1r = m * (er + wt * ei - (ar - abr) - (lr - lbr))
    e1i = m * (ei - wt * er - (ai - abi) - (li - lbi))
    sa = (ar + abr) * (ar + abr) + (ai + abi) * (ai + abi)
    sl = (lr + lbr) * (lr + lbr) + (li + lbi) * (li + lbi)
    inv = recip(jnp.maximum(d, TINY_DEPTH))
    ia = recip(THETA * g_across)
    il = recip(THETA * g_along)
    var = 0.125 * (ia * ia * sa + il * il * sl) * (inv * inv)
    var = var + rolled(var, -1, 0)
    z1r = e1r - (er - zr)
    z1i = e1i - (ei - zi)
    return (z1r, z1i, d, coef_a, e1r, e1i), var


def rim_kernel(rows, after, m2, m1, f2, f1, mn, ms, fn_ref, fs_ref, s_out, n_out, w_out, e_out, sums):
    kdev = 2
    width = mn.shape[1] - LANES
    pad = m1.shape[1]
    ws = omegas(kdev)
    ty, count = lax.axis_index("ty"), lax.axis_size("ty")
    first = (ty * rows).astype(F32)
    total = rows * count
    fn = jnp.where(ty < count - 1, fn_ref[:MSG, :], 0.0)
    fs = jnp.where(ty > 0, fs_ref[:MSG, :], 0.0)

    ay = AY
    line = lax.broadcasted_iota(jnp.int32, (8, LANES), 0) // 2
    for low, high, start, out, at in ((fs, ms[...], -2, s_out, 0), (mn[...], fn, rows - 2, n_out, 2)):
        ax = metric((line + start).astype(F32) + first, total)
        ax = jnp.concatenate([ax] * (low.shape[1] // LANES), axis=1)
        held, var = strip_sweep(low, high, ws, ay, ax)
        for k, x in enumerate(held):
            out[8 * k : 8 * k + 8, :] = x
        for p in range(2):
            sums[at + p, :] = var[2 + 2 * p, :width]

    mw, me = roles(m1[...], m2[:MSG, :])
    fw, fe = roles(f1[...], f2[:MSG, :])
    mw, me, fw, fe = mw, me, fw, fe
    hi = rows - (pad - LANES)
    lane = lax.broadcasted_iota(jnp.int32, (MSG, LANES), 1)
    fn_end, fn_lo, fn_hi = fn[:, width:], fn[:, :LANES], fn[:, width - LANES : width]
    fs_end, fs_lo, fs_hi = fs[:, width:], fs[:, :LANES], fs[:, width - LANES : width]
    down = lambda x: rolled(x, 2, 0)
    up = lambda x: rolled(x, -2, 0)

    def ended(msg, north, north_lane, south, south_lane):
        block = msg[:, pad - LANES :]
        block = jnp.where(lane == hi, rolled(north, hi - north_lane, 1), block)
        block = jnp.where(lane == LANES - 1, rolled(south, LANES - 1 - south_lane, 1), block)
        return jnp.concatenate([msg[:, : pad - LANES], block], axis=1)

    last = LANES - 1
    low_w = ended(fw, down(fn_end), last, fs_end, last)
    high_w = ended(mw, fn_lo, 0, up(fs_lo), 0)
    low_e = ended(me, down(fn_hi), last, fs_hi, last)
    high_e = ended(fe, fn_end, 0, up(fs_end), 0)
    row = lax.broadcasted_iota(jnp.int32, (8, pad), 1).astype(F32) + first
    ax = metric(jnp.minimum(row, first + rows), total)
    for low, high, out, at in ((low_w, high_w, w_out, 4), (low_e, high_e, e_out, 5)):
        held, var = strip_sweep(low, high, ws, ax, ay)
        for k, x in enumerate(held):
            out[8 * k : 8 * k + 8, :] = x
        for p in range(2):
            sums[at, p * pad : (p + 1) * pad] = var[2 + 2 * p, :]
    sums[6:, :] = jnp.zeros((2, width), F32)


def rim(rows, m1, m2, f1, f2, mn, ms, fn, fs, after):
    row = pltpu.VMEM((48, mn.shape[1]), F32)
    col = pltpu.VMEM((48, m1.shape[1]), F32)
    sums = pltpu.VMEM((8, mn.shape[1] - LANES), F32)
    return pl.pallas_call(
        functools.partial(rim_kernel, rows),
        out_shape=(row, row, col, col, sums),
        in_specs=[pl.BlockSpec(memory_space=pltpu.VMEM)] * 9,
        out_specs=[pl.BlockSpec(memory_space=pltpu.VMEM)] * 5,
        compiler_params=PARAMS,
        name="rim",
    )(*map(vmem, (after, m2, m1, f2, f1, mn, ms, fn, fs)))


def prepare_kernel(e1_in, q, d, m, ss, sn, sw, se, du, dv, base, coef, e1, cols):
    kdev, _, rows, width = e1_in.shape
    size = 16
    ws = omegas(kdev)
    e1[...] = e1_in[...]
    for p in range(2):
        cols[2 * p : 2 * p + 2, :] = sw[8 * (4 + p) + 4 : 8 * (4 + p) + 6, :]
        cols[4 + 2 * p : 6 + 2 * p, :] = se[8 * (4 + p) + 2 : 8 * (4 + p) + 4, :]
    turned = cols[...].T
    lane = lax.broadcasted_iota(jnp.int32, (rows, LANES), 1)
    left, right = slice(0, LANES), slice(width - LANES, width)
    last = LANES - 1
    for p in range(2):
        for c in range(kdev):
            e1[c, p, 0:1, :] = ss[8 * (4 + p) + 4 + c : 8 * (4 + p) + 5 + c, :width]
            e1[c, p, rows - 1 : rows, :] = sn[8 * (4 + p) + 2 + c : 8 * (4 + p) + 3 + c, :width]
            k = 2 * p + c
            e1[c, p, :, left] = jnp.where(lane == 0, rolled(turned[:rows], -k, 1), e1[c, p, :, left])
            k = 4 + 2 * p + c
            e1[c, p, :, right] = jnp.where(lane == last, rolled(turned[:rows], last - k, 1), e1[c, p, :, right])
    for at in range(0, rows, size):
        nxt = min(at + size, rows - 8)
        here = slice(at, at + size)
        _, ax = row_metric(at, size, width, rows)
        md, mn = tile_rows(m, at, size, nxt)
        dd, dn = tile_rows(d, at, size, nxt)
        coef[0, here, :] = (THETA * ax * ax) * (md * east(md) * (dd + east(dd)))
        coef[1, here, :] = (THETA * AY * AY) * (md * mn * (dd + dn))
        for c in range(kdev):
            wt = THETA * ws[c]
            er, ern = tile_rows(e1.at[c, 0], at, size, nxt)
            ei, ein = tile_rows(e1.at[c, 1], at, size, nxt)
            qr, qrn = tile_rows(q.at[c, 0], at, size, nxt)
            qi, qin = tile_rows(q.at[c, 1], at, size, nxt)
            zr, zi = er - qr, ei - qi
            du[c, 0, here, :] = zr - east(zr)
            du[c, 1, here, :] = zi - east(zi)
            dv[c, 0, here, :] = zr - (ern - qrn)
            dv[c, 1, here, :] = zi - (ein - qin)
            base[c, 0, here, :] = md * (er + wt * ei)
            base[c, 1, here, :] = md * (ei - wt * er)


def prepare(e1, q, d, m, ss, sn, sw, se):
    plane = pltpu.VMEM(e1.shape, F32)
    return pl.pallas_call(
        prepare_kernel,
        out_shape=(plane, plane, plane, pltpu.VMEM((2, *d.shape), F32)),
        in_specs=[pl.BlockSpec(memory_space=pltpu.VMEM)] * 8,
        out_specs=[pl.BlockSpec(memory_space=pltpu.VMEM)] * 4,
        scratch_shapes=[pltpu.VMEM(e1.shape, F32), pltpu.VMEM((LANES, sw.shape[1]), F32)],
        compiler_params=PARAMS,
        cost_estimate=pl.CostEstimate(flops=40 * e1.size, bytes_accessed=160 * e1.size, transcendentals=0),
        name="prepare",
    )(*map(vmem, (e1, q, d, m, ss, sn, sw, se)))


def rate(var, d):
    s = var + BACKGROUND
    return (DRAG * (s * lax.rsqrt(s))) * recip(d)


def second_kernel(
    du, dv, base, coef, d, m, mine, other, ss, sn, sw, se, eta_out, fric_out, eta, fric, cols, sems
):
    kdev, _, rows, width = eta.shape
    pad = sw.shape[1]
    size = 16
    ws = omegas(kdev)
    half = rows // 2
    core = lax.rem(lax.axis_index("cons"), 2)
    fric[pl.ds(pl.multiple_of(core * half, 8), half), :] = mine[:half, :]
    fric[pl.ds(pl.multiple_of((1 - core) * half, 8), half), :] = other[:half, :]
    rims = mine[half:, :] + other[half:, :]

    def edge(strip, var_a, var_b):
        zr, zi, dep, ca = (strip[8 * k : 8 * k + 8, :] for k in range(4))
        var = jnp.concatenate([var_a, var_a, var_a, var_a, var_b, var_b, var_b, var_b], axis=0)
        f = rate(var, jnp.maximum(dep, TINY_DEPTH))
        up = lambda x: rolled(x, -2, 0)
        w2 = 2.0 * strip_omega(zr.shape, ws)
        return face(zr, zi, up(zr), up(zi), f + up(f), ca, w2)

    none = jnp.zeros((1, LANES), F32)
    wide = lambda x: jnp.concatenate([x, none], axis=1)
    south = edge(ss, wide(rims[0:1]), wide(rims[1:2]))
    north = edge(sn, wide(rims[2:3]), wide(rims[3:4]))
    west = edge(sw, rims[4:5, :pad], rims[4:5, pad : 2 * pad])
    east_ = edge(se, rims[5:6, :pad], rims[5:6, pad : 2 * pad])

    for p in range(2):
        cols[2 * p : 2 * p + 2, :] = west[p][2:4]
        cols[4 + 2 * p : 6 + 2 * p, :] = east_[p][2:4]
    cols[8:9, :] = rims[4:5, pad : 2 * pad]
    cols[9:10, :] = rims[5:6, :pad]
    turned = cols[...].T

    lane = lax.broadcasted_iota(jnp.int32, (rows, LANES), 1)
    left, right = slice(0, LANES), slice(width - LANES, width)
    last = LANES - 1
    fric[0:1, :] = rims[1:2]
    fric[rows - 1 : rows, :] = rims[2:3]
    fric[:, left] = jnp.where(lane == 0, rolled(turned[:rows], -8, 1), fric[:, left])
    fric[:, right] = jnp.where(lane == last, rolled(turned[:rows], last - 9, 1), fric[:, right])
    for at in range(0, rows, size):
        fric[at : at + size, :] = rate(fric[at : at + size, :], d[at : at + size, :])
    copies = [pltpu.make_async_copy(fric, fric_out, sems.at[0])]
    copies[0].start()

    lane = lax.broadcasted_iota(jnp.int32, (size, LANES), 1)
    last_v = [None] * (2 * kdev)
    for c in range(kdev):
        for p in range(2):
            last_v[2 * c + p] = south[p][2 + c : 3 + c, :width]
    for at in range(0, rows, size):
        nxt = min(at + size, rows - 8)
        here = slice(at, at + size)
        edges = turned[here]
        md = m[here, :]
        rd, rn = tile_rows(fric, at, size, nxt)
        coef_u, coef_v = coef[0, here, :], coef[1, here, :]
        r2u = rd + east(rd)
        r2v = rd + rn
        squ, sqv = r2u * r2u, r2v * r2v

        def with_east(u, k):
            block = jnp.where(lane == last, rolled(edges, last - k, 1), u[:, right])
            return jnp.concatenate([u[:, : width - LANES], block], axis=1)

        def from_west(u, k):
            u = rolled(u, 1, 1)
            block = jnp.where(lane == 0, rolled(edges, -k, 1), u[:, left])
            return jnp.concatenate([block, u[:, LANES:]], axis=1)

        for c in range(kdev):
            w2 = 2.0 * ws[c]
            gu = coef_u * recip(squ + w2 * w2)
            gv = coef_v * recip(sqv + w2 * w2)
            ur, ui = flux(du[c, 0, here, :], du[c, 1, here, :], gu, gu * r2u, w2)
            vr, vi = flux(dv[c, 0, here, :], dv[c, 1, here, :], gv, gv * r2v, w2)
            ur, ui = with_east(ur, 4 + c), with_east(ui, 6 + c)
            if at + size == rows:
                vr = jnp.concatenate([vr[:-1], north[0][2 + c : 3 + c, :width]], axis=0)
                vi = jnp.concatenate([vi[:-1], north[1][2 + c : 3 + c, :width]], axis=0)
            uwr, uwi = from_west(ur, c), from_west(ui, 2 + c)
            vsr = jnp.concatenate([last_v[2 * c], vr[:-1]], axis=0)
            vsi = jnp.concatenate([last_v[2 * c + 1], vi[:-1]], axis=0)
            last_v[2 * c], last_v[2 * c + 1] = vr[-1:], vi[-1:]
            eta[c, 0, here, :] = base[c, 0, here, :] - md * ((ur - uwr) + (vr - vsr))
            eta[c, 1, here, :] = base[c, 1, here, :] - md * ((ui - uwi) + (vi - vsi))
        copies.append(
            pltpu.make_async_copy(eta.at[:, :, here, :], eta_out.at[:, :, here, :], sems.at[len(copies)])
        )
        copies[-1].start()
    for copy in copies:
        copy.wait()


def second_sweep(du, dv, base, coef, d, m, mine, other, ss, sn, sw, se):
    args = (du, dv, base, coef, d, m, mine, other, ss, sn, sw, se)
    return pl.pallas_call(
        second_kernel,
        out_shape=(jax.ShapeDtypeStruct(du.shape, F32), jax.ShapeDtypeStruct(d.shape, F32)),
        in_specs=[pl.BlockSpec(memory_space=pltpu.VMEM)] * len(args),
        out_specs=[pl.BlockSpec(memory_space=pltpu.HBM)] * 2,
        scratch_shapes=[
            pltpu.VMEM(du.shape, F32),
            pltpu.VMEM(d.shape, F32),
            pltpu.VMEM((LANES, sw.shape[1]), F32),
            pltpu.SemaphoreType.DMA((1 + d.shape[0] // 16,)),
        ],
        compiler_params=PARAMS,
        name="second_sweep",
    )(*map(vmem, args))


def swapped(x, axis, bit):
    return lax.ppermute(x, axis, [(i, i ^ bit) for i in range(lax.axis_size(axis))])


def body(elevation, equilibrium, depth, land_mask, friction_prev):
    rows = depth.shape[0]
    ntx, nty, ncons = (lax.axis_size(a) for a in ("tx", "ty", "cons"))
    fields = (elevation, equilibrium, depth, land_mask, friction_prev)
    m2, m1 = pack_columns(*fields)
    elev, equil, depth, mask, fric, mn, ms = pack(*fields, m1)
    f2 = lax.ppermute(m2, "tx", [(i, (i - 1 if i % 2 == 0 else i + 1) % ntx) for i in range(ntx)])
    f1 = swapped(m1, "tx", 1)
    e1, send, keep = first_sweep(elev, equil, depth, mask, fric, m1)
    mn, ms, my, send = merge(rows, f1, f2, mn, ms, send)
    recv = swapped(send, "cons", 1)
    if nty == 2:
        fn = fs = swapped(my, "ty", 1)
    else:
        fn = lax.ppermute(ms, "ty", [(i, i - 1) for i in range(1, nty)])
        fs = lax.ppermute(mn, "ty", [(i, i + 1) for i in range(nty - 1)])
    left, right = halves(recv, keep, my)
    ss, sn, sw, se, rims = rim(rows, m1, m2, f1, f2, mn, ms, fn, fs, left)
    prepared = prepare(e1, equil, depth, mask, ss, sn, sw, se)
    parts, bit = [(left, right, rims)], 2
    if bit < ncons:
        parts.append(tuple(swapped(x, "cons", bit) for x in parts[0]))
        bit *= 2
    sums = joined(parts, prepared[2])
    while bit < ncons:
        sums = added(sums, swapped(sums, "cons", bit))
        bit *= 2
    return second_sweep(*prepared, depth, mask, sums, swapped(sums, "cons", 1), ss, sn, sw, se)


def solution(mesh):
    return jax.shard_map(
        body,
        mesh=mesh,
        in_specs=(
            P("cons", None, "ty", "tx"),
            P("cons", None, "ty", "tx"),
            P("ty", "tx"),
            P("ty", "tx"),
            P("ty", "tx"),
        ),
        out_specs=(P("cons", None, "ty", "tx"), P("ty", "tx")),
        check_vma=False,
    )
```

```python
import functools
import math

import jax
import jax.numpy as jnp
from jax import lax
from jax.experimental import pallas as pl
from jax.experimental.pallas import tpu as pltpu
from jax.sharding import PartitionSpec as P

OMEGA_TABLE = (1.0, 1.0351, 0.9582, 1.0379, 0.5181, 0.4816, 0.5164, 0.4454)
AY = 0.5
THETA = 0.05
DRAG = 0.5
BACKGROUND = 0.01
F32 = jnp.float32
LANES = 128
MSG = 16
TINY_DEPTH = 1e-6
PARAMS = pltpu.CompilerParams(vmem_limit_bytes=16 * 1024 * 1024)


def vmem(x):
    return pltpu.with_memory_space_constraint(x, pltpu.VMEM)


def hbm(x):
    return pltpu.with_memory_space_constraint(x, pltpu.HBM)


def recip(x):
    return pl.reciprocal(x, approx=True) if jnp.ndim(x) else 1.0 / x


def metric(rows, total):
    lat = (rows + 0.5) * (120.0 / total * math.pi / 180.0) - math.pi / 3.0
    s = lat * lat
    acc = jnp.full_like(s, 1.0 / math.factorial(16))
    for n in (14, 12, 10, 8, 6, 4, 2, 0):
        acc = ((-1.0) ** (n // 2)) / math.factorial(n) + s * acc
    return 0.5 / acc


def omegas(kdev):
    index = lax.axis_index("cons")
    out = []
    for c in range(kdev):
        w = jnp.float32(OMEGA_TABLE[c])
        for i in range(1, len(OMEGA_TABLE) // kdev):
            w = jnp.where(index == i, jnp.float32(OMEGA_TABLE[i * kdev + c]), w)
        out.append(w)
    return out


def rolled(x, shift, axis):
    return pltpu.roll(x, shift % x.shape[axis], axis)


def face(zr, zi, zr_next, zi_next, r2, coef, w2):
    g = coef * recip(r2 * r2 + w2 * w2)
    a = g * r2
    b = g * w2
    dr = zr - zr_next
    di = zi - zi_next
    return a * dr + b * di, a * di - b * dr


def flux(dr, di, g, a, w2):
    b = g * w2
    return a * dr + b * di, a * di - b * dr


def pack_columns_kernel(e_in, q_in, d_in, m_in, r_in, m2, m1, e, q, d, m, r, turned, sems):
    rows, width = d_in.shape
    copies = []
    for s, side in enumerate((slice(0, LANES), slice(width - LANES, width))):
        for src, dst in ((e_in, e), (q_in, q)):
            copies.append((src.at[:, :, :, side], dst.at[s]))
        for src, dst in ((d_in, d), (m_in, m), (r_in, r)):
            copies.append((src.at[:, side], dst.at[s]))
    copies = [pltpu.make_async_copy(src, dst, sems.at[k]) for k, (src, dst) in enumerate(copies)]
    for copy in copies:
        copy.start()
    for copy in copies:
        copy.wait()
    lane = lax.broadcasted_iota(jnp.int32, (rows, LANES), 1)

    def edges(plane):
        return jnp.where(lane < LANES // 2, plane(0), plane(1))

    elev = [edges(lambda s: e[s, c, p]) for p in range(2) for c in range(2)]
    equil = [edges(lambda s: q[s, c, p]) for p in range(2) for c in range(2)]
    planes = [x - y for x, y in zip(elev, equil)]
    planes += [edges(lambda s: r[s]), edges(lambda s: d[s]), edges(lambda s: m[s]).astype(F32)]
    both = jnp.zeros((rows, LANES), F32)
    for k, plane in enumerate(planes + elev):
        both = jnp.where((lane >= 4 * k) & (lane < 4 * k + 4), rolled(plane, 4 * k + 2, 1), both)
    pad = turned.shape[1]
    turned[...] = jnp.concatenate([both, jnp.zeros((pad - rows, LANES), F32)], axis=0).T
    odd = lax.rem(lax.axis_index("tx"), 2) == 1
    first = (lax.axis_index("ty") * rows).astype(F32)
    lat_row = jnp.minimum(lax.broadcasted_iota(jnp.int32, (1, pad), 1), rows).astype(F32) + first
    ax = metric(lat_row, rows * lax.axis_size("ty"))
    ws = omegas(2)

    def line(k, at):
        return turned[4 * k + at : 4 * k + at + 1, :]

    def message(near, far):
        low, high = min(near, far), max(near, far)
        coef = (THETA * ax * ax) * (line(6, low) * line(6, high) * (line(5, low) + line(5, high)))
        r2 = line(4, low) + line(4, high)
        behind = []
        for c in range(2):
            behind.append(
                face(line(c, low), line(2 + c, low), line(c, high), line(2 + c, high), r2, coef, 2.0 * ws[c])
            )
        out = [line(k, near) for k in range(4)]
        out += [behind[c][p] for p in range(2) for c in range(2)]
        return out + [line(k, near) for k in (7, 8, 9, 10, 4, 5, 6)]

    for k, (x, y) in enumerate(zip(message(1, 0), message(2, 3))):
        m1[k : k + 1, :] = jnp.where(odd, y, x)
        m2[k : k + 1, :] = jnp.where(odd, x, y)[:, :rows]
    m1[MSG - 1 :, :] = jnp.zeros((1, pad), F32)
    m2[MSG - 1 :, :] = jnp.zeros((1, rows), F32)


def pack_columns(elevation, equilibrium, depth, land_mask, friction):
    kdev, _, rows, width = elevation.shape
    pad = -(-rows // LANES) * LANES
    cut, plane = pltpu.VMEM((2, kdev, 2, rows, LANES), F32), pltpu.VMEM((2, rows, LANES), F32)
    return pl.pallas_call(
        pack_columns_kernel,
        out_shape=(pltpu.VMEM((MSG, rows), F32), pltpu.VMEM((MSG, pad), F32)),
        in_specs=[pl.BlockSpec(memory_space=pltpu.HBM)] * 5,
        out_specs=[pl.BlockSpec(memory_space=pltpu.VMEM)] * 2,
        scratch_shapes=[
            cut,
            cut,
            plane,
            pltpu.VMEM((2, rows, LANES), jnp.int32),
            plane,
            pltpu.VMEM((LANES, pad), F32),
            pltpu.SemaphoreType.DMA((10,)),
        ],
        compiler_params=PARAMS,
        name="pack_columns",
    )(*map(hbm, (elevation, equilibrium, depth, land_mask, friction)))


def pack_kernel(e, q, d, ints, r, after, m, mn, ms):
    del after
    kdev, _, rows, width = e.shape
    m[...] = ints[...].astype(F32)
    ws = omegas(kdev)
    for out, end, near, low in ((ms, slice(0, 8), 0, 0), (mn, slice(rows - 8, rows), 7, 6)):
        out[:, width:] = jnp.zeros((MSG, LANES), F32)
        r8, d8, m8 = r[end, :], d[end, :], m[end, :]
        up = lambda x: rolled(x, -1, 0)
        coef = (THETA * AY * AY) * (m8 * up(m8) * (d8 + up(d8)))
        r2 = r8 + up(r8)
        for c in range(kdev):
            elev = [e[c, p, end, :] for p in range(2)]
            z = [elev[p] - q[c, p, end, :] for p in range(2)]
            v = face(z[0], z[1], up(z[0]), up(z[1]), r2, coef, 2.0 * ws[c])
            for p in range(2):
                out[2 * p + c, :width] = z[p][near, :]
                out[4 + 2 * p + c, :width] = v[p][low, :]
                out[8 + 2 * p + c, :width] = elev[p][near, :]
        for k, plane in enumerate((r8, d8, m8)):
            out[12 + k, :width] = plane[near, :]
        out[MSG - 1, :width] = jnp.zeros((width,), F32)


def pack(elevation, equilibrium, depth, land_mask, friction, after):
    kdev, _, rows, width = elevation.shape
    plane = pltpu.VMEM(depth.shape, F32)
    row = pltpu.VMEM((MSG, width + LANES), F32)
    return pl.pallas_call(
        pack_kernel,
        out_shape=(plane, row, row),
        in_specs=[pl.BlockSpec(memory_space=pltpu.VMEM)] * 6,
        out_specs=[pl.BlockSpec(memory_space=pltpu.VMEM)] * 3,
        compiler_params=PARAMS,
        name="pack",
    )(*map(vmem, (elevation, equilibrium, depth, land_mask, friction, after)))


def tile_rows(ref, at, size, nxt):
    here = ref[at : at + size, :]
    after = ref[nxt : nxt + 8, :]
    return here, jnp.concatenate([here[1:], after[0:1]], axis=0)


def east(x):
    return rolled(x, -1, 1)


def row_metric(at, size, width, rows):
    first = lax.axis_index("ty") * rows
    index = lax.broadcasted_iota(jnp.int32, (size, LANES), 0) + (first + at)
    ax = metric(index.astype(F32), rows * lax.axis_size("ty"))
    return ax, jnp.concatenate([ax] * (width // LANES), axis=1)


def first_kernel(e, q, d, mask, r, after, e1, send, keep, var):
    del after
    kdev, _, rows, width = e.shape
    size = 16
    ws = omegas(kdev)
    last_v = [jnp.zeros((1, width), F32)] * (2 * kdev)
    for at in range(0, rows, size):
        nxt = min(at + size, rows - 8)
        _, ax = row_metric(at, size, width, rows)
        md, mn = tile_rows(mask, at, size, nxt)
        dd, dn = tile_rows(d, at, size, nxt)
        rd, rn = tile_rows(r, at, size, nxt)
        coef_u = (THETA * ax * ax) * (md * east(md) * (dd + east(dd)))
        coef_v = (THETA * AY * AY) * (md * mn * (dd + dn))
        r2u = rd + east(rd)
        r2v = rd + rn
        squ, sqv = r2u * r2u, r2v * r2v
        sum_u = sum_v = None
        for c in range(kdev):
            w2 = 2.0 * ws[c]
            wt = THETA * ws[c]
            er, ern = tile_rows(e.at[c, 0], at, size, nxt)
            ei, ein = tile_rows(e.at[c, 1], at, size, nxt)
            qr, qrn = tile_rows(q.at[c, 0], at, size, nxt)
            qi, qin = tile_rows(q.at[c, 1], at, size, nxt)
            zr, zi = er - qr, ei - qi
            gu = coef_u * recip(squ + w2 * w2)
            gv = coef_v * recip(sqv + w2 * w2)
            ur, ui = flux(zr - east(zr), zi - east(zi), gu, gu * r2u, w2)
            vr, vi = flux(zr - (ern - qrn), zi - (ein - qin), gv, gv * r2v, w2)
            uwr, uwi = rolled(ur, 1, 1), rolled(ui, 1, 1)
            vsr = jnp.concatenate([last_v[2 * c], vr[:-1]], axis=0)
            vsi = jnp.concatenate([last_v[2 * c + 1], vi[:-1]], axis=0)
            last_v[2 * c], last_v[2 * c + 1] = vr[-1:], vi[-1:]
            e1[c, 0, at : at + size, :] = md * (er + wt * ei - (ur - uwr) - (vr - vsr))
            e1[c, 1, at : at + size, :] = md * (ei - wt * er - (ui - uwi) - (vi - vsi))
            su = (ur + uwr) * (ur + uwr) + (ui + uwi) * (ui + uwi)
            sv = (vr + vsr) * (vr + vsr) + (vi + vsi) * (vi + vsi)
            sum_u = su if sum_u is None else sum_u + su
            sum_v = sv if sum_v is None else sum_v + sv
        inv = recip(dd)
        ia = recip(THETA * ax)
        total = (0.125 * ia * ia) * sum_u + (0.125 / (THETA * AY) ** 2) * sum_v
        var[at : at + size, :] = total * (inv * inv)
    half = rows // 2
    core = lax.rem(lax.axis_index("cons"), 2)
    send[...] = var[pl.ds(pl.multiple_of((1 - core) * half, 8), half), :]
    keep[...] = var[pl.ds(pl.multiple_of(core * half, 8), half), :]


def first_sweep(e, q, d, m, r, after):
    kdev, _, rows, width = e.shape
    half = pltpu.VMEM((rows // 2, width), F32)
    return pl.pallas_call(
        first_kernel,
        out_shape=(pltpu.VMEM(e.shape, F32), half, half),
        in_specs=[pl.BlockSpec(memory_space=pltpu.VMEM)] * 6,
        out_specs=[pl.BlockSpec(memory_space=pltpu.VMEM)] * 3,
        scratch_shapes=[pltpu.VMEM(d.shape, F32)],
        compiler_params=PARAMS,
        cost_estimate=pl.CostEstimate(flops=80 * e.size, bytes_accessed=160 * e.size, transcendentals=0),
        name="first_sweep",
    )(*map(vmem, (e, q, d, m, r, after)))


def add_kernel(a, b, *refs):
    refs[-1][...] = a[...] + b[...]


def added(a, b, *after):
    return pl.pallas_call(
        add_kernel,
        out_shape=pltpu.VMEM(a.shape, F32),
        in_specs=[pl.BlockSpec(memory_space=pltpu.VMEM)] * (2 + len(after)),
        out_specs=pl.BlockSpec(memory_space=pltpu.VMEM),
        compiler_params=PARAMS,
        name="added",
    )(vmem(a), vmem(b), *map(vmem, after))


def cut_kernel(a, b, after, *outs):
    del after
    at = 0
    for out in outs:
        here = slice(at, at + out.shape[0])
        out[...] = a[here, :] + b[here, :]
        at += out.shape[0]


def cut_sum(a, b, after):
    rows, width = a.shape
    large = pltpu.VMEM(((rows - 8) // 2, width), F32)
    return pl.pallas_call(
        cut_kernel,
        out_shape=(large, large, pltpu.VMEM((8, width), F32)),
        in_specs=[pl.BlockSpec(memory_space=pltpu.VMEM)] * 3,
        out_specs=[pl.BlockSpec(memory_space=pltpu.VMEM)] * 3,
        compiler_params=PARAMS,
        name="cut_sum",
    )(vmem(a), vmem(b), vmem(after))


def tree_sum(terms):
    while len(terms) > 1:
        terms = [a + b for a, b in zip(terms[::2], terms[1::2])]
    return terms[0]


def join_kernel(after, *refs):
    del after
    mine, rims = refs[-2:]
    pieces, partner, others = refs[:3], refs[3:6], refs[6:-2]
    large = pieces[0].shape[0]
    mine[:large, :] = pieces[0][...] + partner[0][...]
    mine[large : 2 * large, :] = pieces[1][...] + partner[1][...]
    mine[2 * large :, :] = pieces[2][:8, :] + partner[2][:8, :]
    terms = [x[...] for x in others]
    rims[...] = tree_sum([pieces[2][8:, :], terms[0], partner[2][8:, :], *terms[1:]])


def joined(pieces, partner, others, after):
    width = pieces[0].shape[1]
    args = (after, *pieces, *partner, *others)
    return pl.pallas_call(
        join_kernel,
        out_shape=(pltpu.VMEM((2 * pieces[0].shape[0] + 8, width), F32), pltpu.VMEM((8, width), F32)),
        in_specs=[pl.BlockSpec(memory_space=pltpu.VMEM)] * len(args),
        out_specs=[pl.BlockSpec(memory_space=pltpu.VMEM)] * 2,
        compiler_params=PARAMS,
        name="joined",
    )(*map(vmem, args))


def roles(a, b):
    even = lax.rem(lax.axis_index("tx"), 2) == 0
    return jnp.where(even, b, a), jnp.where(even, a, b)


def padded(x, pad):
    return jnp.concatenate([x, jnp.zeros((x.shape[0], pad - x.shape[1]), F32)], axis=1)


def merge_kernel(rows, f2, f1, mn, ms, send, mn_out, ms_out, my_out, send_out):
    width = mn.shape[1] - LANES
    fw, fe = roles(f1[...], padded(f2[...], f1.shape[1]))
    lane = lax.broadcasted_iota(jnp.int32, (MSG, LANES), 1)
    last = LANES - 1

    def ends(at):
        east_, west = fe[:, at // LANES * LANES :][:, :LANES], fw[:, at // LANES * LANES :][:, :LANES]
        east_, west = rolled(east_, -(at % LANES), 1), rolled(west, last - at % LANES, 1)
        return jnp.where(lane == 0, east_, jnp.where(lane == last, west, 0.0))

    mn_out[:, :width] = mn[:, :width]
    ms_out[:, :width] = ms[:, :width]
    mn_out[:, width:] = ends(rows - 1)
    ms_out[:, width:] = ends(0)
    low = lax.axis_index("ty") == 0
    my_out[...] = jnp.where(low, mn_out[...], ms_out[...])
    send_out[...] = send[...]


def merge(rows, f1, f2, mn, ms, send):
    out = pltpu.VMEM(mn.shape, F32)
    return pl.pallas_call(
        functools.partial(merge_kernel, rows),
        out_shape=(out, out, out, pltpu.VMEM(send.shape, F32)),
        in_specs=[pl.BlockSpec(memory_space=pltpu.VMEM)] * 5,
        out_specs=[pl.BlockSpec(memory_space=pltpu.VMEM)] * 4,
        compiler_params=PARAMS,
        name="merge",
    )(*map(vmem, (f2, f1, mn, ms, send)))


def strip_omega(shape, ws):
    odd = lax.rem(lax.broadcasted_iota(jnp.int32, shape, 0), 2)
    return jnp.where(odd == 0, ws[0], ws[1])


def strip_sweep(low, high, ws, g_across, g_along):
    none = jnp.zeros((2, low.shape[1]), F32)

    def field(at):
        return jnp.concatenate([none, low[at : at + 2], high[at : at + 2], none], axis=0)

    def single(at):
        a, b = low[at : at + 1], high[at : at + 1]
        return jnp.concatenate([none, a, a, b, b, none], axis=0)

    def given(at):
        return jnp.concatenate([low[at : at + 2], none, high[at : at + 2], none], axis=0)

    zr, zi, er, ei = field(0), field(2), field(8), field(10)
    r, d, m = single(12), single(13), single(14)
    w = strip_omega(zr.shape, ws)
    w2 = 2.0 * w
    wt = THETA * w
    up = lambda x: rolled(x, -2, 0)
    nx = lambda x: rolled(x, -1, 1)
    coef_a = (THETA * g_across * g_across) * (m * up(m) * (d + up(d)))
    coef_l = (THETA * g_along * g_along) * (m * nx(m) * (d + nx(d)))
    ar, ai = face(zr, zi, up(zr), up(zi), r + up(r), coef_a, w2)
    middle = lax.broadcasted_iota(jnp.int32, zr.shape, 0) // 2 == 1
    ar, ai = jnp.where(middle, ar, given(4)), jnp.where(middle, ai, given(6))
    lr, li = face(zr, zi, nx(zr), nx(zi), r + nx(r), coef_l, w2)
    abr, abi = rolled(ar, 2, 0), rolled(ai, 2, 0)
    lbr, lbi = rolled(lr, 1, 1), rolled(li, 1, 1)
    e1r = m * (er + wt * ei - (ar - abr) - (lr - lbr))
    e1i = m * (ei - wt * er - (ai - abi) - (li - lbi))
    sa = (ar + abr) * (ar + abr) + (ai + abi) * (ai + abi)
    sl = (lr + lbr) * (lr + lbr) + (li + lbi) * (li + lbi)
    inv = recip(jnp.maximum(d, TINY_DEPTH))
    ia = recip(THETA * g_across)
    il = recip(THETA * g_along)
    var = 0.125 * (ia * ia * sa + il * il * sl) * (inv * inv)
    var = var + rolled(var, -1, 0)
    z1r = e1r - (er - zr)
    z1i = e1i - (ei - zi)
    return (z1r, z1i, d, coef_a, e1r, e1i), var


def rim_kernel(rows, late, m2, m1, f2, f1, mn, ms, fn_ref, fs_ref, s_out, n_out, w_out, e_out, sums, tail):
    kdev = 2
    width = mn.shape[1] - LANES
    pad = m1.shape[1]
    ws = omegas(kdev)
    ty, count = lax.axis_index("ty"), lax.axis_size("ty")
    first = (ty * rows).astype(F32)
    total = rows * count
    fn = jnp.where(ty < count - 1, fn_ref[...], 0.0)
    fs = jnp.where(ty > 0, fs_ref[...], 0.0)

    ay = AY
    line = lax.broadcasted_iota(jnp.int32, (8, LANES), 0) // 2
    for low, high, start, out, at in ((fs, ms[...], -2, s_out, 0), (mn[...], fn, rows - 2, n_out, 2)):
        ax = metric((line + start).astype(F32) + first, total)
        ax = jnp.concatenate([ax] * (low.shape[1] // LANES), axis=1)
        held, var = strip_sweep(low, high, ws, ay, ax)
        for k, x in enumerate(held):
            out[8 * k : 8 * k + 8, :] = x
        for p in range(2):
            sums[at + p, :] = var[2 + 2 * p, :width]

    mw, me = roles(m1[...], padded(m2[...], pad))
    fw, fe = roles(f1[...], padded(f2[...], pad))
    hi = rows - (pad - LANES)
    last = LANES - 1
    lane = lax.broadcasted_iota(jnp.int32, (MSG, LANES), 1)

    def ended(msg, block, at):
        end = msg[:, pad - LANES :]
        end = jnp.where(lane == hi, rolled(fn[:, block : block + LANES], hi - at, 1), end)
        end = jnp.where(lane == last, rolled(fs[:, block : block + LANES], last - at, 1), end)
        return jnp.concatenate([msg[:, : pad - LANES], end], axis=1)

    low_w, high_w = ended(fw, width, last), ended(mw, 0, 0)
    low_e, high_e = ended(me, width - LANES, last), ended(fe, width, 0)
    row = lax.broadcasted_iota(jnp.int32, (8, pad), 1).astype(F32) + first
    ax = metric(jnp.minimum(row, first + rows), total)
    for low, high, out, at in ((low_w, high_w, w_out, 4), (low_e, high_e, e_out, 5)):
        held, var = strip_sweep(low, high, ws, ax, ay)
        for k, x in enumerate(held):
            out[8 * k : 8 * k + 8, :] = x
        for p in range(2):
            sums[at, p * pad : (p + 1) * pad] = var[2 + 2 * p, :]
    sums[6:, :] = jnp.zeros((2, width), F32)
    tail[:8, :] = late[...]
    tail[8:, :] = sums[...]


def rim(rows, m1, m2, f1, f2, mn, ms, fn, fs, late):
    row = pltpu.VMEM((48, mn.shape[1]), F32)
    col = pltpu.VMEM((48, m1.shape[1]), F32)
    sums = pltpu.VMEM((8, mn.shape[1] - LANES), F32)
    return pl.pallas_call(
        functools.partial(rim_kernel, rows),
        out_shape=(row, row, col, col, sums, pltpu.VMEM((16, mn.shape[1] - LANES), F32)),
        in_specs=[pl.BlockSpec(memory_space=pltpu.VMEM)] * 9,
        out_specs=[pl.BlockSpec(memory_space=pltpu.VMEM)] * 6,
        compiler_params=PARAMS,
        name="rim",
    )(*map(vmem, (late, m2, m1, f2, f1, mn, ms, fn, fs)))


def prepare_kernel(e1_in, q, d, m, ss, sn, sw, se, du, dv, base, coef, e1, cols):
    kdev, _, rows, width = e1_in.shape
    size = 16
    ws = omegas(kdev)
    e1[...] = e1_in[...]
    for p in range(2):
        cols[2 * p : 2 * p + 2, :] = sw[8 * (4 + p) + 4 : 8 * (4 + p) + 6, :]
        cols[4 + 2 * p : 6 + 2 * p, :] = se[8 * (4 + p) + 2 : 8 * (4 + p) + 4, :]
    turned = cols[...].T
    lane = lax.broadcasted_iota(jnp.int32, (rows, LANES), 1)
    left, right = slice(0, LANES), slice(width - LANES, width)
    last = LANES - 1
    for p in range(2):
        for c in range(kdev):
            e1[c, p, 0:1, :] = ss[8 * (4 + p) + 4 + c : 8 * (4 + p) + 5 + c, :width]
            e1[c, p, rows - 1 : rows, :] = sn[8 * (4 + p) + 2 + c : 8 * (4 + p) + 3 + c, :width]
            k = 2 * p + c
            e1[c, p, :, left] = jnp.where(lane == 0, rolled(turned[:rows], -k, 1), e1[c, p, :, left])
            k = 4 + 2 * p + c
            e1[c, p, :, right] = jnp.where(lane == last, rolled(turned[:rows], last - k, 1), e1[c, p, :, right])
    for at in range(0, rows, size):
        nxt = min(at + size, rows - 8)
        here = slice(at, at + size)
        _, ax = row_metric(at, size, width, rows)
        md, mn = tile_rows(m, at, size, nxt)
        dd, dn = tile_rows(d, at, size, nxt)
        coef[0, here, :] = (THETA * ax * ax) * (md * east(md) * (dd + east(dd)))
        coef[1, here, :] = (THETA * AY * AY) * (md * mn * (dd + dn))
        for c in range(kdev):
            wt = THETA * ws[c]
            er, ern = tile_rows(e1.at[c, 0], at, size, nxt)
            ei, ein = tile_rows(e1.at[c, 1], at, size, nxt)
            qr, qrn = tile_rows(q.at[c, 0], at, size, nxt)
            qi, qin = tile_rows(q.at[c, 1], at, size, nxt)
            zr, zi = er - qr, ei - qi
            du[c, 0, here, :] = zr - east(zr)
            du[c, 1, here, :] = zi - east(zi)
            dv[c, 0, here, :] = zr - (ern - qrn)
            dv[c, 1, here, :] = zi - (ein - qin)
            base[c, 0, here, :] = md * (er + wt * ei)
            base[c, 1, here, :] = md * (ei - wt * er)


def prepare(e1, q, d, m, ss, sn, sw, se):
    plane = pltpu.VMEM(e1.shape, F32)
    return pl.pallas_call(
        prepare_kernel,
        out_shape=(plane, plane, plane, pltpu.VMEM((2, *d.shape), F32)),
        in_specs=[pl.BlockSpec(memory_space=pltpu.VMEM)] * 8,
        out_specs=[pl.BlockSpec(memory_space=pltpu.VMEM)] * 4,
        scratch_shapes=[pltpu.VMEM(e1.shape, F32), pltpu.VMEM((LANES, sw.shape[1]), F32)],
        compiler_params=PARAMS,
        cost_estimate=pl.CostEstimate(flops=40 * e1.size, bytes_accessed=160 * e1.size, transcendentals=0),
        name="prepare",
    )(*map(vmem, (e1, q, d, m, ss, sn, sw, se)))


def rate(var, d):
    s = var + BACKGROUND
    return (DRAG * (s * lax.rsqrt(s))) * recip(d)


def sweep_tile(row, size, r, r_north, du, dv, base, coef, m, turned, ws, last_v, top):
    kdev, width = du.shape[0], du.shape[3]
    here = pl.ds(row, size)
    edges = turned[here, :]
    md = m[here, :]
    coef_u, coef_v = coef[0, here, :], coef[1, here, :]
    r2u = r + east(r)
    r2v = r + r_north
    squ, sqv = r2u * r2u, r2v * r2v
    lane = lax.broadcasted_iota(jnp.int32, (size, LANES), 1)
    last = LANES - 1

    def with_east(u, k):
        block = jnp.where(lane == last, rolled(edges, last - k, 1), u[:, width - LANES :])
        return jnp.concatenate([u[:, : width - LANES], block], axis=1)

    def from_west(u, k):
        u = rolled(u, 1, 1)
        block = jnp.where(lane == 0, rolled(edges, -k, 1), u[:, :LANES])
        return jnp.concatenate([block, u[:, LANES:]], axis=1)

    planes, out_v = {}, {}
    for c in range(kdev):
        w2 = 2.0 * ws[c]
        gu = coef_u * recip(squ + w2 * w2)
        gv = coef_v * recip(sqv + w2 * w2)
        u = flux(du[c, 0, here, :], du[c, 1, here, :], gu, gu * r2u, w2)
        v = flux(dv[c, 0, here, :], dv[c, 1, here, :], gv, gv * r2v, w2)
        for p in range(2):
            up, vp = with_east(u[p], 4 + 2 * p + c), v[p]
            if top is not None:
                vp = jnp.concatenate([vp[:-1], top(c, p, vp[-1:])], axis=0)
            uw = from_west(up, 2 * p + c)
            vs = jnp.concatenate([last_v[c, p], vp[:-1]], axis=0)
            out_v[c, p] = vp[-1:]
            planes[c, p] = base[c, p, here, :] - md * ((up - uw) + (vp - vs))
    return planes, out_v


def pairs(kdev):
    return [(c, p) for c in range(kdev) for p in range(2)]


def half_rate(var, rims, turned, d, row, low, half):
    here = pl.ds(row, half)
    edges = turned[here, :]
    width = var.shape[1]
    index = lax.broadcasted_iota(jnp.int32, (8, width), 0)
    first = jnp.where(low & (index == 0), rims[1:2], var[:8])
    final = jnp.where(jnp.logical_not(low) & (index == 7), rims[2:3], var[half - 8 :])
    var = jnp.concatenate([first, var[8 : half - 8], final], axis=0)
    lane = lax.broadcasted_iota(jnp.int32, (half, LANES), 1)
    left = jnp.where(lane == 0, rolled(edges, -8, 1), var[:, :LANES])
    right = jnp.where(lane == LANES - 1, rolled(edges, LANES - 1 - 9, 1), var[:, width - LANES :])
    return rate(jnp.concatenate([left, var[:, LANES : width - LANES], right], axis=1), d[here, :])


def own_kernel(du, dv, base, coef, d, m, mine, rims_ref, ss, sn, sw, se, eta, fric, vs_out, vn_out, turned, cols):
    kdev, _, half, width = eta.shape
    pad = sw.shape[1]
    ws = omegas(kdev)
    core = lax.rem(lax.axis_index("cons"), 2)
    low = core == 0
    rims = rims_ref[...]

    def edge(strip, var_a, var_b):
        zr, zi, dep, ca = (strip[8 * k : 8 * k + 8, :] for k in range(4))
        var = jnp.concatenate([var_a, var_a, var_a, var_a, var_b, var_b, var_b, var_b], axis=0)
        f = rate(var, jnp.maximum(dep, TINY_DEPTH))
        up = lambda x: rolled(x, -2, 0)
        w2 = 2.0 * strip_omega(zr.shape, ws)
        return face(zr, zi, up(zr), up(zi), f + up(f), ca, w2)

    none = jnp.zeros((1, LANES), F32)
    wide = lambda x: jnp.concatenate([x, none], axis=1)
    south = edge(ss, wide(rims[0:1]), wide(rims[1:2]))
    north = edge(sn, wide(rims[2:3]), wide(rims[3:4]))
    west = edge(sw, rims[4:5, :pad], rims[4:5, pad : 2 * pad])
    east_ = edge(se, rims[5:6, :pad], rims[5:6, pad : 2 * pad])
    for p in range(2):
        cols[2 * p : 2 * p + 2, :] = west[p][2:4]
        cols[4 + 2 * p : 6 + 2 * p, :] = east_[p][2:4]
        for c in range(kdev):
            vs_out[2 * c + p : 2 * c + p + 1, :] = south[p][2 + c : 3 + c, :width]
            vn_out[2 * c + p : 2 * c + p + 1, :] = north[p][2 + c : 3 + c, :width]
    cols[8:9, :] = rims[4:5, pad : 2 * pad]
    cols[9:10, :] = rims[5:6, :pad]
    turned[...] = cols[...].T

    first = pl.multiple_of(core * half, 8)
    fric[...] = half_rate(mine[...], rims, turned, d, first, low, half)
    size = 24
    last_v = {(c, p): jnp.where(low, vs_out[2 * c + p : 2 * c + p + 1, :], 0.0) for c, p in pairs(kdev)}

    def top(c, p, own):
        return jnp.where(low, 0.0, vn_out[2 * c + p : 2 * c + p + 1, :])

    for at in range(0, half, size):
        r, rn = tile_rows(fric, at, size, min(at + size, half - 8))
        planes, last_v = sweep_tile(
            pl.multiple_of(first + at, 8), size, r, rn, du, dv, base, coef, m, turned, ws, last_v,
            top if at + size == half else None,
        )
        for c, p in pairs(kdev):
            eta[c, p, at : at + size, :] = planes[c, p]


def own_half(du, dv, base, coef, d, m, mine, rims, ss, sn, sw, se):
    kdev, _, rows, width = du.shape
    pad = sw.shape[1]
    args = (du, dv, base, coef, d, m, mine, rims, ss, sn, sw, se)
    line = pltpu.VMEM((8, width), F32)
    return pl.pallas_call(
        own_kernel,
        out_shape=(
            pltpu.VMEM((kdev, 2, rows // 2, width), F32),
            pltpu.VMEM((rows // 2, width), F32),
            line,
            line,
            pltpu.VMEM((pad, LANES), F32),
        ),
        in_specs=[pl.BlockSpec(memory_space=pltpu.VMEM)] * len(args),
        out_specs=[pl.BlockSpec(memory_space=pltpu.VMEM)] * 5,
        scratch_shapes=[pltpu.VMEM((LANES, pad), F32)],
        compiler_params=PARAMS,
        name="own_half",
    )(*map(vmem, args))


def other_kernel(
    du, dv, base, coef, d, m, other, rims, eta_own, fric_own, vs, vn, turned,
    eta_out, fric_out, eta, fric, fixed, sems,
):
    kdev, _, half, width = eta.shape
    ws = omegas(kdev)
    core = lax.rem(lax.axis_index("cons"), 2)
    own_low = core == 0
    own, first = pl.multiple_of(core * half, 8), pl.multiple_of((1 - core) * half, 8)
    copies = []

    def put(src, dst):
        copy = pltpu.make_async_copy(src, dst, sems.at[len(copies)])
        copy.start()
        copies.append(copy)

    skip = pl.multiple_of(core * 8, 8)
    put(
        eta_own.at[:, :, pl.ds(skip, half - 8), :],
        eta_out.at[:, :, pl.ds(pl.multiple_of(own + skip, 8), half - 8), :],
    )
    put(fric_own, fric_out.at[pl.ds(own, half), :])
    fric[pl.ds(own, half), :] = fric_own[...]
    fric[pl.ds(first, half), :] = half_rate(other[...], rims[...], turned, d, first, jnp.logical_not(own_low), half)
    put(fric.at[pl.ds(first, half), :], fric_out.at[pl.ds(first, half), :])

    r, rn = tile_rows(fric, half - 8, 8, half)
    r2 = r + rn
    between = {}
    for c in range(kdev):
        w2 = 2.0 * ws[c]
        g = coef[1, half - 8 : half, :] * recip(r2 * r2 + w2 * w2)
        v = flux(dv[c, 0, half - 8 : half, :], dv[c, 1, half - 8 : half, :], g, g * r2, w2)
        for p in range(2):
            between[c, p] = v[p][7:8]
    index = lax.broadcasted_iota(jnp.int32, (8, width), 0)
    at_face = index == jnp.where(own_low, 7, 0)
    sign = jnp.where(own_low, -1.0, 1.0)
    local = pl.ds(pl.multiple_of((1 - core) * (half - 8), 8), 8)
    border = pl.ds(pl.multiple_of(half - 8 + 8 * core, 8), 8)
    md = m[border, :]
    for c, p in pairs(kdev):
        fixed[c, p] = eta_own[c, p, local, :] + jnp.where(at_face, sign * (md * between[c, p]), 0.0)
    put(fixed, eta_out.at[:, :, border, :])

    size = 24
    rows = 2 * half
    last_v = {(c, p): jnp.where(own_low, between[c, p], vs[2 * c + p : 2 * c + p + 1, :]) for c, p in pairs(kdev)}

    def top(c, p, own_v):
        return jnp.where(own_low, vn[2 * c + p : 2 * c + p + 1, :], own_v)

    for at in range(0, half, size):
        row = pl.multiple_of(first + at, 8)
        r = fric[pl.ds(row, size), :]
        after = fric[pl.ds(pl.multiple_of(jnp.minimum(row + size, rows - 8), 8), 8), :]
        rn = jnp.concatenate([r[1:], after[0:1]], axis=0)
        planes, last_v = sweep_tile(
            row, size, r, rn, du, dv, base, coef, m, turned, ws, last_v, top if at + size == half else None
        )
        for c, p in pairs(kdev):
            eta[c, p, at : at + size, :] = planes[c, p]
        put(eta.at[:, :, at : at + size, :], eta_out.at[:, :, pl.ds(row, size), :])
    for copy in copies:
        copy.wait()


def other_half(du, dv, base, coef, d, m, other, rims, eta_own, fric_own, vs, vn, turned):
    kdev, _, rows, width = du.shape
    args = (du, dv, base, coef, d, m, other, rims, eta_own, fric_own, vs, vn, turned)
    return pl.pallas_call(
        other_kernel,
        out_shape=(jax.ShapeDtypeStruct(du.shape, F32), jax.ShapeDtypeStruct(d.shape, F32)),
        in_specs=[pl.BlockSpec(memory_space=pltpu.VMEM)] * len(args),
        out_specs=[pl.BlockSpec(memory_space=pltpu.HBM)] * 2,
        scratch_shapes=[
            pltpu.VMEM((kdev, 2, rows // 2, width), F32),
            pltpu.VMEM(d.shape, F32),
            pltpu.VMEM((kdev, 2, 8, width), F32),
            pltpu.SemaphoreType.DMA((4 + rows // 2 // 24,)),
        ],
        compiler_params=PARAMS,
        name="other_half",
    )(*map(vmem, args))


def swapped(x, axis, bit):
    return lax.ppermute(x, axis, [(i, i ^ bit) for i in range(lax.axis_size(axis))])


def body(elevation, equilibrium, depth, land_mask, friction_prev):
    rows = depth.shape[0]
    ntx, nty, ncons = (lax.axis_size(a) for a in ("tx", "ty", "cons"))
    fields = (elevation, equilibrium, depth, land_mask, friction_prev)
    m2, m1 = pack_columns(*fields)
    elev, equil, depth, mask, fric = elevation, equilibrium, depth, land_mask, friction_prev
    mask, mn, ms = pack(*fields, m1)
    f2 = lax.ppermute(m2, "tx", [(i, (i - 1 if i % 2 == 0 else i + 1) % ntx) for i in range(ntx)])
    f1 = swapped(m1, "tx", 1)
    e1, send, keep = first_sweep(elev, equil, depth, mask, fric, m1)
    mn, ms, my, send = merge(rows, f1, f2, mn, ms, send)
    recv = swapped(send, "cons", 1)
    if nty == 2:
        fn = fs = swapped(my, "ty", 1)
    else:
        fn = lax.ppermute(ms, "ty", [(i, i - 1) for i in range(1, nty)])
        fs = lax.ppermute(mn, "ty", [(i, i + 1) for i in range(nty - 1)])
    first, second, late = cut_sum(recv, keep, my)
    ss, sn, sw, se, rims, tail = rim(rows, m1, m2, f1, f2, mn, ms, fn, fs, late)
    prepared = prepare(e1, equil, depth, mask, ss, sn, sw, se)
    pieces = (first, second, tail)
    partner = [swapped(x, "cons", 2) for x in pieces]
    others = [swapped(rims, "cons", k) for k in range(1, ncons) if k != 2]
    mine, rims = joined(pieces, partner, others, prepared[2])
    bit = 4
    while bit < ncons:
        mine = added(mine, swapped(mine, "cons", bit))
        bit *= 2
    other = swapped(mine, "cons", 1)
    fields = (*prepared, depth, mask)
    return other_half(*fields, other, rims, *own_half(*fields, mine, rims, ss, sn, sw, se))


def solution(mesh):
    return jax.shard_map(
        body,
        mesh=mesh,
        in_specs=(
            P("cons", None, "ty", "tx"),
            P("cons", None, "ty", "tx"),
            P("ty", "tx"),
            P("ty", "tx"),
            P("ty", "tx"),
        ),
        out_specs=(P("cons", None, "ty", "tx"), P("ty", "tx")),
        check_vma=False,
    )
```

```python
import functools
import math

import jax
import jax.numpy as jnp
from jax import lax
from jax.experimental import pallas as pl
from jax.experimental.pallas import tpu as pltpu
from jax.sharding import PartitionSpec as P

OMEGA_TABLE = (1.0, 1.0351, 0.9582, 1.0379, 0.5181, 0.4816, 0.5164, 0.4454)
AY = 0.5
THETA = 0.05
DRAG = 0.5
BACKGROUND = 0.01
F32 = jnp.float32
LANES = 128
MSG = 16
TINY_DEPTH = 1e-6
PARAMS = pltpu.CompilerParams(vmem_limit_bytes=16 * 1024 * 1024)


def vmem(x):
    return pltpu.with_memory_space_constraint(x, pltpu.VMEM)


def hbm(x):
    return pltpu.with_memory_space_constraint(x, pltpu.HBM)


def recip(x):
    return pl.reciprocal(x, approx=True) if jnp.ndim(x) else 1.0 / x


def metric(rows, total):
    lat = (rows + 0.5) * (120.0 / total * math.pi / 180.0) - math.pi / 3.0
    s = lat * lat
    acc = jnp.full_like(s, 1.0 / math.factorial(16))
    for n in (14, 12, 10, 8, 6, 4, 2, 0):
        acc = ((-1.0) ** (n // 2)) / math.factorial(n) + s * acc
    return 0.5 / acc


def omegas(kdev):
    index = lax.axis_index("cons")
    out = []
    for c in range(kdev):
        w = jnp.float32(OMEGA_TABLE[c])
        for i in range(1, len(OMEGA_TABLE) // kdev):
            w = jnp.where(index == i, jnp.float32(OMEGA_TABLE[i * kdev + c]), w)
        out.append(w)
    return out


def rolled(x, shift, axis):
    return pltpu.roll(x, shift % x.shape[axis], axis)


def face(zr, zi, zr_next, zi_next, r2, coef, w2):
    g = coef * recip(r2 * r2 + w2 * w2)
    a = g * r2
    b = g * w2
    dr = zr - zr_next
    di = zi - zi_next
    return a * dr + b * di, a * di - b * dr


def flux(dr, di, g, a, w2):
    b = g * w2
    return a * dr + b * di, a * di - b * dr


def pack_columns_kernel(e_in, q_in, d_in, m_in, r_in, m2, m1, e, q, d, m, r, turned, behind, sems):
    rows, width = d_in.shape
    copies = []
    for s, side in enumerate((slice(0, LANES), slice(width - LANES, width))):
        for src, dst in ((e_in, e), (q_in, q)):
            copies.append((src.at[:, :, :, side], dst.at[s]))
        for src, dst in ((d_in, d), (m_in, m), (r_in, r)):
            copies.append((src.at[:, side], dst.at[s]))
    copies = [pltpu.make_async_copy(src, dst, sems.at[k]) for k, (src, dst) in enumerate(copies)]
    for copy in copies:
        copy.start()
    for copy in copies:
        copy.wait()
    lane = lax.broadcasted_iota(jnp.int32, (rows, LANES), 1)

    def edges(plane):
        return jnp.where(lane < LANES // 2, plane(0), plane(1))

    elev = [edges(lambda s: e[s, c, p]) for p in range(2) for c in range(2)]
    equil = [edges(lambda s: q[s, c, p]) for p in range(2) for c in range(2)]
    planes = [x - y for x, y in zip(elev, equil)]
    planes += [edges(lambda s: r[s]), edges(lambda s: d[s]), edges(lambda s: m[s]).astype(F32)]
    both = jnp.zeros((rows, LANES), F32)
    for k, plane in enumerate(planes + elev):
        both = jnp.where((lane >= 4 * k) & (lane < 4 * k + 4), rolled(plane, 4 * k + 2, 1), both)
    pad = turned.shape[1]
    turned[...] = jnp.concatenate([both, jnp.zeros((pad - rows, LANES), F32)], axis=0).T
    odd = lax.rem(lax.axis_index("tx"), 2)
    first = (lax.axis_index("ty") * rows).astype(F32)
    lat_row = jnp.minimum(lax.broadcasted_iota(jnp.int32, (8, pad), 1), rows).astype(F32) + first
    ax = metric(lat_row, rows * lax.axis_size("ty"))
    w0, w1 = omegas(2)
    w2 = 2.0 * jnp.where(lax.broadcasted_iota(jnp.int32, (8, pad), 0) < 4, w0, w1)
    up = lambda x: rolled(x, -1, 0)
    zr, zi = turned[0:8, :], turned[8:16, :]
    r8, d8, m8 = (jnp.concatenate([turned[at : at + 4, :]] * 2, axis=0) for at in (16, 20, 24))
    coef = (THETA * ax * ax) * (m8 * up(m8) * (d8 + up(d8)))
    behind[0:8, :], behind[8:16, :] = face(zr, zi, up(zr), up(zi), r8 + up(r8), coef, w2)
    for out, west in ((m1, odd), (m2, 1 - odd)):
        lanes = slice(0, out.shape[1])
        for k in range(4):
            out[k : k + 1, :] = turned[pl.ds(4 * k + 1 + west, 1), lanes]
            out[4 + k : 5 + k, :] = behind[pl.ds(4 * k + 2 * west, 1), lanes]
            out[8 + k : 9 + k, :] = turned[pl.ds(4 * (7 + k) + 1 + west, 1), lanes]
        for k in range(3):
            out[12 + k : 13 + k, :] = turned[pl.ds(4 * (4 + k) + 1 + west, 1), lanes]
        out[MSG - 1 :, :] = jnp.zeros((1, out.shape[1]), F32)


def pack_columns(elevation, equilibrium, depth, land_mask, friction):
    kdev, _, rows, width = elevation.shape
    pad = -(-rows // LANES) * LANES
    cut, plane = pltpu.VMEM((2, kdev, 2, rows, LANES), F32), pltpu.VMEM((2, rows, LANES), F32)
    return pl.pallas_call(
        pack_columns_kernel,
        out_shape=(pltpu.VMEM((MSG, rows), F32), pltpu.VMEM((MSG, pad), F32)),
        in_specs=[pl.BlockSpec(memory_space=pltpu.HBM)] * 5,
        out_specs=[pl.BlockSpec(memory_space=pltpu.VMEM)] * 2,
        scratch_shapes=[
            cut,
            cut,
            plane,
            pltpu.VMEM((2, rows, LANES), jnp.int32),
            plane,
            pltpu.VMEM((LANES, pad), F32),
            pltpu.VMEM((16, pad), F32),
            pltpu.SemaphoreType.DMA((10,)),
        ],
        compiler_params=PARAMS,
        name="pack_columns",
    )(*map(hbm, (elevation, equilibrium, depth, land_mask, friction)))


def pack_kernel(e, q, d, ints, r, after, m, mn, ms):
    del after
    kdev, _, rows, width = e.shape
    m[...] = ints[...].astype(F32)
    ws = omegas(kdev)
    for out, end, near, low in ((ms, slice(0, 8), 0, 0), (mn, slice(rows - 8, rows), 7, 6)):
        out[:, width:] = jnp.zeros((MSG, LANES), F32)
        r8, d8, m8 = r[end, :], d[end, :], m[end, :]
        up = lambda x: rolled(x, -1, 0)
        coef = (THETA * AY * AY) * (m8 * up(m8) * (d8 + up(d8)))
        r2 = r8 + up(r8)
        for c in range(kdev):
            elev = [e[c, p, end, :] for p in range(2)]
            z = [elev[p] - q[c, p, end, :] for p in range(2)]
            v = face(z[0], z[1], up(z[0]), up(z[1]), r2, coef, 2.0 * ws[c])
            for p in range(2):
                out[2 * p + c, :width] = z[p][near, :]
                out[4 + 2 * p + c, :width] = v[p][low, :]
                out[8 + 2 * p + c, :width] = elev[p][near, :]
        for k, plane in enumerate((r8, d8, m8)):
            out[12 + k, :width] = plane[near, :]
        out[MSG - 1, :width] = jnp.zeros((width,), F32)


def pack(elevation, equilibrium, depth, land_mask, friction, after):
    kdev, _, rows, width = elevation.shape
    plane = pltpu.VMEM(depth.shape, F32)
    row = pltpu.VMEM((MSG, width + LANES), F32)
    return pl.pallas_call(
        pack_kernel,
        out_shape=(plane, row, row),
        in_specs=[pl.BlockSpec(memory_space=pltpu.VMEM)] * 6,
        out_specs=[pl.BlockSpec(memory_space=pltpu.VMEM)] * 3,
        compiler_params=PARAMS,
        name="pack",
    )(*map(vmem, (elevation, equilibrium, depth, land_mask, friction, after)))


def tile_rows(ref, at, size, nxt):
    here = ref[at : at + size, :]
    after = ref[nxt : nxt + 8, :]
    return here, jnp.concatenate([here[1:], after[0:1]], axis=0)


def east(x):
    return rolled(x, -1, 1)


def row_metric(at, size, width, rows):
    first = lax.axis_index("ty") * rows
    index = lax.broadcasted_iota(jnp.int32, (size, LANES), 0) + (first + at)
    ax = metric(index.astype(F32), rows * lax.axis_size("ty"))
    return ax, jnp.concatenate([ax] * (width // LANES), axis=1)


def first_kernel(e, q, d, mask, r, after, e1, send, keep, coef, var):
    del after
    kdev, _, rows, width = e.shape
    size = 16
    ws = omegas(kdev)
    last_v = [jnp.zeros((1, width), F32)] * (2 * kdev)
    for at in range(0, rows, size):
        nxt = min(at + size, rows - 8)
        _, ax = row_metric(at, size, width, rows)
        md, mn = tile_rows(mask, at, size, nxt)
        dd, dn = tile_rows(d, at, size, nxt)
        rd, rn = tile_rows(r, at, size, nxt)
        coef_u = (THETA * ax * ax) * (md * east(md) * (dd + east(dd)))
        coef_v = (THETA * AY * AY) * (md * mn * (dd + dn))
        coef[0, at : at + size, :], coef[1, at : at + size, :] = coef_u, coef_v
        r2u = rd + east(rd)
        r2v = rd + rn
        squ, sqv = r2u * r2u, r2v * r2v
        sum_u = sum_v = None
        for c in range(kdev):
            w2 = 2.0 * ws[c]
            wt = THETA * ws[c]
            er, ern = tile_rows(e.at[c, 0], at, size, nxt)
            ei, ein = tile_rows(e.at[c, 1], at, size, nxt)
            qr, qrn = tile_rows(q.at[c, 0], at, size, nxt)
            qi, qin = tile_rows(q.at[c, 1], at, size, nxt)
            zr, zi = er - qr, ei - qi
            gu = coef_u * recip(squ + w2 * w2)
            gv = coef_v * recip(sqv + w2 * w2)
            ur, ui = flux(zr - east(zr), zi - east(zi), gu, gu * r2u, w2)
            vr, vi = flux(zr - (ern - qrn), zi - (ein - qin), gv, gv * r2v, w2)
            uwr, uwi = rolled(ur, 1, 1), rolled(ui, 1, 1)
            vsr = jnp.concatenate([last_v[2 * c], vr[:-1]], axis=0)
            vsi = jnp.concatenate([last_v[2 * c + 1], vi[:-1]], axis=0)
            last_v[2 * c], last_v[2 * c + 1] = vr[-1:], vi[-1:]
            e1[c, 0, at : at + size, :] = md * (er + wt * ei - (ur - uwr) - (vr - vsr))
            e1[c, 1, at : at + size, :] = md * (ei - wt * er - (ui - uwi) - (vi - vsi))
            su = (ur + uwr) * (ur + uwr) + (ui + uwi) * (ui + uwi)
            sv = (vr + vsr) * (vr + vsr) + (vi + vsi) * (vi + vsi)
            sum_u = su if sum_u is None else sum_u + su
            sum_v = sv if sum_v is None else sum_v + sv
        inv = recip(dd)
        ia = recip(THETA * ax)
        total = (0.125 * ia * ia) * sum_u + (0.125 / (THETA * AY) ** 2) * sum_v
        var[at : at + size, :] = total * (inv * inv)
    half = rows // 2
    core = lax.rem(lax.axis_index("cons"), 2)
    send[:half, :] = var[pl.ds(pl.multiple_of((1 - core) * half, 8), half), :]
    keep[:half, :] = var[pl.ds(pl.multiple_of(core * half, 8), half), :]
    send[half:, :] = keep[half - 8 : half, :]
    keep[half:, :] = send[half - 8 : half, :]


def first_sweep(e, q, d, m, r, after):
    kdev, _, rows, width = e.shape
    half = pltpu.VMEM((rows // 2 + 8, width), F32)
    return pl.pallas_call(
        first_kernel,
        out_shape=(pltpu.VMEM(e.shape, F32), half, half, pltpu.VMEM((2, *d.shape), F32)),
        in_specs=[pl.BlockSpec(memory_space=pltpu.VMEM)] * 6,
        out_specs=[pl.BlockSpec(memory_space=pltpu.VMEM)] * 4,
        scratch_shapes=[pltpu.VMEM(d.shape, F32)],
        compiler_params=PARAMS,
        cost_estimate=pl.CostEstimate(flops=80 * e.size, bytes_accessed=160 * e.size, transcendentals=0),
        name="first_sweep",
    )(*map(vmem, (e, q, d, m, r, after)))


def add_kernel(a, b, *refs):
    refs[-1][...] = a[...] + b[...]


def added(a, b, *after):
    return pl.pallas_call(
        add_kernel,
        out_shape=pltpu.VMEM(a.shape, F32),
        in_specs=[pl.BlockSpec(memory_space=pltpu.VMEM)] * (2 + len(after)),
        out_specs=pl.BlockSpec(memory_space=pltpu.VMEM),
        compiler_params=PARAMS,
        name="added",
    )(vmem(a), vmem(b), *map(vmem, after))


def cut_kernel(a, b, after, *outs):
    del after
    at = 0
    for out in outs:
        here = slice(at, at + out.shape[0])
        out[...] = a[here, :] + b[here, :]
        at += out.shape[0]


def cut_sum(a, b, after):
    rows, width = a.shape
    large = pltpu.VMEM(((rows - 16) // 2, width), F32)
    return pl.pallas_call(
        cut_kernel,
        out_shape=(large, large, pltpu.VMEM((16, width), F32)),
        in_specs=[pl.BlockSpec(memory_space=pltpu.VMEM)] * 3,
        out_specs=[pl.BlockSpec(memory_space=pltpu.VMEM)] * 3,
        compiler_params=PARAMS,
        name="cut_sum",
    )(vmem(a), vmem(b), vmem(after))


def tree_sum(terms):
    while len(terms) > 1:
        terms = [a + b for a, b in zip(terms[::2], terms[1::2])]
    return terms[0]


def early_kernel(after, *refs):
    del after
    pieces, partner, outs = refs[:2], refs[2:4], refs[4:]
    thin = outs[0].shape[0]
    for k, out in enumerate(outs):
        part, at = divmod(k * thin, pieces[0].shape[0])
        out[...] = pieces[part][at : at + thin, :] + partner[part][at : at + thin, :]


def early_sums(pieces, partner, after):
    rows, width = pieces[0].shape
    count = 2 * rows // 16
    return pl.pallas_call(
        early_kernel,
        out_shape=(pltpu.VMEM((16, width), F32),) * count,
        in_specs=[pl.BlockSpec(memory_space=pltpu.VMEM)] * 5,
        out_specs=[pl.BlockSpec(memory_space=pltpu.VMEM)] * count,
        compiler_params=PARAMS,
        name="early_sums",
    )(*map(vmem, (after, *pieces, *partner)))


def join_kernel(tail, partner, *refs):
    *others, late, rims = refs
    late[...] = tail[:16, :] + partner[:16, :]
    terms = [x[...] for x in others]
    rims[...] = tree_sum([tail[16:, :], terms[0], partner[16:, :], *terms[1:]])


def joined(*args):
    width = args[0].shape[1]
    return pl.pallas_call(
        join_kernel,
        out_shape=(pltpu.VMEM((16, width), F32), pltpu.VMEM((8, width), F32)),
        in_specs=[pl.BlockSpec(memory_space=pltpu.VMEM)] * len(args),
        out_specs=[pl.BlockSpec(memory_space=pltpu.VMEM)] * 2,
        compiler_params=PARAMS,
        name="joined",
    )(*map(vmem, args))


def roles(a, b):
    even = lax.rem(lax.axis_index("tx"), 2) == 0
    return jnp.where(even, b, a), jnp.where(even, a, b)


def padded(x, pad):
    return jnp.concatenate([x, jnp.zeros((x.shape[0], pad - x.shape[1]), F32)], axis=1)


def merge_kernel(rows, f2, f1, mn, ms, send, mn_out, ms_out, my_out, send_out):
    width = mn.shape[1] - LANES
    fw, fe = roles(f1[...], padded(f2[...], f1.shape[1]))
    lane = lax.broadcasted_iota(jnp.int32, (MSG, LANES), 1)
    last = LANES - 1

    def ends(at):
        east_, west = fe[:, at // LANES * LANES :][:, :LANES], fw[:, at // LANES * LANES :][:, :LANES]
        east_, west = rolled(east_, -(at % LANES), 1), rolled(west, last - at % LANES, 1)
        return jnp.where(lane == 0, east_, jnp.where(lane == last, west, 0.0))

    mn_out[:, :width] = mn[:, :width]
    ms_out[:, :width] = ms[:, :width]
    mn_out[:, width:] = ends(rows - 1)
    ms_out[:, width:] = ends(0)
    low = lax.axis_index("ty") == 0
    my_out[...] = jnp.where(low, mn_out[...], ms_out[...])
    send_out[...] = send[...]


def merge(rows, f1, f2, mn, ms, send):
    out = pltpu.VMEM(mn.shape, F32)
    return pl.pallas_call(
        functools.partial(merge_kernel, rows),
        out_shape=(out, out, out, pltpu.VMEM(send.shape, F32)),
        in_specs=[pl.BlockSpec(memory_space=pltpu.VMEM)] * 5,
        out_specs=[pl.BlockSpec(memory_space=pltpu.VMEM)] * 4,
        compiler_params=PARAMS,
        name="merge",
    )(*map(vmem, (f2, f1, mn, ms, send)))


def strip_omega(shape, ws):
    odd = lax.rem(lax.broadcasted_iota(jnp.int32, shape, 0), 2)
    return jnp.where(odd == 0, ws[0], ws[1])


def strip_sweep(low, high, ws, g_across, g_along):
    none = jnp.zeros((2, low.shape[1]), F32)

    def field(at):
        return jnp.concatenate([none, low[at : at + 2], high[at : at + 2], none], axis=0)

    def single(at):
        a, b = low[at : at + 1], high[at : at + 1]
        return jnp.concatenate([none, a, a, b, b, none], axis=0)

    def given(at):
        return jnp.concatenate([low[at : at + 2], none, high[at : at + 2], none], axis=0)

    zr, zi, er, ei = field(0), field(2), field(8), field(10)
    r, d, m = single(12), single(13), single(14)
    w = strip_omega(zr.shape, ws)
    w2 = 2.0 * w
    wt = THETA * w
    up = lambda x: rolled(x, -2, 0)
    nx = lambda x: rolled(x, -1, 1)
    coef_a = (THETA * g_across * g_across) * (m * up(m) * (d + up(d)))
    coef_l = (THETA * g_along * g_along) * (m * nx(m) * (d + nx(d)))
    ar, ai = face(zr, zi, up(zr), up(zi), r + up(r), coef_a, w2)
    middle = lax.broadcasted_iota(jnp.int32, zr.shape, 0) // 2 == 1
    ar, ai = jnp.where(middle, ar, given(4)), jnp.where(middle, ai, given(6))
    lr, li = face(zr, zi, nx(zr), nx(zi), r + nx(r), coef_l, w2)
    abr, abi = rolled(ar, 2, 0), rolled(ai, 2, 0)
    lbr, lbi = rolled(lr, 1, 1), rolled(li, 1, 1)
    e1r = m * (er + wt * ei - (ar - abr) - (lr - lbr))
    e1i = m * (ei - wt * er - (ai - abi) - (li - lbi))
    sa = (ar + abr) * (ar + abr) + (ai + abi) * (ai + abi)
    sl = (lr + lbr) * (lr + lbr) + (li + lbi) * (li + lbi)
    inv = recip(jnp.maximum(d, TINY_DEPTH))
    ia = recip(THETA * g_across)
    il = recip(THETA * g_along)
    var = 0.125 * (ia * ia * sa + il * il * sl) * (inv * inv)
    var = var + rolled(var, -1, 0)
    z1r = e1r - (er - zr)
    z1i = e1i - (ei - zi)
    return (z1r, z1i, d, coef_a, e1r, e1i), var


def strips(rows, m2, m1, f2, f1, mn, ms, fn_ref, fs_ref):
    kdev = 2
    width = mn.shape[1] - LANES
    pad = m1.shape[1]
    ws = omegas(kdev)
    ty, count = lax.axis_index("ty"), lax.axis_size("ty")
    first = (ty * rows).astype(F32)
    total = rows * count
    fn = jnp.where(ty < count - 1, fn_ref[...], 0.0)
    fs = jnp.where(ty > 0, fs_ref[...], 0.0)

    ay = AY
    line = lax.broadcasted_iota(jnp.int32, (8, LANES), 0) // 2
    out = []
    for low, high, start in ((fs, ms[...], -2), (mn[...], fn, rows - 2)):
        ax = metric((line + start).astype(F32) + first, total)
        ax = jnp.concatenate([ax] * (low.shape[1] // LANES), axis=1)
        out.append(strip_sweep(low, high, ws, ay, ax))

    mw, me = roles(m1[...], padded(m2[...], pad))
    fw, fe = roles(f1[...], padded(f2[...], pad))
    hi = rows - (pad - LANES)
    last = LANES - 1
    lane = lax.broadcasted_iota(jnp.int32, (MSG, LANES), 1)

    def ended(msg, block, at):
        end = msg[:, pad - LANES :]
        end = jnp.where(lane == hi, rolled(fn[:, block : block + LANES], hi - at, 1), end)
        end = jnp.where(lane == last, rolled(fs[:, block : block + LANES], last - at, 1), end)
        return jnp.concatenate([msg[:, : pad - LANES], end], axis=1)

    low_w, high_w = ended(fw, width, last), ended(mw, 0, 0)
    low_e, high_e = ended(me, width - LANES, last), ended(fe, width, 0)
    row = lax.broadcasted_iota(jnp.int32, (8, pad), 1).astype(F32) + first
    ax = metric(jnp.minimum(row, first + rows), total)
    for low, high in ((low_w, high_w), (low_e, high_e)):
        out.append(strip_sweep(low, high, ws, ax, ay))
    return out


def rim_kernel(rows, after, *refs):
    del after
    *refs, row_sums, col_sums = refs
    width, pad = row_sums.shape[1], refs[1].shape[1]
    for k, (_, var) in enumerate(strips(rows, *refs)):
        for p in range(2):
            if k < 2:
                row_sums[2 * k + p, :] = var[2 + 2 * p, :width]
            else:
                col_sums[k - 2, p * pad : (p + 1) * pad] = var[2 + 2 * p, :]
    col_sums[2:, :] = jnp.zeros((2, width), F32)


def strips_kernel(rows, *refs):
    for out, (held, _) in zip(refs[-4:], strips(rows, *refs[:-4])):
        for k, x in enumerate(held):
            out[8 * k : 8 * k + 8, :] = x


def rim(rows, late, *messages):
    width = late.shape[1]
    return pl.pallas_call(
        functools.partial(rim_kernel, rows),
        out_shape=(pltpu.VMEM((4, width), F32),) * 2,
        in_specs=[pl.BlockSpec(memory_space=pltpu.VMEM)] * 9,
        out_specs=[pl.BlockSpec(memory_space=pltpu.VMEM)] * 2,
        compiler_params=PARAMS,
        name="rim",
    )(*map(vmem, (late, *messages)))


def stack_kernel(a, b, out):
    out[: a.shape[0], :] = a[...]
    out[a.shape[0] :, :] = b[...]


def stacked(a, b):
    return pl.pallas_call(
        stack_kernel,
        out_shape=pltpu.VMEM((a.shape[0] + b.shape[0], a.shape[1]), F32),
        in_specs=[pl.BlockSpec(memory_space=pltpu.VMEM)] * 2,
        out_specs=pl.BlockSpec(memory_space=pltpu.VMEM),
        compiler_params=PARAMS,
        name="stacked",
    )(vmem(a), vmem(b))


def held_strips(rows, *messages):
    row = pltpu.VMEM((48, messages[4].shape[1]), F32)
    col = pltpu.VMEM((48, messages[1].shape[1]), F32)
    return pl.pallas_call(
        functools.partial(strips_kernel, rows),
        out_shape=(row, row, col, col),
        in_specs=[pl.BlockSpec(memory_space=pltpu.VMEM)] * 8,
        out_specs=[pl.BlockSpec(memory_space=pltpu.VMEM)] * 4,
        compiler_params=PARAMS,
        name="held_strips",
    )(*map(vmem, messages))


def prepare_kernel(e1_in, q, m, ss, sn, sw, se, du, dv, base, e1, cols):
    kdev, _, rows, width = e1_in.shape
    size = 16
    ws = omegas(kdev)
    e1[...] = e1_in[...]
    for p in range(2):
        cols[2 * p : 2 * p + 2, :] = sw[8 * (4 + p) + 4 : 8 * (4 + p) + 6, :]
        cols[4 + 2 * p : 6 + 2 * p, :] = se[8 * (4 + p) + 2 : 8 * (4 + p) + 4, :]
    turned = cols[...].T
    lane = lax.broadcasted_iota(jnp.int32, (rows, LANES), 1)
    left, right = slice(0, LANES), slice(width - LANES, width)
    last = LANES - 1
    for p in range(2):
        for c in range(kdev):
            e1[c, p, 0:1, :] = ss[8 * (4 + p) + 4 + c : 8 * (4 + p) + 5 + c, :width]
            e1[c, p, rows - 1 : rows, :] = sn[8 * (4 + p) + 2 + c : 8 * (4 + p) + 3 + c, :width]
            k = 2 * p + c
            e1[c, p, :, left] = jnp.where(lane == 0, rolled(turned[:rows], -k, 1), e1[c, p, :, left])
            k = 4 + 2 * p + c
            e1[c, p, :, right] = jnp.where(lane == last, rolled(turned[:rows], last - k, 1), e1[c, p, :, right])
    for at in range(0, rows, size):
        nxt = min(at + size, rows - 8)
        here = slice(at, at + size)
        md = m[here, :]
        for c in range(kdev):
            wt = THETA * ws[c]
            er, ern = tile_rows(e1.at[c, 0], at, size, nxt)
            ei, ein = tile_rows(e1.at[c, 1], at, size, nxt)
            qr, qrn = tile_rows(q.at[c, 0], at, size, nxt)
            qi, qin = tile_rows(q.at[c, 1], at, size, nxt)
            zr, zi = er - qr, ei - qi
            du[c, 0, here, :] = zr - east(zr)
            du[c, 1, here, :] = zi - east(zi)
            dv[c, 0, here, :] = zr - (ern - qrn)
            dv[c, 1, here, :] = zi - (ein - qin)
            base[c, 0, here, :] = md * (er + wt * ei)
            base[c, 1, here, :] = md * (ei - wt * er)


def prepare(e1, q, m, ss, sn, sw, se):
    plane = pltpu.VMEM(e1.shape, F32)
    return pl.pallas_call(
        prepare_kernel,
        out_shape=(plane, plane, plane),
        in_specs=[pl.BlockSpec(memory_space=pltpu.VMEM)] * 7,
        out_specs=[pl.BlockSpec(memory_space=pltpu.VMEM)] * 3,
        scratch_shapes=[pltpu.VMEM(e1.shape, F32), pltpu.VMEM((LANES, sw.shape[1]), F32)],
        compiler_params=PARAMS,
        cost_estimate=pl.CostEstimate(flops=40 * e1.size, bytes_accessed=160 * e1.size, transcendentals=0),
        name="prepare",
    )(*map(vmem, (e1, q, m, ss, sn, sw, se)))


def rate(var, d):
    s = var + BACKGROUND
    return (DRAG * (s * lax.rsqrt(s))) * recip(d)


def sweep_tile(row, size, r, r_north, du, dv, base, coef, m, turned, ws, last_v, top):
    kdev, width = du.shape[0], du.shape[3]
    here = pl.ds(row, size)
    edges = turned[here, :]
    md = m[here, :]
    coef_u, coef_v = coef[0, here, :], coef[1, here, :]
    r2u = r + east(r)
    r2v = r + r_north
    squ, sqv = r2u * r2u, r2v * r2v
    lane = lax.broadcasted_iota(jnp.int32, (size, LANES), 1)
    last = LANES - 1

    def with_east(u, k):
        block = jnp.where(lane == last, rolled(edges, last - k, 1), u[:, width - LANES :])
        return jnp.concatenate([u[:, : width - LANES], block], axis=1)

    def from_west(u, k):
        u = rolled(u, 1, 1)
        block = jnp.where(lane == 0, rolled(edges, -k, 1), u[:, :LANES])
        return jnp.concatenate([block, u[:, LANES:]], axis=1)

    planes, out_v = {}, {}
    for c in range(kdev):
        w2 = 2.0 * ws[c]
        gu = coef_u * recip(squ + w2 * w2)
        gv = coef_v * recip(sqv + w2 * w2)
        u = flux(du[c, 0, here, :], du[c, 1, here, :], gu, gu * r2u, w2)
        v = flux(dv[c, 0, here, :], dv[c, 1, here, :], gv, gv * r2v, w2)
        for p in range(2):
            up, vp = with_east(u[p], 4 + 2 * p + c), v[p]
            if top is not None:
                vp = jnp.concatenate([vp[:-1], top(c, p, vp[-1:])], axis=0)
            uw = from_west(up, 2 * p + c)
            vs = jnp.concatenate([last_v[c, p], vp[:-1]], axis=0)
            out_v[c, p] = vp[-1:]
            planes[c, p] = base[c, p, here, :], md * ((up - uw) + (vp - vs))
    return planes, out_v


def pairs(kdev):
    return [(c, p) for c in range(kdev) for p in range(2)]


def half_rate(var, rims, turned, d, row, low, half):
    here = pl.ds(row, half)
    edges = turned[here, :]
    width = var.shape[1]
    index = lax.broadcasted_iota(jnp.int32, (8, width), 0)
    first = jnp.where(low & (index == 0), rims[1:2], var[:8])
    final = jnp.where(jnp.logical_not(low) & (index == 7), rims[2:3], var[half - 8 :])
    var = jnp.concatenate([first, var[8 : half - 8], final], axis=0)
    lane = lax.broadcasted_iota(jnp.int32, (half, LANES), 1)
    left = jnp.where(lane == 0, rolled(edges, -8, 1), var[:, :LANES])
    right = jnp.where(lane == LANES - 1, rolled(edges, LANES - 1 - 9, 1), var[:, width - LANES :])
    return rate(jnp.concatenate([left, var[:, LANES : width - LANES], right], axis=1), d[here, :])


def own_kernel(du, dv, base, coef, d, m, late, rims_ref, ss, sn, sw, se, *refs):
    *mine, first_part, update, fric, vs_out, vn_out, turned, cols = refs
    kdev, _, half, width = update.shape
    pad = sw.shape[1]
    ws = omegas(kdev)
    core = lax.rem(lax.axis_index("cons"), 2)
    low = core == 0
    rims = rims_ref[...]

    def edge(strip, var_a, var_b):
        zr, zi, dep, ca = (strip[8 * k : 8 * k + 8, :] for k in range(4))
        var = jnp.concatenate([var_a, var_a, var_a, var_a, var_b, var_b, var_b, var_b], axis=0)
        f = rate(var, jnp.maximum(dep, TINY_DEPTH))
        up = lambda x: rolled(x, -2, 0)
        w2 = 2.0 * strip_omega(zr.shape, ws)
        return face(zr, zi, up(zr), up(zi), f + up(f), ca, w2)

    none = jnp.zeros((1, LANES), F32)
    wide = lambda x: jnp.concatenate([x, none], axis=1)
    south = edge(ss, wide(rims[0:1]), wide(rims[1:2]))
    north = edge(sn, wide(rims[2:3]), wide(rims[3:4]))
    west = edge(sw, rims[4:5, :pad], rims[4:5, pad : 2 * pad])
    east_ = edge(se, rims[5:6, :pad], rims[5:6, pad : 2 * pad])
    for p in range(2):
        cols[2 * p : 2 * p + 2, :] = west[p][2:4]
        cols[4 + 2 * p : 6 + 2 * p, :] = east_[p][2:4]
        for c in range(kdev):
            vs_out[2 * c + p : 2 * c + p + 1, :] = south[p][2 + c : 3 + c, :width]
            vn_out[2 * c + p : 2 * c + p + 1, :] = north[p][2 + c : 3 + c, :width]
    cols[8:9, :] = rims[4:5, pad : 2 * pad]
    cols[9:10, :] = rims[5:6, :pad]
    turned[...] = cols[...].T

    first = pl.multiple_of(core * half, 8)
    var = jnp.concatenate([x[...] for x in mine] + [late[:8, :]], axis=0)
    fric[...] = half_rate(var, rims, turned, d, first, low, half)
    size = 24
    last_v = {(c, p): jnp.where(low, vs_out[2 * c + p : 2 * c + p + 1, :], 0.0) for c, p in pairs(kdev)}

    def top(c, p, own):
        return jnp.where(low, 0.0, vn_out[2 * c + p : 2 * c + p + 1, :])

    for at in range(0, half, size):
        r, rn = tile_rows(fric, at, size, min(at + size, half - 8))
        planes, last_v = sweep_tile(
            pl.multiple_of(first + at, 8), size, r, rn, du, dv, base, coef, m, turned, ws, last_v,
            top if at + size == half else None,
        )
        for c, p in pairs(kdev):
            first_part[c, p, at : at + size, :], update[c, p, at : at + size, :] = planes[c, p]


def own_half(*args):
    kdev, _, rows, width = args[0].shape
    pad = args[10].shape[1]
    line = pltpu.VMEM((8, width), F32)
    return pl.pallas_call(
        own_kernel,
        out_shape=(
            pltpu.VMEM((kdev, 2, rows // 2, width), F32),
            pltpu.VMEM((kdev, 2, rows // 2, width), F32),
            pltpu.VMEM((rows // 2, width), F32),
            line,
            line,
            pltpu.VMEM((pad, LANES), F32),
        ),
        in_specs=[pl.BlockSpec(memory_space=pltpu.VMEM)] * len(args),
        out_specs=[pl.BlockSpec(memory_space=pltpu.VMEM)] * 6,
        scratch_shapes=[pltpu.VMEM((LANES, pad), F32)],
        compiler_params=PARAMS,
        name="own_half",
    )(*map(vmem, args))


def other_kernel(du, dv, base, coef, d, m, late, rims, eta_own, fric_own, vs, vn, turned, *refs):
    *other, eta_out, fric_out, eta, fric, fixed, sems = refs
    kdev, _, half, width = eta.shape
    ws = omegas(kdev)
    core = lax.rem(lax.axis_index("cons"), 2)
    own_low = core == 0
    own, first = pl.multiple_of(core * half, 8), pl.multiple_of((1 - core) * half, 8)
    copies = []

    def put(src, dst):
        copy = pltpu.make_async_copy(src, dst, sems.at[len(copies)])
        copy.start()
        copies.append(copy)

    skip = pl.multiple_of(core * 8, 8)
    put(
        eta_own.at[:, :, pl.ds(skip, half - 8), :],
        eta_out.at[:, :, pl.ds(pl.multiple_of(own + skip, 8), half - 8), :],
    )
    put(fric_own, fric_out.at[pl.ds(own, half), :])
    fric[pl.ds(own, half), :] = fric_own[...]
    fric[pl.ds(first, half), :] = half_rate(
        jnp.concatenate([x[...] for x in other] + [late[8:, :]], axis=0),
        rims[...], turned, d, first, jnp.logical_not(own_low), half,
    )
    put(fric.at[pl.ds(first, half), :], fric_out.at[pl.ds(first, half), :])

    r, rn = tile_rows(fric, half - 8, 8, half)
    r2 = r + rn
    between = {}
    for c in range(kdev):
        w2 = 2.0 * ws[c]
        g = coef[1, half - 8 : half, :] * recip(r2 * r2 + w2 * w2)
        v = flux(dv[c, 0, half - 8 : half, :], dv[c, 1, half - 8 : half, :], g, g * r2, w2)
        for p in range(2):
            between[c, p] = v[p][7:8]
    index = lax.broadcasted_iota(jnp.int32, (8, width), 0)
    at_face = index == jnp.where(own_low, 7, 0)
    sign = jnp.where(own_low, -1.0, 1.0)
    local = pl.ds(pl.multiple_of((1 - core) * (half - 8), 8), 8)
    border = pl.ds(pl.multiple_of(half - 8 + 8 * core, 8), 8)
    md = m[border, :]
    for c, p in pairs(kdev):
        fixed[c, p] = eta_own[c, p, local, :] + jnp.where(at_face, sign * (md * between[c, p]), 0.0)
    put(fixed, eta_out.at[:, :, border, :])

    size = 24
    rows = 2 * half
    last_v = {(c, p): jnp.where(own_low, between[c, p], vs[2 * c + p : 2 * c + p + 1, :]) for c, p in pairs(kdev)}

    def top(c, p, own_v):
        return jnp.where(own_low, vn[2 * c + p : 2 * c + p + 1, :], own_v)

    for at in range(0, half, size):
        row = pl.multiple_of(first + at, 8)
        r = fric[pl.ds(row, size), :]
        after = fric[pl.ds(pl.multiple_of(jnp.minimum(row + size, rows - 8), 8), 8), :]
        rn = jnp.concatenate([r[1:], after[0:1]], axis=0)
        planes, last_v = sweep_tile(
            row, size, r, rn, du, dv, base, coef, m, turned, ws, last_v, top if at + size == half else None
        )
        for c, p in pairs(kdev):
            eta[c, p, at : at + size, :] = planes[c, p][0] - planes[c, p][1]
        put(eta.at[:, :, at : at + size, :], eta_out.at[:, :, pl.ds(row, size), :])
    for copy in copies:
        copy.wait()


def other_half(*args):
    du, d = args[0], args[4]
    kdev, _, rows, width = du.shape
    return pl.pallas_call(
        other_kernel,
        out_shape=(jax.ShapeDtypeStruct(du.shape, F32), jax.ShapeDtypeStruct(d.shape, F32)),
        in_specs=[pl.BlockSpec(memory_space=pltpu.VMEM)] * len(args),
        out_specs=[pl.BlockSpec(memory_space=pltpu.HBM)] * 2,
        scratch_shapes=[
            pltpu.VMEM((kdev, 2, rows // 2, width), F32),
            pltpu.VMEM(d.shape, F32),
            pltpu.VMEM((kdev, 2, 8, width), F32),
            pltpu.SemaphoreType.DMA((4 + rows // 2 // 24,)),
        ],
        compiler_params=PARAMS,
        name="other_half",
    )(*map(vmem, args))


def swapped(x, axis, bit):
    return lax.ppermute(x, axis, [(i, i ^ bit) for i in range(lax.axis_size(axis))])


def body(elevation, equilibrium, depth, land_mask, friction_prev):
    rows = depth.shape[0]
    ntx, nty, ncons = (lax.axis_size(a) for a in ("tx", "ty", "cons"))
    fields = (elevation, equilibrium, depth, land_mask, friction_prev)
    m2, m1 = pack_columns(*fields)
    elev, equil, depth, mask, fric = elevation, equilibrium, depth, land_mask, friction_prev
    mask, mn, ms = pack(*fields, m1)
    f2 = lax.ppermute(m2, "tx", [(i, (i - 1 if i % 2 == 0 else i + 1) % ntx) for i in range(ntx)])
    f1 = swapped(m1, "tx", 1)
    e1, send, keep, coef = first_sweep(elev, equil, depth, mask, fric, m1)
    mn, ms, my, send = merge(rows, f1, f2, mn, ms, send)
    recv = swapped(send, "cons", 1)
    if nty == 2:
        fn = fs = swapped(my, "ty", 1)
    else:
        fn = lax.ppermute(ms, "ty", [(i, i - 1) for i in range(1, nty)])
        fs = lax.ppermute(mn, "ty", [(i, i + 1) for i in range(nty - 1)])
    first, second, late = cut_sum(recv, keep, my)
    messages = (m2, m1, f2, f1, mn, ms, fn, fs)
    rims = jnp.concatenate(rim(rows, late, *messages), axis=0)
    tail = stacked(late, rims)
    ss, sn, sw, se = held_strips(rows, *messages)
    prepared = prepare(e1, equil, mask, ss, sn, sw, se)
    partner = [swapped(x, "cons", 2) for x in (first, second, tail)]
    others = [swapped(rims, "cons", k) for k in range(1, ncons) if k != 2]
    mine = early_sums((first, second), partner[:2], prepared[2])
    bit = 4
    while bit < ncons:
        mine = [added(x, swapped(x, "cons", bit)) for x in mine]
        tail, partner[2] = added(tail, partner[2]), swapped(added(tail, partner[2]), "cons", bit)
        bit *= 2
    other = [swapped(x, "cons", 1) for x in mine]
    late, rims = joined(tail, partner[2], *others)
    fields = (*prepared, coef, depth, mask, late, rims)
    first_part, update, *own = own_half(*fields, ss, sn, sw, se, *mine)
    return other_half(*fields, first_part - update, *own, *other)


def solution(mesh):
    return jax.shard_map(
        body,
        mesh=mesh,
        in_specs=(
            P("cons", None, "ty", "tx"),
            P("cons", None, "ty", "tx"),
            P("ty", "tx"),
            P("ty", "tx"),
            P("ty", "tx"),
        ),
        out_specs=(P("cons", None, "ty", "tx"), P("ty", "tx")),
        check_vma=False,
    )
```

```python
import functools
import math

import jax
import jax.numpy as jnp
from jax import lax
from jax.experimental import pallas as pl
from jax.experimental.pallas import tpu as pltpu
from jax.sharding import PartitionSpec as P

OMEGA_TABLE = (1.0, 1.0351, 0.9582, 1.0379, 0.5181, 0.4816, 0.5164, 0.4454)
AY = 0.5
THETA = 0.05
DRAG = 0.5
BACKGROUND = 0.01
F32 = jnp.float32
LANES = 128
MSG = 16
TINY_DEPTH = 1e-6
PARAMS = pltpu.CompilerParams(vmem_limit_bytes=16 * 1024 * 1024)


def vmem(x):
    return pltpu.with_memory_space_constraint(x, pltpu.VMEM)


def hbm(x):
    return pltpu.with_memory_space_constraint(x, pltpu.HBM)


def recip(x):
    return pl.reciprocal(x, approx=True) if jnp.ndim(x) else 1.0 / x


def metric(rows, total):
    lat = (rows + 0.5) * (120.0 / total * math.pi / 180.0) - math.pi / 3.0
    s = lat * lat
    acc = jnp.full_like(s, 1.0 / math.factorial(16))
    for n in (14, 12, 10, 8, 6, 4, 2, 0):
        acc = ((-1.0) ** (n // 2)) / math.factorial(n) + s * acc
    return 0.5 / acc


def omegas(kdev):
    index = lax.axis_index("cons")
    out = []
    for c in range(kdev):
        w = jnp.float32(OMEGA_TABLE[c])
        for i in range(1, len(OMEGA_TABLE) // kdev):
            w = jnp.where(index == i, jnp.float32(OMEGA_TABLE[i * kdev + c]), w)
        out.append(w)
    return out


def rolled(x, shift, axis):
    return pltpu.roll(x, shift % x.shape[axis], axis)


def face(zr, zi, zr_next, zi_next, r2, coef, w2):
    g = coef * recip(r2 * r2 + w2 * w2)
    a = g * r2
    b = g * w2
    dr = zr - zr_next
    di = zi - zi_next
    return a * dr + b * di, a * di - b * dr


def flux(dr, di, g, a, w2):
    b = g * w2
    return a * dr + b * di, a * di - b * dr


def pack_columns_kernel(e_in, q_in, d_in, m_in, r_in, m2, m1, e, q, d, m, r, turned, behind, sems):
    rows, width = d_in.shape
    copies = []
    for s, side in enumerate((slice(0, LANES), slice(width - LANES, width))):
        for src, dst in ((e_in, e), (q_in, q)):
            copies.append((src.at[:, :, :, side], dst.at[s]))
        for src, dst in ((d_in, d), (m_in, m), (r_in, r)):
            copies.append((src.at[:, side], dst.at[s]))
    copies = [pltpu.make_async_copy(src, dst, sems.at[k]) for k, (src, dst) in enumerate(copies)]
    for copy in copies:
        copy.start()
    for copy in copies:
        copy.wait()
    lane = lax.broadcasted_iota(jnp.int32, (rows, LANES), 1)

    def edges(plane):
        return jnp.where(lane < LANES // 2, plane(0), plane(1))

    elev = [edges(lambda s: e[s, c, p]) for p in range(2) for c in range(2)]
    equil = [edges(lambda s: q[s, c, p]) for p in range(2) for c in range(2)]
    planes = [x - y for x, y in zip(elev, equil)]
    planes += [edges(lambda s: r[s]), edges(lambda s: d[s]), edges(lambda s: m[s]).astype(F32)]
    both = jnp.zeros((rows, LANES), F32)
    for k, plane in enumerate(planes + elev):
        both = jnp.where((lane >= 4 * k) & (lane < 4 * k + 4), rolled(plane, 4 * k + 2, 1), both)
    pad = turned.shape[1]
    turned[...] = jnp.concatenate([both, jnp.zeros((pad - rows, LANES), F32)], axis=0).T
    odd = lax.rem(lax.axis_index("tx"), 2)
    first = (lax.axis_index("ty") * rows).astype(F32)
    lat_row = jnp.minimum(lax.broadcasted_iota(jnp.int32, (8, pad), 1), rows).astype(F32) + first
    ax = metric(lat_row, rows * lax.axis_size("ty"))
    w0, w1 = omegas(2)
    w2 = 2.0 * jnp.where(lax.broadcasted_iota(jnp.int32, (8, pad), 0) < 4, w0, w1)
    up = lambda x: rolled(x, -1, 0)
    zr, zi = turned[0:8, :], turned[8:16, :]
    r8, d8, m8 = (jnp.concatenate([turned[at : at + 4, :]] * 2, axis=0) for at in (16, 20, 24))
    coef = (THETA * ax * ax) * (m8 * up(m8) * (d8 + up(d8)))
    behind[0:8, :], behind[8:16, :] = face(zr, zi, up(zr), up(zi), r8 + up(r8), coef, w2)
    for out, west in ((m1, odd), (m2, 1 - odd)):
        lanes = slice(0, out.shape[1])
        for k in range(4):
            out[k : k + 1, :] = turned[pl.ds(4 * k + 1 + west, 1), lanes]
            out[4 + k : 5 + k, :] = behind[pl.ds(4 * k + 2 * west, 1), lanes]
            out[8 + k : 9 + k, :] = turned[pl.ds(4 * (7 + k) + 1 + west, 1), lanes]
        for k in range(3):
            out[12 + k : 13 + k, :] = turned[pl.ds(4 * (4 + k) + 1 + west, 1), lanes]
        out[MSG - 1 :, :] = jnp.zeros((1, out.shape[1]), F32)


def pack_columns(elevation, equilibrium, depth, land_mask, friction):
    kdev, _, rows, width = elevation.shape
    pad = -(-rows // LANES) * LANES
    cut, plane = pltpu.VMEM((2, kdev, 2, rows, LANES), F32), pltpu.VMEM((2, rows, LANES), F32)
    return pl.pallas_call(
        pack_columns_kernel,
        out_shape=(pltpu.VMEM((MSG, rows), F32), pltpu.VMEM((MSG, pad), F32)),
        in_specs=[pl.BlockSpec(memory_space=pltpu.HBM)] * 5,
        out_specs=[pl.BlockSpec(memory_space=pltpu.VMEM)] * 2,
        scratch_shapes=[
            cut,
            cut,
            plane,
            pltpu.VMEM((2, rows, LANES), jnp.int32),
            plane,
            pltpu.VMEM((LANES, pad), F32),
            pltpu.VMEM((16, pad), F32),
            pltpu.SemaphoreType.DMA((10,)),
        ],
        compiler_params=PARAMS,
        name="pack_columns",
    )(*map(hbm, (elevation, equilibrium, depth, land_mask, friction)))


def pack_kernel(e, q, d, ints, r, after, m, mn, ms):
    del after
    kdev, _, rows, width = e.shape
    m[...] = ints[...].astype(F32)
    ws = omegas(kdev)
    for out, end, near, low in ((ms, slice(0, 8), 0, 0), (mn, slice(rows - 8, rows), 7, 6)):
        out[:, width:] = jnp.zeros((MSG, LANES), F32)
        r8, d8, m8 = r[end, :], d[end, :], m[end, :]
        up = lambda x: rolled(x, -1, 0)
        coef = (THETA * AY * AY) * (m8 * up(m8) * (d8 + up(d8)))
        r2 = r8 + up(r8)
        for c in range(kdev):
            elev = [e[c, p, end, :] for p in range(2)]
            z = [elev[p] - q[c, p, end, :] for p in range(2)]
            v = face(z[0], z[1], up(z[0]), up(z[1]), r2, coef, 2.0 * ws[c])
            for p in range(2):
                out[2 * p + c, :width] = z[p][near, :]
                out[4 + 2 * p + c, :width] = v[p][low, :]
                out[8 + 2 * p + c, :width] = elev[p][near, :]
        for k, plane in enumerate((r8, d8, m8)):
            out[12 + k, :width] = plane[near, :]
        out[MSG - 1, :width] = jnp.zeros((width,), F32)


def pack(elevation, equilibrium, depth, land_mask, friction, after):
    kdev, _, rows, width = elevation.shape
    plane = pltpu.VMEM(depth.shape, F32)
    row = pltpu.VMEM((MSG, width + LANES), F32)
    return pl.pallas_call(
        pack_kernel,
        out_shape=(plane, row, row),
        in_specs=[pl.BlockSpec(memory_space=pltpu.VMEM)] * 6,
        out_specs=[pl.BlockSpec(memory_space=pltpu.VMEM)] * 3,
        compiler_params=PARAMS,
        name="pack",
    )(*map(vmem, (elevation, equilibrium, depth, land_mask, friction, after)))


def tile_rows(ref, at, size, nxt):
    here = ref[at : at + size, :]
    after = ref[nxt : nxt + 8, :]
    return here, jnp.concatenate([here[1:], after[0:1]], axis=0)


def east(x):
    return rolled(x, -1, 1)


def row_metric(at, size, width, rows):
    first = lax.axis_index("ty") * rows
    index = lax.broadcasted_iota(jnp.int32, (size, LANES), 0) + (first + at)
    ax = metric(index.astype(F32), rows * lax.axis_size("ty"))
    return ax, jnp.concatenate([ax] * (width // LANES), axis=1)


def first_kernel(e, q, d, mask, r, after, e1, send, keep, coef, var):
    del after
    kdev, _, rows, width = e.shape
    size = 16
    ws = omegas(kdev)
    last_v = [jnp.zeros((1, width), F32)] * (2 * kdev)
    for at in range(0, rows, size):
        nxt = min(at + size, rows - 8)
        _, ax = row_metric(at, size, width, rows)
        md, mn = tile_rows(mask, at, size, nxt)
        dd, dn = tile_rows(d, at, size, nxt)
        rd, rn = tile_rows(r, at, size, nxt)
        coef_u = (THETA * ax * ax) * (md * east(md) * (dd + east(dd)))
        coef_v = (THETA * AY * AY) * (md * mn * (dd + dn))
        coef[0, at : at + size, :], coef[1, at : at + size, :] = coef_u, coef_v
        r2u = rd + east(rd)
        r2v = rd + rn
        squ, sqv = r2u * r2u, r2v * r2v
        sum_u = sum_v = None
        for c in range(kdev):
            w2 = 2.0 * ws[c]
            wt = THETA * ws[c]
            er, ern = tile_rows(e.at[c, 0], at, size, nxt)
            ei, ein = tile_rows(e.at[c, 1], at, size, nxt)
            qr, qrn = tile_rows(q.at[c, 0], at, size, nxt)
            qi, qin = tile_rows(q.at[c, 1], at, size, nxt)
            zr, zi = er - qr, ei - qi
            gu = coef_u * recip(squ + w2 * w2)
            gv = coef_v * recip(sqv + w2 * w2)
            ur, ui = flux(zr - east(zr), zi - east(zi), gu, gu * r2u, w2)
            vr, vi = flux(zr - (ern - qrn), zi - (ein - qin), gv, gv * r2v, w2)
            uwr, uwi = rolled(ur, 1, 1), rolled(ui, 1, 1)
            vsr = jnp.concatenate([last_v[2 * c], vr[:-1]], axis=0)
            vsi = jnp.concatenate([last_v[2 * c + 1], vi[:-1]], axis=0)
            last_v[2 * c], last_v[2 * c + 1] = vr[-1:], vi[-1:]
            e1[c, 0, at : at + size, :] = md * (er + wt * ei - (ur - uwr) - (vr - vsr))
            e1[c, 1, at : at + size, :] = md * (ei - wt * er - (ui - uwi) - (vi - vsi))
            su = (ur + uwr) * (ur + uwr) + (ui + uwi) * (ui + uwi)
            sv = (vr + vsr) * (vr + vsr) + (vi + vsi) * (vi + vsi)
            sum_u = su if sum_u is None else sum_u + su
            sum_v = sv if sum_v is None else sum_v + sv
        inv = recip(dd)
        ia = recip(THETA * ax)
        total = (0.125 * ia * ia) * sum_u + (0.125 / (THETA * AY) ** 2) * sum_v
        var[at : at + size, :] = total * (inv * inv)
    half = rows // 2
    core = lax.rem(lax.axis_index("cons"), 2)
    send[:half, :] = var[pl.ds(pl.multiple_of((1 - core) * half, 8), half), :]
    keep[:half, :] = var[pl.ds(pl.multiple_of(core * half, 8), half), :]
    send[half:, :] = keep[half - 8 : half, :]
    keep[half:, :] = send[half - 8 : half, :]


def first_sweep(e, q, d, m, r, after):
    kdev, _, rows, width = e.shape
    half = pltpu.VMEM((rows // 2 + 8, width), F32)
    return pl.pallas_call(
        first_kernel,
        out_shape=(pltpu.VMEM(e.shape, F32), half, half, pltpu.VMEM((2, *d.shape), F32)),
        in_specs=[pl.BlockSpec(memory_space=pltpu.VMEM)] * 6,
        out_specs=[pl.BlockSpec(memory_space=pltpu.VMEM)] * 4,
        scratch_shapes=[pltpu.VMEM(d.shape, F32)],
        compiler_params=PARAMS,
        cost_estimate=pl.CostEstimate(flops=80 * e.size, bytes_accessed=160 * e.size, transcendentals=0),
        name="first_sweep",
    )(*map(vmem, (e, q, d, m, r, after)))


def add_kernel(a, b, *refs):
    refs[-1][...] = a[...] + b[...]


def added(a, b, *after):
    return pl.pallas_call(
        add_kernel,
        out_shape=pltpu.VMEM(a.shape, F32),
        in_specs=[pl.BlockSpec(memory_space=pltpu.VMEM)] * (2 + len(after)),
        out_specs=pl.BlockSpec(memory_space=pltpu.VMEM),
        compiler_params=PARAMS,
        name="added",
    )(vmem(a), vmem(b), *map(vmem, after))


def cut_kernel(a, b, after, *outs):
    del after
    at = 0
    for out in outs:
        here = slice(at, at + out.shape[0])
        out[...] = a[here, :] + b[here, :]
        at += out.shape[0]


def cut_sum(a, b, after):
    rows, width = a.shape
    large = pltpu.VMEM(((rows - 16) // 2, width), F32)
    return pl.pallas_call(
        cut_kernel,
        out_shape=(large, large, pltpu.VMEM((16, width), F32)),
        in_specs=[pl.BlockSpec(memory_space=pltpu.VMEM)] * 3,
        out_specs=[pl.BlockSpec(memory_space=pltpu.VMEM)] * 3,
        compiler_params=PARAMS,
        name="cut_sum",
    )(vmem(a), vmem(b), vmem(after))


def tree_sum(terms):
    while len(terms) > 1:
        terms = [a + b for a, b in zip(terms[::2], terms[1::2])]
    return terms[0]


def early_kernel(after, *refs):
    del after
    pieces, partner, outs = refs[:2], refs[2:4], refs[4:]
    thin = outs[0].shape[0]
    for k, out in enumerate(outs):
        part, at = divmod(k * thin, pieces[0].shape[0])
        out[...] = pieces[part][at : at + thin, :] + partner[part][at : at + thin, :]


def early_sums(pieces, partner, after):
    rows, width = pieces[0].shape
    count = 2 * rows // 16
    return pl.pallas_call(
        early_kernel,
        out_shape=(pltpu.VMEM((16, width), F32),) * count,
        in_specs=[pl.BlockSpec(memory_space=pltpu.VMEM)] * 5,
        out_specs=[pl.BlockSpec(memory_space=pltpu.VMEM)] * count,
        compiler_params=PARAMS,
        name="early_sums",
    )(*map(vmem, (after, *pieces, *partner)))


def join_kernel(tail, partner, both, after, *refs):
    del after
    *others, late, rims = refs
    late[...] = tail[:16, :] + partner[:16, :]
    terms = [x[...] for x in others]
    rims[...] = tree_sum([both[...], partner[16:, :] + terms[0], *[a + b for a, b in zip(terms[1::2], terms[2::2])]])


def joined(*args):
    width = args[0].shape[1]
    return pl.pallas_call(
        join_kernel,
        out_shape=(pltpu.VMEM((16, width), F32), pltpu.VMEM((8, width), F32)),
        in_specs=[pl.BlockSpec(memory_space=pltpu.VMEM)] * len(args),
        out_specs=[pl.BlockSpec(memory_space=pltpu.VMEM)] * 2,
        compiler_params=PARAMS,
        name="joined",
    )(*map(vmem, args))


def roles(a, b):
    even = lax.rem(lax.axis_index("tx"), 2) == 0
    return jnp.where(even, b, a), jnp.where(even, a, b)


def padded(x, pad):
    return jnp.concatenate([x, jnp.zeros((x.shape[0], pad - x.shape[1]), F32)], axis=1)


def merge_kernel(rows, f2, f1, mn, ms, send, mn_out, ms_out, my_out, send_out):
    width = mn.shape[1] - LANES
    fw, fe = roles(f1[...], padded(f2[...], f1.shape[1]))
    lane = lax.broadcasted_iota(jnp.int32, (MSG, LANES), 1)
    last = LANES - 1

    def ends(at):
        east_, west = fe[:, at // LANES * LANES :][:, :LANES], fw[:, at // LANES * LANES :][:, :LANES]
        east_, west = rolled(east_, -(at % LANES), 1), rolled(west, last - at % LANES, 1)
        return jnp.where(lane == 0, east_, jnp.where(lane == last, west, 0.0))

    mn_out[:, :width] = mn[:, :width]
    ms_out[:, :width] = ms[:, :width]
    mn_out[:, width:] = ends(rows - 1)
    ms_out[:, width:] = ends(0)
    low = lax.axis_index("ty") == 0
    my_out[...] = jnp.where(low, mn_out[...], ms_out[...])
    send_out[...] = send[...]


def merge(rows, f1, f2, mn, ms, send):
    out = pltpu.VMEM(mn.shape, F32)
    return pl.pallas_call(
        functools.partial(merge_kernel, rows),
        out_shape=(out, out, out, pltpu.VMEM(send.shape, F32)),
        in_specs=[pl.BlockSpec(memory_space=pltpu.VMEM)] * 5,
        out_specs=[pl.BlockSpec(memory_space=pltpu.VMEM)] * 4,
        compiler_params=PARAMS,
        name="merge",
    )(*map(vmem, (f2, f1, mn, ms, send)))


def strip_omega(shape, ws):
    odd = lax.rem(lax.broadcasted_iota(jnp.int32, shape, 0), 2)
    return jnp.where(odd == 0, ws[0], ws[1])


def strip_sweep(low, high, ws, g_across, g_along):
    none = jnp.zeros((2, low.shape[1]), F32)

    def field(at):
        return jnp.concatenate([none, low[at : at + 2], high[at : at + 2], none], axis=0)

    def single(at):
        a, b = low[at : at + 1], high[at : at + 1]
        return jnp.concatenate([none, a, a, b, b, none], axis=0)

    def given(at):
        return jnp.concatenate([low[at : at + 2], none, high[at : at + 2], none], axis=0)

    zr, zi, er, ei = field(0), field(2), field(8), field(10)
    r, d, m = single(12), single(13), single(14)
    w = strip_omega(zr.shape, ws)
    w2 = 2.0 * w
    wt = THETA * w
    up = lambda x: rolled(x, -2, 0)
    nx = lambda x: rolled(x, -1, 1)
    coef_a = (THETA * g_across * g_across) * (m * up(m) * (d + up(d)))
    coef_l = (THETA * g_along * g_along) * (m * nx(m) * (d + nx(d)))
    ar, ai = face(zr, zi, up(zr), up(zi), r + up(r), coef_a, w2)
    middle = lax.broadcasted_iota(jnp.int32, zr.shape, 0) // 2 == 1
    ar, ai = jnp.where(middle, ar, given(4)), jnp.where(middle, ai, given(6))
    lr, li = face(zr, zi, nx(zr), nx(zi), r + nx(r), coef_l, w2)
    abr, abi = rolled(ar, 2, 0), rolled(ai, 2, 0)
    lbr, lbi = rolled(lr, 1, 1), rolled(li, 1, 1)
    e1r = m * (er + wt * ei - (ar - abr) - (lr - lbr))
    e1i = m * (ei - wt * er - (ai - abi) - (li - lbi))
    sa = (ar + abr) * (ar + abr) + (ai + abi) * (ai + abi)
    sl = (lr + lbr) * (lr + lbr) + (li + lbi) * (li + lbi)
    inv = recip(jnp.maximum(d, TINY_DEPTH))
    ia = recip(THETA * g_across)
    il = recip(THETA * g_along)
    var = 0.125 * (ia * ia * sa + il * il * sl) * (inv * inv)
    var = var + rolled(var, -1, 0)
    z1r = e1r - (er - zr)
    z1i = e1i - (ei - zi)
    return (z1r, z1i, d, coef_a, e1r, e1i), var


def strips(rows, m2, m1, f2, f1, mn, ms, fn_ref, fs_ref):
    kdev = 2
    width = mn.shape[1] - LANES
    pad = m1.shape[1]
    ws = omegas(kdev)
    ty, count = lax.axis_index("ty"), lax.axis_size("ty")
    first = (ty * rows).astype(F32)
    total = rows * count
    fn = jnp.where(ty < count - 1, fn_ref[...], 0.0)
    fs = jnp.where(ty > 0, fs_ref[...], 0.0)

    ay = AY
    line = lax.broadcasted_iota(jnp.int32, (8, LANES), 0) // 2
    out = []
    for low, high, start in ((fs, ms[...], -2), (mn[...], fn, rows - 2)):
        ax = metric((line + start).astype(F32) + first, total)
        ax = jnp.concatenate([ax] * (low.shape[1] // LANES), axis=1)
        out.append(strip_sweep(low, high, ws, ay, ax))

    mw, me = roles(m1[...], padded(m2[...], pad))
    fw, fe = roles(f1[...], padded(f2[...], pad))
    hi = rows - (pad - LANES)
    last = LANES - 1
    lane = lax.broadcasted_iota(jnp.int32, (MSG, LANES), 1)

    def ended(msg, block, at):
        end = msg[:, pad - LANES :]
        end = jnp.where(lane == hi, rolled(fn[:, block : block + LANES], hi - at, 1), end)
        end = jnp.where(lane == last, rolled(fs[:, block : block + LANES], last - at, 1), end)
        return jnp.concatenate([msg[:, : pad - LANES], end], axis=1)

    low_w, high_w = ended(fw, width, last), ended(mw, 0, 0)
    low_e, high_e = ended(me, width - LANES, last), ended(fe, width, 0)
    row = lax.broadcasted_iota(jnp.int32, (8, pad), 1).astype(F32) + first
    ax = metric(jnp.minimum(row, first + rows), total)
    for low, high in ((low_w, high_w), (low_e, high_e)):
        out.append(strip_sweep(low, high, ws, ax, ay))
    return out


def rim_kernel(rows, after, *refs):
    del after
    *refs, row_sums, col_sums = refs
    width, pad = row_sums.shape[1], refs[1].shape[1]
    for k, (_, var) in enumerate(strips(rows, *refs)):
        for p in range(2):
            if k < 2:
                row_sums[2 * k + p, :] = var[2 + 2 * p, :width]
            else:
                col_sums[k - 2, p * pad : (p + 1) * pad] = var[2 + 2 * p, :]
    col_sums[2:, :] = jnp.zeros((2, width), F32)


def strips_kernel(rows, *refs):
    for out, (held, _) in zip(refs[-4:], strips(rows, *refs[:-4])):
        for k, x in enumerate(held):
            out[8 * k : 8 * k + 8, :] = x


def rim(rows, late, *messages):
    width = late.shape[1]
    return pl.pallas_call(
        functools.partial(rim_kernel, rows),
        out_shape=(pltpu.VMEM((4, width), F32),) * 2,
        in_specs=[pl.BlockSpec(memory_space=pltpu.VMEM)] * 9,
        out_specs=[pl.BlockSpec(memory_space=pltpu.VMEM)] * 2,
        compiler_params=PARAMS,
        name="rim",
    )(*map(vmem, (late, *messages)))


def stack_kernel(a, b, out):
    out[: a.shape[0], :] = a[...]
    out[a.shape[0] :, :] = b[...]


def stacked(a, b):
    return pl.pallas_call(
        stack_kernel,
        out_shape=pltpu.VMEM((a.shape[0] + b.shape[0], a.shape[1]), F32),
        in_specs=[pl.BlockSpec(memory_space=pltpu.VMEM)] * 2,
        out_specs=pl.BlockSpec(memory_space=pltpu.VMEM),
        compiler_params=PARAMS,
        name="stacked",
    )(vmem(a), vmem(b))


def held_strips(rows, *messages):
    row = pltpu.VMEM((48, messages[4].shape[1]), F32)
    col = pltpu.VMEM((48, messages[1].shape[1]), F32)
    return pl.pallas_call(
        functools.partial(strips_kernel, rows),
        out_shape=(row, row, col, col),
        in_specs=[pl.BlockSpec(memory_space=pltpu.VMEM)] * 8,
        out_specs=[pl.BlockSpec(memory_space=pltpu.VMEM)] * 4,
        compiler_params=PARAMS,
        name="held_strips",
    )(*map(vmem, messages))


def prepare_kernel(e1_in, q, m, ss, sn, sw, se, du, dv, base, e1, cols):
    kdev, _, rows, width = e1_in.shape
    size = 16
    ws = omegas(kdev)
    e1[...] = e1_in[...]
    for p in range(2):
        cols[2 * p : 2 * p + 2, :] = sw[8 * (4 + p) + 4 : 8 * (4 + p) + 6, :]
        cols[4 + 2 * p : 6 + 2 * p, :] = se[8 * (4 + p) + 2 : 8 * (4 + p) + 4, :]
    turned = cols[...].T
    lane = lax.broadcasted_iota(jnp.int32, (rows, LANES), 1)
    left, right = slice(0, LANES), slice(width - LANES, width)
    last = LANES - 1
    for p in range(2):
        for c in range(kdev):
            e1[c, p, 0:1, :] = ss[8 * (4 + p) + 4 + c : 8 * (4 + p) + 5 + c, :width]
            e1[c, p, rows - 1 : rows, :] = sn[8 * (4 + p) + 2 + c : 8 * (4 + p) + 3 + c, :width]
            k = 2 * p + c
            e1[c, p, :, left] = jnp.where(lane == 0, rolled(turned[:rows], -k, 1), e1[c, p, :, left])
            k = 4 + 2 * p + c
            e1[c, p, :, right] = jnp.where(lane == last, rolled(turned[:rows], last - k, 1), e1[c, p, :, right])
    for at in range(0, rows, size):
        nxt = min(at + size, rows - 8)
        here = slice(at, at + size)
        md = m[here, :]
        for c in range(kdev):
            wt = THETA * ws[c]
            er, ern = tile_rows(e1.at[c, 0], at, size, nxt)
            ei, ein = tile_rows(e1.at[c, 1], at, size, nxt)
            qr, qrn = tile_rows(q.at[c, 0], at, size, nxt)
            qi, qin = tile_rows(q.at[c, 1], at, size, nxt)
            zr, zi = er - qr, ei - qi
            du[c, 0, here, :] = zr - east(zr)
            du[c, 1, here, :] = zi - east(zi)
            dv[c, 0, here, :] = zr - (ern - qrn)
            dv[c, 1, here, :] = zi - (ein - qin)
            base[c, 0, here, :] = md * (er + wt * ei)
            base[c, 1, here, :] = md * (ei - wt * er)


def prepare(e1, q, m, ss, sn, sw, se):
    plane = pltpu.VMEM(e1.shape, F32)
    return pl.pallas_call(
        prepare_kernel,
        out_shape=(plane, plane, plane),
        in_specs=[pl.BlockSpec(memory_space=pltpu.VMEM)] * 7,
        out_specs=[pl.BlockSpec(memory_space=pltpu.VMEM)] * 3,
        scratch_shapes=[pltpu.VMEM(e1.shape, F32), pltpu.VMEM((LANES, sw.shape[1]), F32)],
        compiler_params=PARAMS,
        cost_estimate=pl.CostEstimate(flops=40 * e1.size, bytes_accessed=160 * e1.size, transcendentals=0),
        name="prepare",
    )(*map(vmem, (e1, q, m, ss, sn, sw, se)))


def rate(var, d):
    s = var + BACKGROUND
    return (DRAG * (s * lax.rsqrt(s))) * recip(d)


def sweep_tile(row, size, r, r_north, du, dv, base, coef, m, turned, ws, last_v, top):
    kdev, width = du.shape[0], du.shape[3]
    here = pl.ds(row, size)
    edges = turned[here, :]
    md = m[here, :]
    coef_u, coef_v = coef[0, here, :], coef[1, here, :]
    r2u = r + east(r)
    r2v = r + r_north
    squ, sqv = r2u * r2u, r2v * r2v
    lane = lax.broadcasted_iota(jnp.int32, (size, LANES), 1)
    last = LANES - 1

    def with_east(u, k):
        block = jnp.where(lane == last, rolled(edges, last - k, 1), u[:, width - LANES :])
        return jnp.concatenate([u[:, : width - LANES], block], axis=1)

    def from_west(u, k):
        u = rolled(u, 1, 1)
        block = jnp.where(lane == 0, rolled(edges, -k, 1), u[:, :LANES])
        return jnp.concatenate([block, u[:, LANES:]], axis=1)

    planes, out_v = {}, {}
    for c in range(kdev):
        w2 = 2.0 * ws[c]
        gu = coef_u * recip(squ + w2 * w2)
        gv = coef_v * recip(sqv + w2 * w2)
        u = flux(du[c, 0, here, :], du[c, 1, here, :], gu, gu * r2u, w2)
        v = flux(dv[c, 0, here, :], dv[c, 1, here, :], gv, gv * r2v, w2)
        for p in range(2):
            up, vp = with_east(u[p], 4 + 2 * p + c), v[p]
            if top is not None:
                vp = jnp.concatenate([vp[:-1], top(c, p, vp[-1:])], axis=0)
            uw = from_west(up, 2 * p + c)
            vs = jnp.concatenate([last_v[c, p], vp[:-1]], axis=0)
            out_v[c, p] = vp[-1:]
            planes[c, p] = base[c, p, here, :], md * ((up - uw) + (vp - vs))
    return planes, out_v


def pairs(kdev):
    return [(c, p) for c in range(kdev) for p in range(2)]


def half_rate(var, rims, turned, d, row, low, half):
    here = pl.ds(row, half)
    edges = turned[here, :]
    width = var.shape[1]
    index = lax.broadcasted_iota(jnp.int32, (8, width), 0)
    first = jnp.where(low & (index == 0), rims[1:2], var[:8])
    final = jnp.where(jnp.logical_not(low) & (index == 7), rims[2:3], var[half - 8 :])
    var = jnp.concatenate([first, var[8 : half - 8], final], axis=0)
    lane = lax.broadcasted_iota(jnp.int32, (half, LANES), 1)
    left = jnp.where(lane == 0, rolled(edges, -8, 1), var[:, :LANES])
    right = jnp.where(lane == LANES - 1, rolled(edges, LANES - 1 - 9, 1), var[:, width - LANES :])
    return rate(jnp.concatenate([left, var[:, LANES : width - LANES], right], axis=1), d[here, :])


def own_kernel(du, dv, base, coef, d, m, late, rims_ref, ss, sn, sw, se, *refs):
    *mine, first_part, update, fric, vs_out, vn_out, turned, cols = refs
    kdev, _, half, width = update.shape
    pad = sw.shape[1]
    ws = omegas(kdev)
    core = lax.rem(lax.axis_index("cons"), 2)
    low = core == 0
    rims = rims_ref[...]

    def edge(strip, var_a, var_b):
        zr, zi, dep, ca = (strip[8 * k : 8 * k + 8, :] for k in range(4))
        var = jnp.concatenate([var_a, var_a, var_a, var_a, var_b, var_b, var_b, var_b], axis=0)
        f = rate(var, jnp.maximum(dep, TINY_DEPTH))
        up = lambda x: rolled(x, -2, 0)
        w2 = 2.0 * strip_omega(zr.shape, ws)
        return face(zr, zi, up(zr), up(zi), f + up(f), ca, w2)

    none = jnp.zeros((1, LANES), F32)
    wide = lambda x: jnp.concatenate([x, none], axis=1)
    south = edge(ss, wide(rims[0:1]), wide(rims[1:2]))
    north = edge(sn, wide(rims[2:3]), wide(rims[3:4]))
    west = edge(sw, rims[4:5, :pad], rims[4:5, pad : 2 * pad])
    east_ = edge(se, rims[5:6, :pad], rims[5:6, pad : 2 * pad])
    for p in range(2):
        cols[2 * p : 2 * p + 2, :] = west[p][2:4]
        cols[4 + 2 * p : 6 + 2 * p, :] = east_[p][2:4]
        for c in range(kdev):
            vs_out[2 * c + p : 2 * c + p + 1, :] = south[p][2 + c : 3 + c, :width]
            vn_out[2 * c + p : 2 * c + p + 1, :] = north[p][2 + c : 3 + c, :width]
    cols[8:9, :] = rims[4:5, pad : 2 * pad]
    cols[9:10, :] = rims[5:6, :pad]
    turned[...] = cols[...].T

    first = pl.multiple_of(core * half, 8)
    var = jnp.concatenate([x[...] for x in mine] + [late[:8, :]], axis=0)
    fric[...] = half_rate(var, rims, turned, d, first, low, half)
    size = 24
    last_v = {(c, p): jnp.where(low, vs_out[2 * c + p : 2 * c + p + 1, :], 0.0) for c, p in pairs(kdev)}

    def top(c, p, own):
        return jnp.where(low, 0.0, vn_out[2 * c + p : 2 * c + p + 1, :])

    for at in range(0, half, size):
        r, rn = tile_rows(fric, at, size, min(at + size, half - 8))
        planes, last_v = sweep_tile(
            pl.multiple_of(first + at, 8), size, r, rn, du, dv, base, coef, m, turned, ws, last_v,
            top if at + size == half else None,
        )
        for c, p in pairs(kdev):
            first_part[c, p, at : at + size, :], update[c, p, at : at + size, :] = planes[c, p]


def own_half(*args):
    kdev, _, rows, width = args[0].shape
    pad = args[10].shape[1]
    line = pltpu.VMEM((8, width), F32)
    return pl.pallas_call(
        own_kernel,
        out_shape=(
            pltpu.VMEM((kdev, 2, rows // 2, width), F32),
            pltpu.VMEM((kdev, 2, rows // 2, width), F32),
            pltpu.VMEM((rows // 2, width), F32),
            line,
            line,
            pltpu.VMEM((pad, LANES), F32),
        ),
        in_specs=[pl.BlockSpec(memory_space=pltpu.VMEM)] * len(args),
        out_specs=[pl.BlockSpec(memory_space=pltpu.VMEM)] * 6,
        scratch_shapes=[pltpu.VMEM((LANES, pad), F32)],
        compiler_params=PARAMS,
        name="own_half",
    )(*map(vmem, args))


def other_kernel(du, dv, base, coef, d, m, late, rims, eta_own, fric_own, vs, vn, turned, *refs):
    *other, eta_out, fric_out, eta, fric, fixed, sems = refs
    kdev, _, half, width = eta.shape
    ws = omegas(kdev)
    core = lax.rem(lax.axis_index("cons"), 2)
    own_low = core == 0
    own, first = pl.multiple_of(core * half, 8), pl.multiple_of((1 - core) * half, 8)
    copies = []

    def put(src, dst):
        copy = pltpu.make_async_copy(src, dst, sems.at[len(copies)])
        copy.start()
        copies.append(copy)

    skip = pl.multiple_of(core * 8, 8)
    put(
        eta_own.at[:, :, pl.ds(skip, half - 8), :],
        eta_out.at[:, :, pl.ds(pl.multiple_of(own + skip, 8), half - 8), :],
    )
    put(fric_own, fric_out.at[pl.ds(own, half), :])
    fric[pl.ds(own, half), :] = fric_own[...]
    fric[pl.ds(first, half), :] = half_rate(
        jnp.concatenate([x[...] for x in other] + [late[8:, :]], axis=0),
        rims[...], turned, d, first, jnp.logical_not(own_low), half,
    )
    put(fric.at[pl.ds(first, half), :], fric_out.at[pl.ds(first, half), :])

    r, rn = tile_rows(fric, half - 8, 8, half)
    r2 = r + rn
    between = {}
    for c in range(kdev):
        w2 = 2.0 * ws[c]
        g = coef[1, half - 8 : half, :] * recip(r2 * r2 + w2 * w2)
        v = flux(dv[c, 0, half - 8 : half, :], dv[c, 1, half - 8 : half, :], g, g * r2, w2)
        for p in range(2):
            between[c, p] = v[p][7:8]
    index = lax.broadcasted_iota(jnp.int32, (8, width), 0)
    at_face = index == jnp.where(own_low, 7, 0)
    sign = jnp.where(own_low, -1.0, 1.0)
    local = pl.ds(pl.multiple_of((1 - core) * (half - 8), 8), 8)
    border = pl.ds(pl.multiple_of(half - 8 + 8 * core, 8), 8)
    md = m[border, :]
    for c, p in pairs(kdev):
        fixed[c, p] = eta_own[c, p, local, :] + jnp.where(at_face, sign * (md * between[c, p]), 0.0)
    put(fixed, eta_out.at[:, :, border, :])

    size = 24
    rows = 2 * half
    last_v = {(c, p): jnp.where(own_low, between[c, p], vs[2 * c + p : 2 * c + p + 1, :]) for c, p in pairs(kdev)}

    def top(c, p, own_v):
        return jnp.where(own_low, vn[2 * c + p : 2 * c + p + 1, :], own_v)

    for at in range(0, half, size):
        row = pl.multiple_of(first + at, 8)
        r = fric[pl.ds(row, size), :]
        after = fric[pl.ds(pl.multiple_of(jnp.minimum(row + size, rows - 8), 8), 8), :]
        rn = jnp.concatenate([r[1:], after[0:1]], axis=0)
        planes, last_v = sweep_tile(
            row, size, r, rn, du, dv, base, coef, m, turned, ws, last_v, top if at + size == half else None
        )
        for c, p in pairs(kdev):
            eta[c, p, at : at + size, :] = planes[c, p][0] - planes[c, p][1]
        put(eta.at[:, :, at : at + size, :], eta_out.at[:, :, pl.ds(row, size), :])
    for copy in copies:
        copy.wait()


def other_half(*args):
    du, d = args[0], args[4]
    kdev, _, rows, width = du.shape
    return pl.pallas_call(
        other_kernel,
        out_shape=(jax.ShapeDtypeStruct(du.shape, F32), jax.ShapeDtypeStruct(d.shape, F32)),
        in_specs=[pl.BlockSpec(memory_space=pltpu.VMEM)] * len(args),
        out_specs=[pl.BlockSpec(memory_space=pltpu.HBM)] * 2,
        scratch_shapes=[
            pltpu.VMEM((kdev, 2, rows // 2, width), F32),
            pltpu.VMEM(d.shape, F32),
            pltpu.VMEM((kdev, 2, 8, width), F32),
            pltpu.SemaphoreType.DMA((4 + rows // 2 // 24,)),
        ],
        compiler_params=PARAMS,
        name="other_half",
    )(*map(vmem, args))


def swapped(x, axis, bit):
    return lax.ppermute(x, axis, [(i, i ^ bit) for i in range(lax.axis_size(axis))])


def body(elevation, equilibrium, depth, land_mask, friction_prev):
    rows = depth.shape[0]
    ntx, nty, ncons = (lax.axis_size(a) for a in ("tx", "ty", "cons"))
    fields = (elevation, equilibrium, depth, land_mask, friction_prev)
    m2, m1 = pack_columns(*fields)
    elev, equil, depth, mask, fric = elevation, equilibrium, depth, land_mask, friction_prev
    mask, mn, ms = pack(*fields, m1)
    f2 = lax.ppermute(m2, "tx", [(i, (i - 1 if i % 2 == 0 else i + 1) % ntx) for i in range(ntx)])
    f1 = swapped(m1, "tx", 1)
    e1, send, keep, coef = first_sweep(elev, equil, depth, mask, fric, m1)
    mn, ms, my, send = merge(rows, f1, f2, mn, ms, send)
    recv = swapped(send, "cons", 1)
    if nty == 2:
        fn = fs = swapped(my, "ty", 1)
    else:
        fn = lax.ppermute(ms, "ty", [(i, i - 1) for i in range(1, nty)])
        fs = lax.ppermute(mn, "ty", [(i, i + 1) for i in range(nty - 1)])
    first, second, late = cut_sum(recv, keep, my)
    messages = (m2, m1, f2, f1, mn, ms, fn, fs)
    rims = jnp.concatenate(rim(rows, late, *messages), axis=0)
    tail = stacked(late, rims)
    ss, sn, sw, se = held_strips(rows, *messages)
    prepared = prepare(e1, equil, mask, ss, sn, sw, se)
    partner = [swapped(x, "cons", 2) for x in (first, second, tail)]
    others = [swapped(rims, "cons", k) for k in range(1, ncons) if k != 2]
    both = added(rims, others[0], prepared[2])
    mine = early_sums((first, second), partner[:2], both)
    bit = 4
    while bit < ncons:
        mine = [added(x, swapped(x, "cons", bit)) for x in mine]
        tail, partner[2] = added(tail, partner[2]), swapped(added(tail, partner[2]), "cons", bit)
        bit *= 2
    other = [swapped(x, "cons", 1) for x in mine]
    late, rims = joined(tail, partner[2], both, other[0], *others[1:])
    fields = (*prepared, coef, depth, mask, late, rims)
    first_part, update, *own = own_half(*fields, ss, sn, sw, se, *mine)
    return other_half(*fields, first_part - update, *own, *other)


def solution(mesh):
    return jax.shard_map(
        body,
        mesh=mesh,
        in_specs=(
            P("cons", None, "ty", "tx"),
            P("cons", None, "ty", "tx"),
            P("ty", "tx"),
            P("ty", "tx"),
            P("ty", "tx"),
        ),
        out_specs=(P("cons", None, "ty", "tx"), P("ty", "tx")),
        check_vma=False,
    )
```

```python
import functools
import math

import jax
import jax.numpy as jnp
from jax import lax
from jax.experimental import pallas as pl
from jax.experimental.pallas import tpu as pltpu
from jax.sharding import PartitionSpec as P

OMEGA_TABLE = (1.0, 1.0351, 0.9582, 1.0379, 0.5181, 0.4816, 0.5164, 0.4454)
AY = 0.5
THETA = 0.05
DRAG = 0.5
BACKGROUND = 0.01
F32 = jnp.float32
LANES = 128
MSG = 16
TINY_DEPTH = 1e-6
PARAMS = pltpu.CompilerParams(vmem_limit_bytes=16 * 1024 * 1024)


def vmem(x):
    return pltpu.with_memory_space_constraint(x, pltpu.VMEM)


def hbm(x):
    return pltpu.with_memory_space_constraint(x, pltpu.HBM)


def recip(x):
    return pl.reciprocal(x, approx=True) if jnp.ndim(x) else 1.0 / x


def metric(rows, total):
    lat = (rows + 0.5) * (120.0 / total * math.pi / 180.0) - math.pi / 3.0
    s = lat * lat
    acc = jnp.full_like(s, 1.0 / math.factorial(16))
    for n in (14, 12, 10, 8, 6, 4, 2, 0):
        acc = ((-1.0) ** (n // 2)) / math.factorial(n) + s * acc
    return 0.5 / acc


def omegas(kdev):
    index = lax.axis_index("cons")
    out = []
    for c in range(kdev):
        w = jnp.float32(OMEGA_TABLE[c])
        for i in range(1, len(OMEGA_TABLE) // kdev):
            w = jnp.where(index == i, jnp.float32(OMEGA_TABLE[i * kdev + c]), w)
        out.append(w)
    return out


def rolled(x, shift, axis):
    return pltpu.roll(x, shift % x.shape[axis], axis)


def face(zr, zi, zr_next, zi_next, r2, coef, w2):
    g = coef * recip(r2 * r2 + w2 * w2)
    a = g * r2
    b = g * w2
    dr = zr - zr_next
    di = zi - zi_next
    return a * dr + b * di, a * di - b * dr


def flux(dr, di, g, a, w2):
    b = g * w2
    return a * dr + b * di, a * di - b * dr


def pack_columns_kernel(e_in, q_in, d_in, m_in, r_in, m2, m1, e, q, d, m, r, turned, behind, sems):
    rows, width = d_in.shape
    copies = []
    for s, side in enumerate((slice(0, LANES), slice(width - LANES, width))):
        for src, dst in ((e_in, e), (q_in, q)):
            copies.append((src.at[:, :, :, side], dst.at[s]))
        for src, dst in ((d_in, d), (m_in, m), (r_in, r)):
            copies.append((src.at[:, side], dst.at[s]))
    copies = [pltpu.make_async_copy(src, dst, sems.at[k]) for k, (src, dst) in enumerate(copies)]
    for copy in copies:
        copy.start()
    for copy in copies:
        copy.wait()
    lane = lax.broadcasted_iota(jnp.int32, (rows, LANES), 1)

    def edges(plane):
        return jnp.where(lane < LANES // 2, plane(0), plane(1))

    elev = [edges(lambda s: e[s, c, p]) for p in range(2) for c in range(2)]
    equil = [edges(lambda s: q[s, c, p]) for p in range(2) for c in range(2)]
    planes = [x - y for x, y in zip(elev, equil)]
    planes += [edges(lambda s: r[s]), edges(lambda s: d[s]), edges(lambda s: m[s]).astype(F32)]
    both = jnp.zeros((rows, LANES), F32)
    for k, plane in enumerate(planes + elev):
        both = jnp.where((lane >= 4 * k) & (lane < 4 * k + 4), rolled(plane, 4 * k + 2, 1), both)
    pad = turned.shape[1]
    turned[...] = jnp.concatenate([both, jnp.zeros((pad - rows, LANES), F32)], axis=0).T
    odd = lax.rem(lax.axis_index("tx"), 2)
    first = (lax.axis_index("ty") * rows).astype(F32)
    lat_row = jnp.minimum(lax.broadcasted_iota(jnp.int32, (8, pad), 1), rows).astype(F32) + first
    ax = metric(lat_row, rows * lax.axis_size("ty"))
    w0, w1 = omegas(2)
    w2 = 2.0 * jnp.where(lax.broadcasted_iota(jnp.int32, (8, pad), 0) < 4, w0, w1)
    up = lambda x: rolled(x, -1, 0)
    zr, zi = turned[0:8, :], turned[8:16, :]
    r8, d8, m8 = (jnp.concatenate([turned[at : at + 4, :]] * 2, axis=0) for at in (16, 20, 24))
    coef = (THETA * ax * ax) * (m8 * up(m8) * (d8 + up(d8)))
    behind[0:8, :], behind[8:16, :] = face(zr, zi, up(zr), up(zi), r8 + up(r8), coef, w2)
    for out, west in ((m1, odd), (m2, 1 - odd)):
        lanes = slice(0, out.shape[1])
        for k in range(4):
            out[k : k + 1, :] = turned[pl.ds(4 * k + 1 + west, 1), lanes]
            out[4 + k : 5 + k, :] = behind[pl.ds(4 * k + 2 * west, 1), lanes]
            out[8 + k : 9 + k, :] = turned[pl.ds(4 * (7 + k) + 1 + west, 1), lanes]
        for k in range(3):
            out[12 + k : 13 + k, :] = turned[pl.ds(4 * (4 + k) + 1 + west, 1), lanes]
        out[MSG - 1 :, :] = jnp.zeros((1, out.shape[1]), F32)


def pack_columns(elevation, equilibrium, depth, land_mask, friction):
    kdev, _, rows, width = elevation.shape
    pad = -(-rows // LANES) * LANES
    cut, plane = pltpu.VMEM((2, kdev, 2, rows, LANES), F32), pltpu.VMEM((2, rows, LANES), F32)
    return pl.pallas_call(
        pack_columns_kernel,
        out_shape=(pltpu.VMEM((MSG, rows), F32), pltpu.VMEM((MSG, pad), F32)),
        in_specs=[pl.BlockSpec(memory_space=pltpu.HBM)] * 5,
        out_specs=[pl.BlockSpec(memory_space=pltpu.VMEM)] * 2,
        scratch_shapes=[
            cut,
            cut,
            plane,
            pltpu.VMEM((2, rows, LANES), jnp.int32),
            plane,
            pltpu.VMEM((LANES, pad), F32),
            pltpu.VMEM((16, pad), F32),
            pltpu.SemaphoreType.DMA((10,)),
        ],
        compiler_params=PARAMS,
        name="pack_columns",
    )(*map(hbm, (elevation, equilibrium, depth, land_mask, friction)))


def pack_kernel(e, q, d, ints, r, after, m, mn, ms):
    del after
    kdev, _, rows, width = e.shape
    m[...] = ints[...].astype(F32)
    ws = omegas(kdev)
    for out, end, near, low in ((ms, slice(0, 8), 0, 0), (mn, slice(rows - 8, rows), 7, 6)):
        out[:, width:] = jnp.zeros((MSG, LANES), F32)
        r8, d8, m8 = r[end, :], d[end, :], m[end, :]
        up = lambda x: rolled(x, -1, 0)
        coef = (THETA * AY * AY) * (m8 * up(m8) * (d8 + up(d8)))
        r2 = r8 + up(r8)
        for c in range(kdev):
            elev = [e[c, p, end, :] for p in range(2)]
            z = [elev[p] - q[c, p, end, :] for p in range(2)]
            v = face(z[0], z[1], up(z[0]), up(z[1]), r2, coef, 2.0 * ws[c])
            for p in range(2):
                out[2 * p + c, :width] = z[p][near, :]
                out[4 + 2 * p + c, :width] = v[p][low, :]
                out[8 + 2 * p + c, :width] = elev[p][near, :]
        for k, plane in enumerate((r8, d8, m8)):
            out[12 + k, :width] = plane[near, :]
        out[MSG - 1, :width] = jnp.zeros((width,), F32)


def pack(elevation, equilibrium, depth, land_mask, friction, after):
    kdev, _, rows, width = elevation.shape
    plane = pltpu.VMEM(depth.shape, F32)
    row = pltpu.VMEM((MSG, width + LANES), F32)
    return pl.pallas_call(
        pack_kernel,
        out_shape=(plane, row, row),
        in_specs=[pl.BlockSpec(memory_space=pltpu.VMEM)] * 6,
        out_specs=[pl.BlockSpec(memory_space=pltpu.VMEM)] * 3,
        compiler_params=PARAMS,
        name="pack",
    )(*map(vmem, (elevation, equilibrium, depth, land_mask, friction, after)))


def tile_rows(ref, at, size, nxt):
    here = ref[at : at + size, :]
    after = ref[nxt : nxt + 8, :]
    return here, jnp.concatenate([here[1:], after[0:1]], axis=0)


def east(x):
    return rolled(x, -1, 1)


def row_metric(at, size, width, rows):
    first = lax.axis_index("ty") * rows
    index = lax.broadcasted_iota(jnp.int32, (size, LANES), 0) + (first + at)
    ax = metric(index.astype(F32), rows * lax.axis_size("ty"))
    return ax, jnp.concatenate([ax] * (width // LANES), axis=1)


def first_kernel(e, q, d, mask, r, after, e1, send, keep, coef, var):
    del after
    kdev, _, rows, width = e.shape
    size = 16
    ws = omegas(kdev)
    last_v = [jnp.zeros((1, width), F32)] * (2 * kdev)
    for at in range(0, rows, size):
        nxt = min(at + size, rows - 8)
        _, ax = row_metric(at, size, width, rows)
        md, mn = tile_rows(mask, at, size, nxt)
        dd, dn = tile_rows(d, at, size, nxt)
        rd, rn = tile_rows(r, at, size, nxt)
        coef_u = (THETA * ax * ax) * (md * east(md) * (dd + east(dd)))
        coef_v = (THETA * AY * AY) * (md * mn * (dd + dn))
        coef[0, at : at + size, :], coef[1, at : at + size, :] = coef_u, coef_v
        r2u = rd + east(rd)
        r2v = rd + rn
        squ, sqv = r2u * r2u, r2v * r2v
        sum_u = sum_v = None
        for c in range(kdev):
            w2 = 2.0 * ws[c]
            wt = THETA * ws[c]
            er, ern = tile_rows(e.at[c, 0], at, size, nxt)
            ei, ein = tile_rows(e.at[c, 1], at, size, nxt)
            qr, qrn = tile_rows(q.at[c, 0], at, size, nxt)
            qi, qin = tile_rows(q.at[c, 1], at, size, nxt)
            zr, zi = er - qr, ei - qi
            gu = coef_u * recip(squ + w2 * w2)
            gv = coef_v * recip(sqv + w2 * w2)
            ur, ui = flux(zr - east(zr), zi - east(zi), gu, gu * r2u, w2)
            vr, vi = flux(zr - (ern - qrn), zi - (ein - qin), gv, gv * r2v, w2)
            uwr, uwi = rolled(ur, 1, 1), rolled(ui, 1, 1)
            vsr = jnp.concatenate([last_v[2 * c], vr[:-1]], axis=0)
            vsi = jnp.concatenate([last_v[2 * c + 1], vi[:-1]], axis=0)
            last_v[2 * c], last_v[2 * c + 1] = vr[-1:], vi[-1:]
            e1[c, 0, at : at + size, :] = md * (er + wt * ei - (ur - uwr) - (vr - vsr))
            e1[c, 1, at : at + size, :] = md * (ei - wt * er - (ui - uwi) - (vi - vsi))
            su = (ur + uwr) * (ur + uwr) + (ui + uwi) * (ui + uwi)
            sv = (vr + vsr) * (vr + vsr) + (vi + vsi) * (vi + vsi)
            sum_u = su if sum_u is None else sum_u + su
            sum_v = sv if sum_v is None else sum_v + sv
        inv = recip(dd)
        ia = recip(THETA * ax)
        total = (0.125 * ia * ia) * sum_u + (0.125 / (THETA * AY) ** 2) * sum_v
        var[at : at + size, :] = total * (inv * inv)
    half = rows // 2
    core = lax.rem(lax.axis_index("cons"), 2)
    send[:half, :] = var[pl.ds(pl.multiple_of((1 - core) * half, 8), half), :]
    keep[:half, :] = var[pl.ds(pl.multiple_of(core * half, 8), half), :]
    send[half:, :] = keep[half - 8 : half, :]
    keep[half:, :] = send[half - 8 : half, :]


def first_sweep(e, q, d, m, r, after):
    kdev, _, rows, width = e.shape
    half = pltpu.VMEM((rows // 2 + 8, width), F32)
    return pl.pallas_call(
        first_kernel,
        out_shape=(pltpu.VMEM(e.shape, F32), half, half, pltpu.VMEM((2, *d.shape), F32)),
        in_specs=[pl.BlockSpec(memory_space=pltpu.VMEM)] * 6,
        out_specs=[pl.BlockSpec(memory_space=pltpu.VMEM)] * 4,
        scratch_shapes=[pltpu.VMEM(d.shape, F32)],
        compiler_params=PARAMS,
        cost_estimate=pl.CostEstimate(flops=80 * e.size, bytes_accessed=160 * e.size, transcendentals=0),
        name="first_sweep",
    )(*map(vmem, (e, q, d, m, r, after)))


def add_kernel(a, b, *refs):
    refs[-1][...] = a[...] + b[...]


def added(a, b, *after):
    return pl.pallas_call(
        add_kernel,
        out_shape=pltpu.VMEM(a.shape, F32),
        in_specs=[pl.BlockSpec(memory_space=pltpu.VMEM)] * (2 + len(after)),
        out_specs=pl.BlockSpec(memory_space=pltpu.VMEM),
        compiler_params=PARAMS,
        name="added",
    )(vmem(a), vmem(b), *map(vmem, after))


def cut_kernel(a, b, after, *outs):
    del after
    at = 0
    for out in outs:
        here = slice(at, at + out.shape[0])
        out[...] = a[here, :] + b[here, :]
        at += out.shape[0]


def cut_sum(a, b, after):
    rows, width = a.shape
    large = pltpu.VMEM(((rows - 16) // 2, width), F32)
    return pl.pallas_call(
        cut_kernel,
        out_shape=(large, large, pltpu.VMEM((16, width), F32)),
        in_specs=[pl.BlockSpec(memory_space=pltpu.VMEM)] * 3,
        out_specs=[pl.BlockSpec(memory_space=pltpu.VMEM)] * 3,
        compiler_params=PARAMS,
        name="cut_sum",
    )(vmem(a), vmem(b), vmem(after))


def tree_sum(terms):
    while len(terms) > 1:
        terms = [a + b for a, b in zip(terms[::2], terms[1::2])]
    return terms[0]


def early_kernel(after, *refs):
    del after
    pieces, partner, outs = refs[:2], refs[2:4], refs[4:]
    thin = outs[0].shape[0]
    for k, out in enumerate(outs):
        part, at = divmod(k * thin, pieces[0].shape[0])
        out[...] = pieces[part][at : at + thin, :] + partner[part][at : at + thin, :]


def early_sums(pieces, partner, after):
    rows, width = pieces[0].shape
    count = 2 * rows // 16
    return pl.pallas_call(
        early_kernel,
        out_shape=(pltpu.VMEM((16, width), F32),) * count,
        in_specs=[pl.BlockSpec(memory_space=pltpu.VMEM)] * 5,
        out_specs=[pl.BlockSpec(memory_space=pltpu.VMEM)] * count,
        compiler_params=PARAMS,
        name="early_sums",
    )(*map(vmem, (after, *pieces, *partner)))


def join_kernel(tail, partner, both, after, *refs):
    del after
    *others, late, rims = refs
    late[...] = tail[:16, :] + partner[:16, :]
    terms = [x[...] for x in others]
    rims[...] = tree_sum([both[...], partner[16:, :] + terms[0], *[a + b for a, b in zip(terms[1::2], terms[2::2])]])


def joined(*args):
    width = args[0].shape[1]
    return pl.pallas_call(
        join_kernel,
        out_shape=(pltpu.VMEM((16, width), F32), pltpu.VMEM((8, width), F32)),
        in_specs=[pl.BlockSpec(memory_space=pltpu.VMEM)] * len(args),
        out_specs=[pl.BlockSpec(memory_space=pltpu.VMEM)] * 2,
        compiler_params=PARAMS,
        name="joined",
    )(*map(vmem, args))


def roles(a, b):
    even = lax.rem(lax.axis_index("tx"), 2) == 0
    return jnp.where(even, b, a), jnp.where(even, a, b)


def padded(x, pad):
    return jnp.concatenate([x, jnp.zeros((x.shape[0], pad - x.shape[1]), F32)], axis=1)


def merge_kernel(rows, f2, f1, mn, ms, send, mn_out, ms_out, my_out, send_out):
    width = mn.shape[1] - LANES
    fw, fe = roles(f1[...], padded(f2[...], f1.shape[1]))
    lane = lax.broadcasted_iota(jnp.int32, (MSG, LANES), 1)
    last = LANES - 1

    def ends(at):
        east_, west = fe[:, at // LANES * LANES :][:, :LANES], fw[:, at // LANES * LANES :][:, :LANES]
        east_, west = rolled(east_, -(at % LANES), 1), rolled(west, last - at % LANES, 1)
        return jnp.where(lane == 0, east_, jnp.where(lane == last, west, 0.0))

    mn_out[:, :width] = mn[:, :width]
    ms_out[:, :width] = ms[:, :width]
    mn_out[:, width:] = ends(rows - 1)
    ms_out[:, width:] = ends(0)
    low = lax.axis_index("ty") == 0
    my_out[...] = jnp.where(low, mn_out[...], ms_out[...])
    send_out[...] = send[...]


def merge(rows, f1, f2, mn, ms, send):
    out = pltpu.VMEM(mn.shape, F32)
    return pl.pallas_call(
        functools.partial(merge_kernel, rows),
        out_shape=(out, out, out, pltpu.VMEM(send.shape, F32)),
        in_specs=[pl.BlockSpec(memory_space=pltpu.VMEM)] * 5,
        out_specs=[pl.BlockSpec(memory_space=pltpu.VMEM)] * 4,
        compiler_params=PARAMS,
        name="merge",
    )(*map(vmem, (f2, f1, mn, ms, send)))


def strip_omega(shape, ws):
    odd = lax.rem(lax.broadcasted_iota(jnp.int32, shape, 0), 2)
    return jnp.where(odd == 0, ws[0], ws[1])


def strip_sweep(low, high, ws, g_across, g_along):
    none = jnp.zeros((2, low.shape[1]), F32)

    def field(at):
        return jnp.concatenate([none, low[at : at + 2], high[at : at + 2], none], axis=0)

    def single(at):
        a, b = low[at : at + 1], high[at : at + 1]
        return jnp.concatenate([none, a, a, b, b, none], axis=0)

    def given(at):
        return jnp.concatenate([low[at : at + 2], none, high[at : at + 2], none], axis=0)

    zr, zi, er, ei = field(0), field(2), field(8), field(10)
    r, d, m = single(12), single(13), single(14)
    w = strip_omega(zr.shape, ws)
    w2 = 2.0 * w
    wt = THETA * w
    up = lambda x: rolled(x, -2, 0)
    nx = lambda x: rolled(x, -1, 1)
    coef_a = (THETA * g_across * g_across) * (m * up(m) * (d + up(d)))
    coef_l = (THETA * g_along * g_along) * (m * nx(m) * (d + nx(d)))
    ar, ai = face(zr, zi, up(zr), up(zi), r + up(r), coef_a, w2)
    middle = lax.broadcasted_iota(jnp.int32, zr.shape, 0) // 2 == 1
    ar, ai = jnp.where(middle, ar, given(4)), jnp.where(middle, ai, given(6))
    lr, li = face(zr, zi, nx(zr), nx(zi), r + nx(r), coef_l, w2)
    abr, abi = rolled(ar, 2, 0), rolled(ai, 2, 0)
    lbr, lbi = rolled(lr, 1, 1), rolled(li, 1, 1)
    e1r = m * (er + wt * ei - (ar - abr) - (lr - lbr))
    e1i = m * (ei - wt * er - (ai - abi) - (li - lbi))
    sa = (ar + abr) * (ar + abr) + (ai + abi) * (ai + abi)
    sl = (lr + lbr) * (lr + lbr) + (li + lbi) * (li + lbi)
    inv = recip(jnp.maximum(d, TINY_DEPTH))
    ia = recip(THETA * g_across)
    il = recip(THETA * g_along)
    var = 0.125 * (ia * ia * sa + il * il * sl) * (inv * inv)
    var = var + rolled(var, -1, 0)
    z1r = e1r - (er - zr)
    z1i = e1i - (ei - zi)
    return (z1r, z1i, d, coef_a, e1r, e1i), var


def strip_lines(rows, m2, m1, f2, f1, mn, ms, fn_ref, fs_ref):
    width = mn.shape[1] - LANES
    pad = m1.shape[1]
    ty, count = lax.axis_index("ty"), lax.axis_size("ty")
    fn = jnp.where(ty < count - 1, fn_ref[...], 0.0)
    fs = jnp.where(ty > 0, fs_ref[...], 0.0)
    mw, me = roles(m1[...], padded(m2[...], pad))
    fw, fe = roles(f1[...], padded(f2[...], pad))
    hi = rows - (pad - LANES)
    last = LANES - 1
    lane = lax.broadcasted_iota(jnp.int32, (MSG, LANES), 1)

    def ended(msg, block, at):
        end = msg[:, pad - LANES :]
        end = jnp.where(lane == hi, rolled(fn[:, block : block + LANES], hi - at, 1), end)
        end = jnp.where(lane == last, rolled(fs[:, block : block + LANES], last - at, 1), end)
        return jnp.concatenate([msg[:, : pad - LANES], end], axis=1)

    low_w, high_w = ended(fw, width, last), ended(mw, 0, 0)
    low_e, high_e = ended(me, width - LANES, last), ended(fe, width, 0)
    return (fs, ms[...]), (mn[...], fn), (low_w, high_w), (low_e, high_e)


def line_metric(lines, rows, width):
    ax = metric((lines + lax.axis_index("ty") * rows).astype(F32), rows * lax.axis_size("ty"))
    return jnp.concatenate([ax] * (width // LANES), axis=1)


def column_metric(rows, pad):
    first = (lax.axis_index("ty") * rows).astype(F32)
    row = lax.broadcasted_iota(jnp.int32, (8, pad), 1).astype(F32) + first
    return metric(jnp.minimum(row, first + rows), rows * lax.axis_size("ty"))


def strips(rows, *refs):
    ws = omegas(2)
    line = lax.broadcasted_iota(jnp.int32, (8, LANES), 0) // 2
    south, north, west, east_ = strip_lines(rows, *refs)
    width, pad = south[0].shape[1], west[0].shape[1]
    out = [
        strip_sweep(*pair, ws, AY, line_metric(line + start, rows, width))
        for pair, start in ((south, -2), (north, rows - 2))
    ]
    ax = column_metric(rows, pad)
    return out + [strip_sweep(*pair, ws, ax, AY) for pair in (west, east_)]


def pair_variance(a, b, ws, g_across, g_along):
    sides = (*a, *b)

    def field(at):
        return jnp.concatenate([x[at : at + 2] for x in sides], axis=0)

    def single(at):
        return jnp.concatenate([x[at : at + 1] for x in sides for _ in range(2)], axis=0)

    zr, zi = field(0), field(2)
    r, d, m = single(12), single(13), single(14)
    w2 = 2.0 * strip_omega(zr.shape, ws)
    up = lambda x: rolled(x, -2, 0)
    nx = lambda x: rolled(x, -1, 1)
    coef_a = (THETA * g_across * g_across) * (m * up(m) * (d + up(d)))
    coef_l = (THETA * g_along * g_along) * (m * nx(m) * (d + nx(d)))
    inner = face(zr, zi, up(zr), up(zi), r + up(r), coef_a, w2)
    low_line = lax.rem(lax.broadcasted_iota(jnp.int32, zr.shape, 0) // 2, 2) == 0
    sa = sl = None
    along = face(zr, zi, nx(zr), nx(zi), r + nx(r), coef_l, w2)
    for p in range(2):
        outer = field(4 + 2 * p)
        both = jnp.where(low_line, inner[p], outer) + jnp.where(low_line, outer, rolled(inner[p], 2, 0))
        other = along[p] + rolled(along[p], 1, 1)
        sa = both * both if sa is None else sa + both * both
        sl = other * other if sl is None else sl + other * other
    inv = recip(jnp.maximum(d, TINY_DEPTH))
    ia = recip(THETA * g_across)
    il = recip(THETA * g_along)
    var = 0.125 * (ia * ia * sa + il * il * sl) * (inv * inv)
    return var + rolled(var, -1, 0)


def rim_kernel(rows, after, *refs):
    del after
    *refs, row_sums, col_sums = refs
    ws = omegas(2)
    south, north, west, east_ = strip_lines(rows, *refs)
    width, pad = row_sums.shape[1], west[0].shape[1]
    index = lax.broadcasted_iota(jnp.int32, (8, LANES), 0)
    line = lax.rem(index // 2, 2) - 1 + index // 4 * rows
    var = pair_variance(south, north, ws, AY, line_metric(line, rows, south[0].shape[1]))
    for k in range(4):
        row_sums[k, :] = var[2 * k, :width]
    var = pair_variance(west, east_, ws, column_metric(rows, pad), AY)
    for k in range(4):
        col_sums[k // 2, k % 2 * pad : (k % 2 + 1) * pad] = var[2 * k, :]
    col_sums[2:, :] = jnp.zeros((2, width), F32)


def strips_kernel(rows, *refs):
    for out, (held, _) in zip(refs[-4:], strips(rows, *refs[:-4])):
        for k, x in enumerate(held):
            out[8 * k : 8 * k + 8, :] = x


def rim(rows, late, *messages):
    width = late.shape[1]
    return pl.pallas_call(
        functools.partial(rim_kernel, rows),
        out_shape=(pltpu.VMEM((4, width), F32),) * 2,
        in_specs=[pl.BlockSpec(memory_space=pltpu.VMEM)] * 9,
        out_specs=[pl.BlockSpec(memory_space=pltpu.VMEM)] * 2,
        compiler_params=PARAMS,
        name="rim",
    )(*map(vmem, (late, *messages)))


def stack_kernel(a, b, out):
    out[: a.shape[0], :] = a[...]
    out[a.shape[0] :, :] = b[...]


def stacked(a, b):
    return pl.pallas_call(
        stack_kernel,
        out_shape=pltpu.VMEM((a.shape[0] + b.shape[0], a.shape[1]), F32),
        in_specs=[pl.BlockSpec(memory_space=pltpu.VMEM)] * 2,
        out_specs=pl.BlockSpec(memory_space=pltpu.VMEM),
        compiler_params=PARAMS,
        name="stacked",
    )(vmem(a), vmem(b))


def held_strips(rows, *messages):
    row = pltpu.VMEM((48, messages[4].shape[1]), F32)
    col = pltpu.VMEM((48, messages[1].shape[1]), F32)
    return pl.pallas_call(
        functools.partial(strips_kernel, rows),
        out_shape=(row, row, col, col),
        in_specs=[pl.BlockSpec(memory_space=pltpu.VMEM)] * 8,
        out_specs=[pl.BlockSpec(memory_space=pltpu.VMEM)] * 4,
        compiler_params=PARAMS,
        name="held_strips",
    )(*map(vmem, messages))


def prepare_kernel(e1_in, q, m, ss, sn, sw, se, du, dv, base, e1, cols):
    kdev, _, rows, width = e1_in.shape
    size = 16
    ws = omegas(kdev)
    e1[...] = e1_in[...]
    for p in range(2):
        cols[2 * p : 2 * p + 2, :] = sw[8 * (4 + p) + 4 : 8 * (4 + p) + 6, :]
        cols[4 + 2 * p : 6 + 2 * p, :] = se[8 * (4 + p) + 2 : 8 * (4 + p) + 4, :]
    turned = cols[...].T
    lane = lax.broadcasted_iota(jnp.int32, (rows, LANES), 1)
    left, right = slice(0, LANES), slice(width - LANES, width)
    last = LANES - 1
    for p in range(2):
        for c in range(kdev):
            e1[c, p, 0:1, :] = ss[8 * (4 + p) + 4 + c : 8 * (4 + p) + 5 + c, :width]
            e1[c, p, rows - 1 : rows, :] = sn[8 * (4 + p) + 2 + c : 8 * (4 + p) + 3 + c, :width]
            k = 2 * p + c
            e1[c, p, :, left] = jnp.where(lane == 0, rolled(turned[:rows], -k, 1), e1[c, p, :, left])
            k = 4 + 2 * p + c
            e1[c, p, :, right] = jnp.where(lane == last, rolled(turned[:rows], last - k, 1), e1[c, p, :, right])
    for at in range(0, rows, size):
        nxt = min(at + size, rows - 8)
        here = slice(at, at + size)
        md = m[here, :]
        for c in range(kdev):
            wt = THETA * ws[c]
            er, ern = tile_rows(e1.at[c, 0], at, size, nxt)
            ei, ein = tile_rows(e1.at[c, 1], at, size, nxt)
            qr, qrn = tile_rows(q.at[c, 0], at, size, nxt)
            qi, qin = tile_rows(q.at[c, 1], at, size, nxt)
            zr, zi = er - qr, ei - qi
            du[c, 0, here, :] = zr - east(zr)
            du[c, 1, here, :] = zi - east(zi)
            dv[c, 0, here, :] = zr - (ern - qrn)
            dv[c, 1, here, :] = zi - (ein - qin)
            base[c, 0, here, :] = md * (er + wt * ei)
            base[c, 1, here, :] = md * (ei - wt * er)


def prepare(e1, q, m, ss, sn, sw, se):
    plane = pltpu.VMEM(e1.shape, F32)
    return pl.pallas_call(
        prepare_kernel,
        out_shape=(plane, plane, plane),
        in_specs=[pl.BlockSpec(memory_space=pltpu.VMEM)] * 7,
        out_specs=[pl.BlockSpec(memory_space=pltpu.VMEM)] * 3,
        scratch_shapes=[pltpu.VMEM(e1.shape, F32), pltpu.VMEM((LANES, sw.shape[1]), F32)],
        compiler_params=PARAMS,
        cost_estimate=pl.CostEstimate(flops=40 * e1.size, bytes_accessed=160 * e1.size, transcendentals=0),
        name="prepare",
    )(*map(vmem, (e1, q, m, ss, sn, sw, se)))


def rate(var, d):
    s = var + BACKGROUND
    return (DRAG * (s * lax.rsqrt(s))) * recip(d)


def sweep_tile(row, size, r, r_north, du, dv, base, coef, m, turned, ws, last_v, top):
    kdev, width = du.shape[0], du.shape[3]
    here = pl.ds(row, size)
    edges = turned[here, :]
    md = m[here, :]
    coef_u, coef_v = coef[0, here, :], coef[1, here, :]
    r2u = r + east(r)
    r2v = r + r_north
    squ, sqv = r2u * r2u, r2v * r2v
    lane = lax.broadcasted_iota(jnp.int32, (size, LANES), 1)
    last = LANES - 1

    def with_east(u, k):
        block = jnp.where(lane == last, rolled(edges, last - k, 1), u[:, width - LANES :])
        return jnp.concatenate([u[:, : width - LANES], block], axis=1)

    def from_west(u, k):
        u = rolled(u, 1, 1)
        block = jnp.where(lane == 0, rolled(edges, -k, 1), u[:, :LANES])
        return jnp.concatenate([block, u[:, LANES:]], axis=1)

    planes, out_v = {}, {}
    for c in range(kdev):
        w2 = 2.0 * ws[c]
        gu = coef_u * recip(squ + w2 * w2)
        gv = coef_v * recip(sqv + w2 * w2)
        u = flux(du[c, 0, here, :], du[c, 1, here, :], gu, gu * r2u, w2)
        v = flux(dv[c, 0, here, :], dv[c, 1, here, :], gv, gv * r2v, w2)
        for p in range(2):
            up, vp = with_east(u[p], 4 + 2 * p + c), v[p]
            if top is not None:
                vp = jnp.concatenate([vp[:-1], top(c, p, vp[-1:])], axis=0)
            uw = from_west(up, 2 * p + c)
            vs = jnp.concatenate([last_v[c, p], vp[:-1]], axis=0)
            out_v[c, p] = vp[-1:]
            planes[c, p] = base[c, p, here, :], md * ((up - uw) + (vp - vs))
    return planes, out_v


def pairs(kdev):
    return [(c, p) for c in range(kdev) for p in range(2)]


def half_rate(var, rims, turned, d, row, low, half):
    here = pl.ds(row, half)
    edges = turned[here, :]
    width = var.shape[1]
    index = lax.broadcasted_iota(jnp.int32, (8, width), 0)
    first = jnp.where(low & (index == 0), rims[1:2], var[:8])
    final = jnp.where(jnp.logical_not(low) & (index == 7), rims[2:3], var[half - 8 :])
    var = jnp.concatenate([first, var[8 : half - 8], final], axis=0)
    lane = lax.broadcasted_iota(jnp.int32, (half, LANES), 1)
    left = jnp.where(lane == 0, rolled(edges, -8, 1), var[:, :LANES])
    right = jnp.where(lane == LANES - 1, rolled(edges, LANES - 1 - 9, 1), var[:, width - LANES :])
    return rate(jnp.concatenate([left, var[:, LANES : width - LANES], right], axis=1), d[here, :])


def own_kernel(du, dv, base, coef, d, m, late, rims_ref, ss, sn, sw, se, *refs):
    *mine, first_part, update, fric, vs_out, vn_out, turned, cols = refs
    kdev, _, half, width = update.shape
    pad = sw.shape[1]
    ws = omegas(kdev)
    core = lax.rem(lax.axis_index("cons"), 2)
    low = core == 0
    rims = rims_ref[...]

    def edge(strip, var_a, var_b):
        zr, zi, dep, ca = (strip[8 * k : 8 * k + 8, :] for k in range(4))
        var = jnp.concatenate([var_a, var_a, var_a, var_a, var_b, var_b, var_b, var_b], axis=0)
        f = rate(var, jnp.maximum(dep, TINY_DEPTH))
        up = lambda x: rolled(x, -2, 0)
        w2 = 2.0 * strip_omega(zr.shape, ws)
        return face(zr, zi, up(zr), up(zi), f + up(f), ca, w2)

    none = jnp.zeros((1, LANES), F32)
    wide = lambda x: jnp.concatenate([x, none], axis=1)
    south = edge(ss, wide(rims[0:1]), wide(rims[1:2]))
    north = edge(sn, wide(rims[2:3]), wide(rims[3:4]))
    west = edge(sw, rims[4:5, :pad], rims[4:5, pad : 2 * pad])
    east_ = edge(se, rims[5:6, :pad], rims[5:6, pad : 2 * pad])
    for p in range(2):
        cols[2 * p : 2 * p + 2, :] = west[p][2:4]
        cols[4 + 2 * p : 6 + 2 * p, :] = east_[p][2:4]
        for c in range(kdev):
            vs_out[2 * c + p : 2 * c + p + 1, :] = south[p][2 + c : 3 + c, :width]
            vn_out[2 * c + p : 2 * c + p + 1, :] = north[p][2 + c : 3 + c, :width]
    cols[8:9, :] = rims[4:5, pad : 2 * pad]
    cols[9:10, :] = rims[5:6, :pad]
    turned[...] = cols[...].T

    first = pl.multiple_of(core * half, 8)
    var = jnp.concatenate([x[...] for x in mine] + [late[:8, :]], axis=0)
    fric[...] = half_rate(var, rims, turned, d, first, low, half)
    size = 24
    last_v = {(c, p): jnp.where(low, vs_out[2 * c + p : 2 * c + p + 1, :], 0.0) for c, p in pairs(kdev)}

    def top(c, p, own):
        return jnp.where(low, 0.0, vn_out[2 * c + p : 2 * c + p + 1, :])

    for at in range(0, half, size):
        r, rn = tile_rows(fric, at, size, min(at + size, half - 8))
        planes, last_v = sweep_tile(
            pl.multiple_of(first + at, 8), size, r, rn, du, dv, base, coef, m, turned, ws, last_v,
            top if at + size == half else None,
        )
        for c, p in pairs(kdev):
            first_part[c, p, at : at + size, :], update[c, p, at : at + size, :] = planes[c, p]


def own_half(*args):
    kdev, _, rows, width = args[0].shape
    pad = args[10].shape[1]
    line = pltpu.VMEM((8, width), F32)
    return pl.pallas_call(
        own_kernel,
        out_shape=(
            pltpu.VMEM((kdev, 2, rows // 2, width), F32),
            pltpu.VMEM((kdev, 2, rows // 2, width), F32),
            pltpu.VMEM((rows // 2, width), F32),
            line,
            line,
            pltpu.VMEM((pad, LANES), F32),
        ),
        in_specs=[pl.BlockSpec(memory_space=pltpu.VMEM)] * len(args),
        out_specs=[pl.BlockSpec(memory_space=pltpu.VMEM)] * 6,
        scratch_shapes=[pltpu.VMEM((LANES, pad), F32)],
        compiler_params=PARAMS,
        name="own_half",
    )(*map(vmem, args))


def other_kernel(du, dv, base, coef, d, m, late, rims, eta_own, fric_own, vs, vn, turned, *refs):
    *other, eta_out, fric_out, eta, fric, fixed, sems = refs
    kdev, _, half, width = eta.shape
    ws = omegas(kdev)
    core = lax.rem(lax.axis_index("cons"), 2)
    own_low = core == 0
    own, first = pl.multiple_of(core * half, 8), pl.multiple_of((1 - core) * half, 8)
    copies = []

    def put(src, dst):
        copy = pltpu.make_async_copy(src, dst, sems.at[len(copies)])
        copy.start()
        copies.append(copy)

    skip = pl.multiple_of(core * 8, 8)
    put(
        eta_own.at[:, :, pl.ds(skip, half - 8), :],
        eta_out.at[:, :, pl.ds(pl.multiple_of(own + skip, 8), half - 8), :],
    )
    put(fric_own, fric_out.at[pl.ds(own, half), :])
    fric[pl.ds(own, half), :] = fric_own[...]
    fric[pl.ds(first, half), :] = half_rate(
        jnp.concatenate([x[...] for x in other] + [late[8:, :]], axis=0),
        rims[...], turned, d, first, jnp.logical_not(own_low), half,
    )
    put(fric.at[pl.ds(first, half), :], fric_out.at[pl.ds(first, half), :])

    r, rn = tile_rows(fric, half - 8, 8, half)
    r2 = r + rn
    between = {}
    for c in range(kdev):
        w2 = 2.0 * ws[c]
        g = coef[1, half - 8 : half, :] * recip(r2 * r2 + w2 * w2)
        v = flux(dv[c, 0, half - 8 : half, :], dv[c, 1, half - 8 : half, :], g, g * r2, w2)
        for p in range(2):
            between[c, p] = v[p][7:8]
    index = lax.broadcasted_iota(jnp.int32, (8, width), 0)
    at_face = index == jnp.where(own_low, 7, 0)
    sign = jnp.where(own_low, -1.0, 1.0)
    local = pl.ds(pl.multiple_of((1 - core) * (half - 8), 8), 8)
    border = pl.ds(pl.multiple_of(half - 8 + 8 * core, 8), 8)
    md = m[border, :]
    for c, p in pairs(kdev):
        fixed[c, p] = eta_own[c, p, local, :] + jnp.where(at_face, sign * (md * between[c, p]), 0.0)
    put(fixed, eta_out.at[:, :, border, :])

    size = 24
    rows = 2 * half
    last_v = {(c, p): jnp.where(own_low, between[c, p], vs[2 * c + p : 2 * c + p + 1, :]) for c, p in pairs(kdev)}

    def top(c, p, own_v):
        return jnp.where(own_low, vn[2 * c + p : 2 * c + p + 1, :], own_v)

    for at in range(0, half, size):
        row = pl.multiple_of(first + at, 8)
        r = fric[pl.ds(row, size), :]
        after = fric[pl.ds(pl.multiple_of(jnp.minimum(row + size, rows - 8), 8), 8), :]
        rn = jnp.concatenate([r[1:], after[0:1]], axis=0)
        planes, last_v = sweep_tile(
            row, size, r, rn, du, dv, base, coef, m, turned, ws, last_v, top if at + size == half else None
        )
        for c, p in pairs(kdev):
            eta[c, p, at : at + size, :] = planes[c, p][0] - planes[c, p][1]
        put(eta.at[:, :, at : at + size, :], eta_out.at[:, :, pl.ds(row, size), :])
    for copy in copies:
        copy.wait()


def other_half(*args):
    du, d = args[0], args[4]
    kdev, _, rows, width = du.shape
    return pl.pallas_call(
        other_kernel,
        out_shape=(jax.ShapeDtypeStruct(du.shape, F32), jax.ShapeDtypeStruct(d.shape, F32)),
        in_specs=[pl.BlockSpec(memory_space=pltpu.VMEM)] * len(args),
        out_specs=[pl.BlockSpec(memory_space=pltpu.HBM)] * 2,
        scratch_shapes=[
            pltpu.VMEM((kdev, 2, rows // 2, width), F32),
            pltpu.VMEM(d.shape, F32),
            pltpu.VMEM((kdev, 2, 8, width), F32),
            pltpu.SemaphoreType.DMA((4 + rows // 2 // 24,)),
        ],
        compiler_params=PARAMS,
        name="other_half",
    )(*map(vmem, args))


def swapped(x, axis, bit):
    return lax.ppermute(x, axis, [(i, i ^ bit) for i in range(lax.axis_size(axis))])


def body(elevation, equilibrium, depth, land_mask, friction_prev):
    rows = depth.shape[0]
    ntx, nty, ncons = (lax.axis_size(a) for a in ("tx", "ty", "cons"))
    fields = (elevation, equilibrium, depth, land_mask, friction_prev)
    m2, m1 = pack_columns(*fields)
    elev, equil, depth, mask, fric = elevation, equilibrium, depth, land_mask, friction_prev
    mask, mn, ms = pack(*fields, m1)
    f2 = lax.ppermute(m2, "tx", [(i, (i - 1 if i % 2 == 0 else i + 1) % ntx) for i in range(ntx)])
    f1 = swapped(m1, "tx", 1)
    e1, send, keep, coef = first_sweep(elev, equil, depth, mask, fric, m1)
    mn, ms, my, send = merge(rows, f1, f2, mn, ms, send)
    recv = swapped(send, "cons", 1)
    if nty == 2:
        fn = fs = swapped(my, "ty", 1)
    else:
        fn = lax.ppermute(ms, "ty", [(i, i - 1) for i in range(1, nty)])
        fs = lax.ppermute(mn, "ty", [(i, i + 1) for i in range(nty - 1)])
    first, second, late = cut_sum(recv, keep, my)
    messages = (m2, m1, f2, f1, mn, ms, fn, fs)
    rims = jnp.concatenate(rim(rows, late, *messages), axis=0)
    tail = stacked(late, rims)
    ss, sn, sw, se = held_strips(rows, *messages)
    prepared = prepare(e1, equil, mask, ss, sn, sw, se)
    partner = [swapped(x, "cons", 2) for x in (first, second, tail)]
    others = [swapped(rims, "cons", k) for k in range(1, ncons) if k != 2]
    both = added(rims, others[0], prepared[2])
    mine = early_sums((first, second), partner[:2], both)
    bit = 4
    while bit < ncons:
        mine = [added(x, swapped(x, "cons", bit)) for x in mine]
        tail, partner[2] = added(tail, partner[2]), swapped(added(tail, partner[2]), "cons", bit)
        bit *= 2
    other = [swapped(x, "cons", 1) for x in mine]
    late, rims = joined(tail, partner[2], both, other[0], *others[1:])
    fields = (*prepared, coef, depth, mask, late, rims)
    first_part, update, *own = own_half(*fields, ss, sn, sw, se, *mine)
    return other_half(*fields, first_part - update, *own, *other)


def solution(mesh):
    return jax.shard_map(
        body,
        mesh=mesh,
        in_specs=(
            P("cons", None, "ty", "tx"),
            P("cons", None, "ty", "tx"),
            P("ty", "tx"),
            P("ty", "tx"),
            P("ty", "tx"),
        ),
        out_specs=(P("cons", None, "ty", "tx"), P("ty", "tx")),
        check_vma=False,
    )
```

```python
import functools
import math

import jax
import jax.numpy as jnp
from jax import lax
from jax.experimental import pallas as pl
from jax.experimental.pallas import tpu as pltpu
from jax.sharding import PartitionSpec as P

OMEGA_TABLE = (1.0, 1.0351, 0.9582, 1.0379, 0.5181, 0.4816, 0.5164, 0.4454)
AY = 0.5
THETA = 0.05
DRAG = 0.5
BACKGROUND = 0.01
F32 = jnp.float32
LANES = 128
MSG = 16
TINY_DEPTH = 1e-6
PARAMS = pltpu.CompilerParams(vmem_limit_bytes=16 * 1024 * 1024)


def vmem(x):
    return pltpu.with_memory_space_constraint(x, pltpu.VMEM)


def hbm(x):
    return pltpu.with_memory_space_constraint(x, pltpu.HBM)


def recip(x):
    return pl.reciprocal(x, approx=True) if jnp.ndim(x) else 1.0 / x


def metric(rows, total):
    lat = (rows + 0.5) * (120.0 / total * math.pi / 180.0) - math.pi / 3.0
    s = lat * lat
    acc = jnp.full_like(s, 1.0 / math.factorial(16))
    for n in (14, 12, 10, 8, 6, 4, 2, 0):
        acc = ((-1.0) ** (n // 2)) / math.factorial(n) + s * acc
    return 0.5 / acc


def omegas(kdev):
    index = lax.axis_index("cons")
    out = []
    for c in range(kdev):
        w = jnp.float32(OMEGA_TABLE[c])
        for i in range(1, len(OMEGA_TABLE) // kdev):
            w = jnp.where(index == i, jnp.float32(OMEGA_TABLE[i * kdev + c]), w)
        out.append(w)
    return out


def rolled(x, shift, axis):
    return pltpu.roll(x, shift % x.shape[axis], axis)


def face(zr, zi, zr_next, zi_next, r2, coef, w2):
    g = coef * recip(r2 * r2 + w2 * w2)
    a = g * r2
    b = g * w2
    dr = zr - zr_next
    di = zi - zi_next
    return a * dr + b * di, a * di - b * dr


def flux(dr, di, g, a, w2):
    b = g * w2
    return a * dr + b * di, a * di - b * dr


def pack_columns_kernel(e_in, q_in, d_in, m_in, r_in, m2, m1, e, q, d, m, r, turned, behind, sems):
    rows, width = d_in.shape
    copies = []
    for s, side in enumerate((slice(0, LANES), slice(width - LANES, width))):
        for src, dst in ((e_in, e), (q_in, q)):
            copies.append((src.at[:, :, :, side], dst.at[s]))
        for src, dst in ((d_in, d), (m_in, m), (r_in, r)):
            copies.append((src.at[:, side], dst.at[s]))
    copies = [pltpu.make_async_copy(src, dst, sems.at[k]) for k, (src, dst) in enumerate(copies)]
    for copy in copies:
        copy.start()
    for copy in copies:
        copy.wait()
    lane = lax.broadcasted_iota(jnp.int32, (rows, LANES), 1)

    def edges(plane):
        return jnp.where(lane < LANES // 2, plane(0), plane(1))

    elev = [edges(lambda s: e[s, c, p]) for p in range(2) for c in range(2)]
    equil = [edges(lambda s: q[s, c, p]) for p in range(2) for c in range(2)]
    planes = [x - y for x, y in zip(elev, equil)]
    planes += [edges(lambda s: r[s]), edges(lambda s: d[s]), edges(lambda s: m[s]).astype(F32)]
    both = jnp.zeros((rows, LANES), F32)
    for k, plane in enumerate(planes + elev):
        both = jnp.where((lane >= 4 * k) & (lane < 4 * k + 4), rolled(plane, 4 * k + 2, 1), both)
    pad = turned.shape[1]
    turned[...] = jnp.concatenate([both, jnp.zeros((pad - rows, LANES), F32)], axis=0).T
    odd = lax.rem(lax.axis_index("tx"), 2)
    first = (lax.axis_index("ty") * rows).astype(F32)
    lat_row = jnp.minimum(lax.broadcasted_iota(jnp.int32, (8, pad), 1), rows).astype(F32) + first
    ax = metric(lat_row, rows * lax.axis_size("ty"))
    w0, w1 = omegas(2)
    w2 = 2.0 * jnp.where(lax.broadcasted_iota(jnp.int32, (8, pad), 0) < 4, w0, w1)
    up = lambda x: rolled(x, -1, 0)
    zr, zi = turned[0:8, :], turned[8:16, :]
    r8, d8, m8 = (jnp.concatenate([turned[at : at + 4, :]] * 2, axis=0) for at in (16, 20, 24))
    coef = (THETA * ax * ax) * (m8 * up(m8) * (d8 + up(d8)))
    behind[0:8, :], behind[8:16, :] = face(zr, zi, up(zr), up(zi), r8 + up(r8), coef, w2)
    for out, west in ((m1, odd), (m2, 1 - odd)):
        lanes = slice(0, out.shape[1])
        for k in range(4):
            out[k : k + 1, :] = turned[pl.ds(4 * k + 1 + west, 1), lanes]
            out[4 + k : 5 + k, :] = behind[pl.ds(4 * k + 2 * west, 1), lanes]
            out[8 + k : 9 + k, :] = turned[pl.ds(4 * (7 + k) + 1 + west, 1), lanes]
        for k in range(3):
            out[12 + k : 13 + k, :] = turned[pl.ds(4 * (4 + k) + 1 + west, 1), lanes]
        out[MSG - 1 :, :] = jnp.zeros((1, out.shape[1]), F32)


def pack_columns(elevation, equilibrium, depth, land_mask, friction):
    kdev, _, rows, width = elevation.shape
    pad = -(-rows // LANES) * LANES
    cut, plane = pltpu.VMEM((2, kdev, 2, rows, LANES), F32), pltpu.VMEM((2, rows, LANES), F32)
    return pl.pallas_call(
        pack_columns_kernel,
        out_shape=(pltpu.VMEM((MSG, rows), F32), pltpu.VMEM((MSG, pad), F32)),
        in_specs=[pl.BlockSpec(memory_space=pltpu.HBM)] * 5,
        out_specs=[pl.BlockSpec(memory_space=pltpu.VMEM)] * 2,
        scratch_shapes=[
            cut,
            cut,
            plane,
            pltpu.VMEM((2, rows, LANES), jnp.int32),
            plane,
            pltpu.VMEM((LANES, pad), F32),
            pltpu.VMEM((16, pad), F32),
            pltpu.SemaphoreType.DMA((10,)),
        ],
        compiler_params=PARAMS,
        name="pack_columns",
    )(*map(hbm, (elevation, equilibrium, depth, land_mask, friction)))


def pack_kernel(e, q, d, ints, r, after, m, mn, ms):
    del after
    kdev, _, rows, width = e.shape
    m[...] = ints[...].astype(F32)
    ws = omegas(kdev)
    for out, end, near, low in ((ms, slice(0, 8), 0, 0), (mn, slice(rows - 8, rows), 7, 6)):
        out[:, width:] = jnp.zeros((MSG, LANES), F32)
        r8, d8, m8 = r[end, :], d[end, :], m[end, :]
        up = lambda x: rolled(x, -1, 0)
        coef = (THETA * AY * AY) * (m8 * up(m8) * (d8 + up(d8)))
        r2 = r8 + up(r8)
        for c in range(kdev):
            elev = [e[c, p, end, :] for p in range(2)]
            z = [elev[p] - q[c, p, end, :] for p in range(2)]
            v = face(z[0], z[1], up(z[0]), up(z[1]), r2, coef, 2.0 * ws[c])
            for p in range(2):
                out[2 * p + c, :width] = z[p][near, :]
                out[4 + 2 * p + c, :width] = v[p][low, :]
                out[8 + 2 * p + c, :width] = elev[p][near, :]
        for k, plane in enumerate((r8, d8, m8)):
            out[12 + k, :width] = plane[near, :]
        out[MSG - 1, :width] = jnp.zeros((width,), F32)


def pack(elevation, equilibrium, depth, land_mask, friction, after):
    kdev, _, rows, width = elevation.shape
    plane = pltpu.VMEM(depth.shape, F32)
    row = pltpu.VMEM((MSG, width + LANES), F32)
    return pl.pallas_call(
        pack_kernel,
        out_shape=(plane, row, row),
        in_specs=[pl.BlockSpec(memory_space=pltpu.VMEM)] * 6,
        out_specs=[pl.BlockSpec(memory_space=pltpu.VMEM)] * 3,
        compiler_params=PARAMS,
        name="pack",
    )(*map(vmem, (elevation, equilibrium, depth, land_mask, friction, after)))


def tile_rows(ref, at, size, nxt):
    here = ref[at : at + size, :]
    after = ref[nxt : nxt + 8, :]
    return here, jnp.concatenate([here[1:], after[0:1]], axis=0)


def east(x):
    return rolled(x, -1, 1)


def row_metric(at, size, width, rows):
    first = lax.axis_index("ty") * rows
    index = lax.broadcasted_iota(jnp.int32, (size, LANES), 0) + (first + at)
    ax = metric(index.astype(F32), rows * lax.axis_size("ty"))
    return ax, jnp.concatenate([ax] * (width // LANES), axis=1)


def first_kernel(e, q, d, mask, r, after, e1, send, keep, coef, var):
    del after
    kdev, _, rows, width = e.shape
    size = 24
    ws = omegas(kdev)
    last_v = [jnp.zeros((1, width), F32)] * (2 * kdev)
    for at in range(0, rows, size):
        nxt = min(at + size, rows - 8)
        _, ax = row_metric(at, size, width, rows)
        md, mn = tile_rows(mask, at, size, nxt)
        dd, dn = tile_rows(d, at, size, nxt)
        rd, rn = tile_rows(r, at, size, nxt)
        coef_u = (THETA * ax * ax) * (md * east(md) * (dd + east(dd)))
        coef_v = (THETA * AY * AY) * (md * mn * (dd + dn))
        coef[0, at : at + size, :], coef[1, at : at + size, :] = coef_u, coef_v
        r2u = rd + east(rd)
        r2v = rd + rn
        squ, sqv = r2u * r2u, r2v * r2v
        sum_u = sum_v = None
        for c in range(kdev):
            w2 = 2.0 * ws[c]
            wt = THETA * ws[c]
            er, ern = tile_rows(e.at[c, 0], at, size, nxt)
            ei, ein = tile_rows(e.at[c, 1], at, size, nxt)
            qr, qrn = tile_rows(q.at[c, 0], at, size, nxt)
            qi, qin = tile_rows(q.at[c, 1], at, size, nxt)
            zr, zi = er - qr, ei - qi
            gu = coef_u * recip(squ + w2 * w2)
            gv = coef_v * recip(sqv + w2 * w2)
            ur, ui = flux(zr - east(zr), zi - east(zi), gu, gu * r2u, w2)
            vr, vi = flux(zr - (ern - qrn), zi - (ein - qin), gv, gv * r2v, w2)
            uwr, uwi = rolled(ur, 1, 1), rolled(ui, 1, 1)
            vsr = jnp.concatenate([last_v[2 * c], vr[:-1]], axis=0)
            vsi = jnp.concatenate([last_v[2 * c + 1], vi[:-1]], axis=0)
            last_v[2 * c], last_v[2 * c + 1] = vr[-1:], vi[-1:]
            e1[c, 0, at : at + size, :] = md * (er + wt * ei - (ur - uwr) - (vr - vsr))
            e1[c, 1, at : at + size, :] = md * (ei - wt * er - (ui - uwi) - (vi - vsi))
            su = (ur + uwr) * (ur + uwr) + (ui + uwi) * (ui + uwi)
            sv = (vr + vsr) * (vr + vsr) + (vi + vsi) * (vi + vsi)
            sum_u = su if sum_u is None else sum_u + su
            sum_v = sv if sum_v is None else sum_v + sv
        inv = recip(dd)
        ia = recip(THETA * ax)
        total = (0.125 * ia * ia) * sum_u + (0.125 / (THETA * AY) ** 2) * sum_v
        var[at : at + size, :] = total * (inv * inv)
    half = rows // 2
    core = lax.rem(lax.axis_index("cons"), 2)
    send[:half, :] = var[pl.ds(pl.multiple_of((1 - core) * half, 8), half), :]
    keep[:half, :] = var[pl.ds(pl.multiple_of(core * half, 8), half), :]
    send[half:, :] = keep[half - 8 : half, :]
    keep[half:, :] = send[half - 8 : half, :]


def first_sweep(e, q, d, m, r, after):
    kdev, _, rows, width = e.shape
    half = pltpu.VMEM((rows // 2 + 8, width), F32)
    return pl.pallas_call(
        first_kernel,
        out_shape=(pltpu.VMEM(e.shape, F32), half, half, pltpu.VMEM((2, *d.shape), F32)),
        in_specs=[pl.BlockSpec(memory_space=pltpu.VMEM)] * 6,
        out_specs=[pl.BlockSpec(memory_space=pltpu.VMEM)] * 4,
        scratch_shapes=[pltpu.VMEM(d.shape, F32)],
        compiler_params=PARAMS,
        cost_estimate=pl.CostEstimate(flops=80 * e.size, bytes_accessed=160 * e.size, transcendentals=0),
        name="first_sweep",
    )(*map(vmem, (e, q, d, m, r, after)))


def add_kernel(a, b, *refs):
    refs[-1][...] = a[...] + b[...]


def added(a, b, *after):
    return pl.pallas_call(
        add_kernel,
        out_shape=pltpu.VMEM(a.shape, F32),
        in_specs=[pl.BlockSpec(memory_space=pltpu.VMEM)] * (2 + len(after)),
        out_specs=pl.BlockSpec(memory_space=pltpu.VMEM),
        compiler_params=PARAMS,
        name="added",
    )(vmem(a), vmem(b), *map(vmem, after))


def cut_kernel(a, b, after, *outs):
    del after
    at = 0
    for out in outs:
        here = slice(at, at + out.shape[0])
        out[...] = a[here, :] + b[here, :]
        at += out.shape[0]


def cut_sum(a, b, after):
    rows, width = a.shape
    large = pltpu.VMEM(((rows - 16) // 2, width), F32)
    return pl.pallas_call(
        cut_kernel,
        out_shape=(large, large, pltpu.VMEM((16, width), F32)),
        in_specs=[pl.BlockSpec(memory_space=pltpu.VMEM)] * 3,
        out_specs=[pl.BlockSpec(memory_space=pltpu.VMEM)] * 3,
        compiler_params=PARAMS,
        name="cut_sum",
    )(vmem(a), vmem(b), vmem(after))


def tree_sum(terms):
    while len(terms) > 1:
        terms = [a + b for a, b in zip(terms[::2], terms[1::2])]
    return terms[0]


def early_kernel(after, *refs):
    del after
    pieces, partner, outs = refs[:2], refs[2:4], refs[4:]
    thin = outs[0].shape[0]
    for k, out in enumerate(outs):
        part, at = divmod(k * thin, pieces[0].shape[0])
        out[...] = pieces[part][at : at + thin, :] + partner[part][at : at + thin, :]


def early_sums(pieces, partner, after):
    rows, width = pieces[0].shape
    count = 2 * rows // 16
    return pl.pallas_call(
        early_kernel,
        out_shape=(pltpu.VMEM((16, width), F32),) * count,
        in_specs=[pl.BlockSpec(memory_space=pltpu.VMEM)] * 5,
        out_specs=[pl.BlockSpec(memory_space=pltpu.VMEM)] * count,
        compiler_params=PARAMS,
        name="early_sums",
    )(*map(vmem, (after, *pieces, *partner)))


def join_kernel(tail, partner, both, after, *refs):
    del after
    *others, late, rims = refs
    late[...] = tail[:16, :] + partner[:16, :]
    terms = [x[...] for x in others]
    rims[...] = tree_sum([both[...], partner[16:, :] + terms[0], *[a + b for a, b in zip(terms[1::2], terms[2::2])]])


def joined(*args):
    width = args[0].shape[1]
    return pl.pallas_call(
        join_kernel,
        out_shape=(pltpu.VMEM((16, width), F32), pltpu.VMEM((8, width), F32)),
        in_specs=[pl.BlockSpec(memory_space=pltpu.VMEM)] * len(args),
        out_specs=[pl.BlockSpec(memory_space=pltpu.VMEM)] * 2,
        compiler_params=PARAMS,
        name="joined",
    )(*map(vmem, args))


def roles(a, b):
    even = lax.rem(lax.axis_index("tx"), 2) == 0
    return jnp.where(even, b, a), jnp.where(even, a, b)


def padded(x, pad):
    return jnp.concatenate([x, jnp.zeros((x.shape[0], pad - x.shape[1]), F32)], axis=1)


def merge_kernel(rows, f2, f1, mn, ms, send, mn_out, ms_out, my_out, send_out):
    width = mn.shape[1] - LANES
    fw, fe = roles(f1[...], padded(f2[...], f1.shape[1]))
    lane = lax.broadcasted_iota(jnp.int32, (MSG, LANES), 1)
    last = LANES - 1

    def ends(at):
        east_, west = fe[:, at // LANES * LANES :][:, :LANES], fw[:, at // LANES * LANES :][:, :LANES]
        east_, west = rolled(east_, -(at % LANES), 1), rolled(west, last - at % LANES, 1)
        return jnp.where(lane == 0, east_, jnp.where(lane == last, west, 0.0))

    mn_out[:, :width] = mn[:, :width]
    ms_out[:, :width] = ms[:, :width]
    mn_out[:, width:] = ends(rows - 1)
    ms_out[:, width:] = ends(0)
    low = lax.axis_index("ty") == 0
    my_out[...] = jnp.where(low, mn_out[...], ms_out[...])
    send_out[...] = send[...]


def merge(rows, f1, f2, mn, ms, send):
    out = pltpu.VMEM(mn.shape, F32)
    return pl.pallas_call(
        functools.partial(merge_kernel, rows),
        out_shape=(out, out, out, pltpu.VMEM(send.shape, F32)),
        in_specs=[pl.BlockSpec(memory_space=pltpu.VMEM)] * 5,
        out_specs=[pl.BlockSpec(memory_space=pltpu.VMEM)] * 4,
        compiler_params=PARAMS,
        name="merge",
    )(*map(vmem, (f2, f1, mn, ms, send)))


def strip_omega(shape, ws):
    odd = lax.rem(lax.broadcasted_iota(jnp.int32, shape, 0), 2)
    return jnp.where(odd == 0, ws[0], ws[1])


def strip_sweep(low, high, ws, g_across, g_along):
    none = jnp.zeros((2, low.shape[1]), F32)

    def field(at):
        return jnp.concatenate([none, low[at : at + 2], high[at : at + 2], none], axis=0)

    def single(at):
        a, b = low[at : at + 1], high[at : at + 1]
        return jnp.concatenate([none, a, a, b, b, none], axis=0)

    def given(at):
        return jnp.concatenate([low[at : at + 2], none, high[at : at + 2], none], axis=0)

    zr, zi, er, ei = field(0), field(2), field(8), field(10)
    r, d, m = single(12), single(13), single(14)
    w = strip_omega(zr.shape, ws)
    w2 = 2.0 * w
    wt = THETA * w
    up = lambda x: rolled(x, -2, 0)
    nx = lambda x: rolled(x, -1, 1)
    coef_a = (THETA * g_across * g_across) * (m * up(m) * (d + up(d)))
    coef_l = (THETA * g_along * g_along) * (m * nx(m) * (d + nx(d)))
    ar, ai = face(zr, zi, up(zr), up(zi), r + up(r), coef_a, w2)
    middle = lax.broadcasted_iota(jnp.int32, zr.shape, 0) // 2 == 1
    ar, ai = jnp.where(middle, ar, given(4)), jnp.where(middle, ai, given(6))
    lr, li = face(zr, zi, nx(zr), nx(zi), r + nx(r), coef_l, w2)
    abr, abi = rolled(ar, 2, 0), rolled(ai, 2, 0)
    lbr, lbi = rolled(lr, 1, 1), rolled(li, 1, 1)
    e1r = m * (er + wt * ei - (ar - abr) - (lr - lbr))
    e1i = m * (ei - wt * er - (ai - abi) - (li - lbi))
    sa = (ar + abr) * (ar + abr) + (ai + abi) * (ai + abi)
    sl = (lr + lbr) * (lr + lbr) + (li + lbi) * (li + lbi)
    inv = recip(jnp.maximum(d, TINY_DEPTH))
    ia = recip(THETA * g_across)
    il = recip(THETA * g_along)
    var = 0.125 * (ia * ia * sa + il * il * sl) * (inv * inv)
    var = var + rolled(var, -1, 0)
    z1r = e1r - (er - zr)
    z1i = e1i - (ei - zi)
    return (z1r, z1i, d, coef_a, e1r, e1i), var


def strip_lines(rows, m2, m1, f2, f1, mn, ms, fn_ref, fs_ref):
    width = mn.shape[1] - LANES
    pad = m1.shape[1]
    ty, count = lax.axis_index("ty"), lax.axis_size("ty")
    fn = jnp.where(ty < count - 1, fn_ref[...], 0.0)
    fs = jnp.where(ty > 0, fs_ref[...], 0.0)
    mw, me = roles(m1[...], padded(m2[...], pad))
    fw, fe = roles(f1[...], padded(f2[...], pad))
    hi = rows - (pad - LANES)
    last = LANES - 1
    lane = lax.broadcasted_iota(jnp.int32, (MSG, LANES), 1)

    def ended(msg, block, at):
        end = msg[:, pad - LANES :]
        end = jnp.where(lane == hi, rolled(fn[:, block : block + LANES], hi - at, 1), end)
        end = jnp.where(lane == last, rolled(fs[:, block : block + LANES], last - at, 1), end)
        return jnp.concatenate([msg[:, : pad - LANES], end], axis=1)

    low_w, high_w = ended(fw, width, last), ended(mw, 0, 0)
    low_e, high_e = ended(me, width - LANES, last), ended(fe, width, 0)
    return (fs, ms[...]), (mn[...], fn), (low_w, high_w), (low_e, high_e)


def line_metric(lines, rows, width):
    ax = metric((lines + lax.axis_index("ty") * rows).astype(F32), rows * lax.axis_size("ty"))
    return jnp.concatenate([ax] * (width // LANES), axis=1)


def column_metric(rows, pad):
    first = (lax.axis_index("ty") * rows).astype(F32)
    row = lax.broadcasted_iota(jnp.int32, (8, pad), 1).astype(F32) + first
    return metric(jnp.minimum(row, first + rows), rows * lax.axis_size("ty"))


def strips(rows, *refs):
    ws = omegas(2)
    line = lax.broadcasted_iota(jnp.int32, (8, LANES), 0) // 2
    south, north, west, east_ = strip_lines(rows, *refs)
    width, pad = south[0].shape[1], west[0].shape[1]
    out = [
        strip_sweep(*pair, ws, AY, line_metric(line + start, rows, width))
        for pair, start in ((south, -2), (north, rows - 2))
    ]
    ax = column_metric(rows, pad)
    return out + [strip_sweep(*pair, ws, ax, AY) for pair in (west, east_)]


def pair_variance(a, b, ws, g_across, g_along):
    sides = (*a, *b)

    def field(at):
        return jnp.concatenate([x[at : at + 2] for x in sides], axis=0)

    def single(at):
        return jnp.concatenate([x[at : at + 1] for x in sides for _ in range(2)], axis=0)

    zr, zi = field(0), field(2)
    r, d, m = single(12), single(13), single(14)
    w2 = 2.0 * strip_omega(zr.shape, ws)
    up = lambda x: rolled(x, -2, 0)
    nx = lambda x: rolled(x, -1, 1)
    coef_a = (THETA * g_across * g_across) * (m * up(m) * (d + up(d)))
    coef_l = (THETA * g_along * g_along) * (m * nx(m) * (d + nx(d)))
    inner = face(zr, zi, up(zr), up(zi), r + up(r), coef_a, w2)
    low_line = lax.rem(lax.broadcasted_iota(jnp.int32, zr.shape, 0) // 2, 2) == 0
    sa = sl = None
    along = face(zr, zi, nx(zr), nx(zi), r + nx(r), coef_l, w2)
    for p in range(2):
        outer = field(4 + 2 * p)
        both = jnp.where(low_line, inner[p], outer) + jnp.where(low_line, outer, rolled(inner[p], 2, 0))
        other = along[p] + rolled(along[p], 1, 1)
        sa = both * both if sa is None else sa + both * both
        sl = other * other if sl is None else sl + other * other
    inv = recip(jnp.maximum(d, TINY_DEPTH))
    ia = recip(THETA * g_across)
    il = recip(THETA * g_along)
    var = 0.125 * (ia * ia * sa + il * il * sl) * (inv * inv)
    return var + rolled(var, -1, 0)


def rim_kernel(rows, after, *refs):
    del after
    *refs, row_sums, col_sums = refs
    ws = omegas(2)
    south, north, west, east_ = strip_lines(rows, *refs)
    width, pad = row_sums.shape[1], west[0].shape[1]
    index = lax.broadcasted_iota(jnp.int32, (8, LANES), 0)
    line = lax.rem(index // 2, 2) - 1 + index // 4 * rows
    var = pair_variance(south, north, ws, AY, line_metric(line, rows, south[0].shape[1]))
    for k in range(4):
        row_sums[k, :] = var[2 * k, :width]
    var = pair_variance(west, east_, ws, column_metric(rows, pad), AY)
    for k in range(4):
        col_sums[k // 2, k % 2 * pad : (k % 2 + 1) * pad] = var[2 * k, :]
    col_sums[2:, :] = jnp.zeros((2, width), F32)


def strips_kernel(rows, *refs):
    for out, (held, _) in zip(refs[-4:], strips(rows, *refs[:-4])):
        for k, x in enumerate(held):
            out[8 * k : 8 * k + 8, :] = x


def rim(rows, late, *messages):
    width = late.shape[1]
    return pl.pallas_call(
        functools.partial(rim_kernel, rows),
        out_shape=(pltpu.VMEM((4, width), F32),) * 2,
        in_specs=[pl.BlockSpec(memory_space=pltpu.VMEM)] * 9,
        out_specs=[pl.BlockSpec(memory_space=pltpu.VMEM)] * 2,
        compiler_params=PARAMS,
        name="rim",
    )(*map(vmem, (late, *messages)))


def stack_kernel(a, b, out):
    out[: a.shape[0], :] = a[...]
    out[a.shape[0] :, :] = b[...]


def stacked(a, b):
    return pl.pallas_call(
        stack_kernel,
        out_shape=pltpu.VMEM((a.shape[0] + b.shape[0], a.shape[1]), F32),
        in_specs=[pl.BlockSpec(memory_space=pltpu.VMEM)] * 2,
        out_specs=pl.BlockSpec(memory_space=pltpu.VMEM),
        compiler_params=PARAMS,
        name="stacked",
    )(vmem(a), vmem(b))


def held_strips(rows, *messages):
    row = pltpu.VMEM((48, messages[4].shape[1]), F32)
    col = pltpu.VMEM((48, messages[1].shape[1]), F32)
    return pl.pallas_call(
        functools.partial(strips_kernel, rows),
        out_shape=(row, row, col, col),
        in_specs=[pl.BlockSpec(memory_space=pltpu.VMEM)] * 8,
        out_specs=[pl.BlockSpec(memory_space=pltpu.VMEM)] * 4,
        compiler_params=PARAMS,
        name="held_strips",
    )(*map(vmem, messages))


def prepare_kernel(e1_in, q, m, ss, sn, sw, se, du, dv, base, e1, cols):
    kdev, _, rows, width = e1_in.shape
    size = 24
    ws = omegas(kdev)
    e1[...] = e1_in[...]
    for p in range(2):
        cols[2 * p : 2 * p + 2, :] = sw[8 * (4 + p) + 4 : 8 * (4 + p) + 6, :]
        cols[4 + 2 * p : 6 + 2 * p, :] = se[8 * (4 + p) + 2 : 8 * (4 + p) + 4, :]
    turned = cols[...].T
    lane = lax.broadcasted_iota(jnp.int32, (rows, LANES), 1)
    left, right = slice(0, LANES), slice(width - LANES, width)
    last = LANES - 1
    for p in range(2):
        for c in range(kdev):
            e1[c, p, 0:1, :] = ss[8 * (4 + p) + 4 + c : 8 * (4 + p) + 5 + c, :width]
            e1[c, p, rows - 1 : rows, :] = sn[8 * (4 + p) + 2 + c : 8 * (4 + p) + 3 + c, :width]
            k = 2 * p + c
            e1[c, p, :, left] = jnp.where(lane == 0, rolled(turned[:rows], -k, 1), e1[c, p, :, left])
            k = 4 + 2 * p + c
            e1[c, p, :, right] = jnp.where(lane == last, rolled(turned[:rows], last - k, 1), e1[c, p, :, right])
    for at in range(0, rows, size):
        nxt = min(at + size, rows - 8)
        here = slice(at, at + size)
        md = m[here, :]
        for c in range(kdev):
            wt = THETA * ws[c]
            er, ern = tile_rows(e1.at[c, 0], at, size, nxt)
            ei, ein = tile_rows(e1.at[c, 1], at, size, nxt)
            qr, qrn = tile_rows(q.at[c, 0], at, size, nxt)
            qi, qin = tile_rows(q.at[c, 1], at, size, nxt)
            zr, zi = er - qr, ei - qi
            du[c, 0, here, :] = zr - east(zr)
            du[c, 1, here, :] = zi - east(zi)
            dv[c, 0, here, :] = zr - (ern - qrn)
            dv[c, 1, here, :] = zi - (ein - qin)
            base[c, 0, here, :] = md * (er + wt * ei)
            base[c, 1, here, :] = md * (ei - wt * er)


def prepare(e1, q, m, ss, sn, sw, se):
    plane = pltpu.VMEM(e1.shape, F32)
    return pl.pallas_call(
        prepare_kernel,
        out_shape=(plane, plane, plane),
        in_specs=[pl.BlockSpec(memory_space=pltpu.VMEM)] * 7,
        out_specs=[pl.BlockSpec(memory_space=pltpu.VMEM)] * 3,
        scratch_shapes=[pltpu.VMEM(e1.shape, F32), pltpu.VMEM((LANES, sw.shape[1]), F32)],
        compiler_params=PARAMS,
        cost_estimate=pl.CostEstimate(flops=40 * e1.size, bytes_accessed=160 * e1.size, transcendentals=0),
        name="prepare",
    )(*map(vmem, (e1, q, m, ss, sn, sw, se)))


def rate(var, d):
    s = var + BACKGROUND
    return (DRAG * (s * lax.rsqrt(s))) * recip(d)


def sweep_tile(row, size, r, r_north, du, dv, base, coef, m, turned, ws, last_v, top):
    kdev, width = du.shape[0], du.shape[3]
    here = pl.ds(row, size)
    edges = turned[here, :]
    md = m[here, :]
    coef_u, coef_v = coef[0, here, :], coef[1, here, :]
    r2u = r + east(r)
    r2v = r + r_north
    squ, sqv = r2u * r2u, r2v * r2v
    lane = lax.broadcasted_iota(jnp.int32, (size, LANES), 1)
    last = LANES - 1

    def with_east(u, k):
        block = jnp.where(lane == last, rolled(edges, last - k, 1), u[:, width - LANES :])
        return jnp.concatenate([u[:, : width - LANES], block], axis=1)

    def from_west(u, k):
        u = rolled(u, 1, 1)
        block = jnp.where(lane == 0, rolled(edges, -k, 1), u[:, :LANES])
        return jnp.concatenate([block, u[:, LANES:]], axis=1)

    planes, out_v = {}, {}
    for c in range(kdev):
        w2 = 2.0 * ws[c]
        gu = coef_u * recip(squ + w2 * w2)
        gv = coef_v * recip(sqv + w2 * w2)
        u = flux(du[c, 0, here, :], du[c, 1, here, :], gu, gu * r2u, w2)
        v = flux(dv[c, 0, here, :], dv[c, 1, here, :], gv, gv * r2v, w2)
        for p in range(2):
            up, vp = with_east(u[p], 4 + 2 * p + c), v[p]
            if top is not None:
                vp = jnp.concatenate([vp[:-1], top(c, p, vp[-1:])], axis=0)
            uw = from_west(up, 2 * p + c)
            vs = jnp.concatenate([last_v[c, p], vp[:-1]], axis=0)
            out_v[c, p] = vp[-1:]
            planes[c, p] = base[c, p, here, :], md * ((up - uw) + (vp - vs))
    return planes, out_v


def pairs(kdev):
    return [(c, p) for c in range(kdev) for p in range(2)]


def half_rate(var, rims, turned, d, row, low, half):
    here = pl.ds(row, half)
    edges = turned[here, :]
    width = var.shape[1]
    index = lax.broadcasted_iota(jnp.int32, (8, width), 0)
    first = jnp.where(low & (index == 0), rims[1:2], var[:8])
    final = jnp.where(jnp.logical_not(low) & (index == 7), rims[2:3], var[half - 8 :])
    var = jnp.concatenate([first, var[8 : half - 8], final], axis=0)
    lane = lax.broadcasted_iota(jnp.int32, (half, LANES), 1)
    left = jnp.where(lane == 0, rolled(edges, -8, 1), var[:, :LANES])
    right = jnp.where(lane == LANES - 1, rolled(edges, LANES - 1 - 9, 1), var[:, width - LANES :])
    return rate(jnp.concatenate([left, var[:, LANES : width - LANES], right], axis=1), d[here, :])


def own_kernel(du, dv, base, coef, d, m, late, rims_ref, ss, sn, sw, se, *refs):
    *mine, first_part, update, fric, vs_out, vn_out, turned, cols = refs
    kdev, _, half, width = update.shape
    pad = sw.shape[1]
    ws = omegas(kdev)
    core = lax.rem(lax.axis_index("cons"), 2)
    low = core == 0
    rims = rims_ref[...]

    def edge(strip, var_a, var_b):
        zr, zi, dep, ca = (strip[8 * k : 8 * k + 8, :] for k in range(4))
        var = jnp.concatenate([var_a, var_a, var_a, var_a, var_b, var_b, var_b, var_b], axis=0)
        f = rate(var, jnp.maximum(dep, TINY_DEPTH))
        up = lambda x: rolled(x, -2, 0)
        w2 = 2.0 * strip_omega(zr.shape, ws)
        return face(zr, zi, up(zr), up(zi), f + up(f), ca, w2)

    none = jnp.zeros((1, LANES), F32)
    wide = lambda x: jnp.concatenate([x, none], axis=1)
    south = edge(ss, wide(rims[0:1]), wide(rims[1:2]))
    north = edge(sn, wide(rims[2:3]), wide(rims[3:4]))
    west = edge(sw, rims[4:5, :pad], rims[4:5, pad : 2 * pad])
    east_ = edge(se, rims[5:6, :pad], rims[5:6, pad : 2 * pad])
    for p in range(2):
        cols[2 * p : 2 * p + 2, :] = west[p][2:4]
        cols[4 + 2 * p : 6 + 2 * p, :] = east_[p][2:4]
        for c in range(kdev):
            vs_out[2 * c + p : 2 * c + p + 1, :] = south[p][2 + c : 3 + c, :width]
            vn_out[2 * c + p : 2 * c + p + 1, :] = north[p][2 + c : 3 + c, :width]
    cols[8:9, :] = rims[4:5, pad : 2 * pad]
    cols[9:10, :] = rims[5:6, :pad]
    turned[...] = cols[...].T

    first = pl.multiple_of(core * half, 8)
    var = jnp.concatenate([x[...] for x in mine] + [late[:8, :]], axis=0)
    fric[...] = half_rate(var, rims, turned, d, first, low, half)
    size = 24
    last_v = {(c, p): jnp.where(low, vs_out[2 * c + p : 2 * c + p + 1, :], 0.0) for c, p in pairs(kdev)}

    def top(c, p, own):
        return jnp.where(low, 0.0, vn_out[2 * c + p : 2 * c + p + 1, :])

    for at in range(0, half, size):
        r, rn = tile_rows(fric, at, size, min(at + size, half - 8))
        planes, last_v = sweep_tile(
            pl.multiple_of(first + at, 8), size, r, rn, du, dv, base, coef, m, turned, ws, last_v,
            top if at + size == half else None,
        )
        for c, p in pairs(kdev):
            first_part[c, p, at : at + size, :], update[c, p, at : at + size, :] = planes[c, p]


def own_half(*args):
    kdev, _, rows, width = args[0].shape
    pad = args[10].shape[1]
    line = pltpu.VMEM((8, width), F32)
    return pl.pallas_call(
        own_kernel,
        out_shape=(
            pltpu.VMEM((kdev, 2, rows // 2, width), F32),
            pltpu.VMEM((kdev, 2, rows // 2, width), F32),
            pltpu.VMEM((rows // 2, width), F32),
            line,
            line,
            pltpu.VMEM((pad, LANES), F32),
        ),
        in_specs=[pl.BlockSpec(memory_space=pltpu.VMEM)] * len(args),
        out_specs=[pl.BlockSpec(memory_space=pltpu.VMEM)] * 6,
        scratch_shapes=[pltpu.VMEM((LANES, pad), F32)],
        compiler_params=PARAMS,
        name="own_half",
    )(*map(vmem, args))


def other_kernel(du, dv, base, coef, d, m, late, rims, eta_own, fric_own, vs, vn, turned, *refs):
    *other, eta_out, fric_out, eta, fric, fixed, sems = refs
    kdev, _, half, width = eta.shape
    ws = omegas(kdev)
    core = lax.rem(lax.axis_index("cons"), 2)
    own_low = core == 0
    own, first = pl.multiple_of(core * half, 8), pl.multiple_of((1 - core) * half, 8)
    copies = []

    def put(src, dst):
        copy = pltpu.make_async_copy(src, dst, sems.at[len(copies)])
        copy.start()
        copies.append(copy)

    skip = pl.multiple_of(core * 8, 8)
    put(
        eta_own.at[:, :, pl.ds(skip, half - 8), :],
        eta_out.at[:, :, pl.ds(pl.multiple_of(own + skip, 8), half - 8), :],
    )
    put(fric_own, fric_out.at[pl.ds(own, half), :])
    fric[pl.ds(own, half), :] = fric_own[...]
    fric[pl.ds(first, half), :] = half_rate(
        jnp.concatenate([x[...] for x in other] + [late[8:, :]], axis=0),
        rims[...], turned, d, first, jnp.logical_not(own_low), half,
    )
    put(fric.at[pl.ds(first, half), :], fric_out.at[pl.ds(first, half), :])

    r, rn = tile_rows(fric, half - 8, 8, half)
    r2 = r + rn
    between = {}
    for c in range(kdev):
        w2 = 2.0 * ws[c]
        g = coef[1, half - 8 : half, :] * recip(r2 * r2 + w2 * w2)
        v = flux(dv[c, 0, half - 8 : half, :], dv[c, 1, half - 8 : half, :], g, g * r2, w2)
        for p in range(2):
            between[c, p] = v[p][7:8]
    index = lax.broadcasted_iota(jnp.int32, (8, width), 0)
    at_face = index == jnp.where(own_low, 7, 0)
    sign = jnp.where(own_low, -1.0, 1.0)
    local = pl.ds(pl.multiple_of((1 - core) * (half - 8), 8), 8)
    border = pl.ds(pl.multiple_of(half - 8 + 8 * core, 8), 8)
    md = m[border, :]
    for c, p in pairs(kdev):
        fixed[c, p] = eta_own[c, p, local, :] + jnp.where(at_face, sign * (md * between[c, p]), 0.0)
    put(fixed, eta_out.at[:, :, border, :])

    size = 24
    rows = 2 * half
    last_v = {(c, p): jnp.where(own_low, between[c, p], vs[2 * c + p : 2 * c + p + 1, :]) for c, p in pairs(kdev)}

    def top(c, p, own_v):
        return jnp.where(own_low, vn[2 * c + p : 2 * c + p + 1, :], own_v)

    for at in range(0, half, size):
        row = pl.multiple_of(first + at, 8)
        r = fric[pl.ds(row, size), :]
        after = fric[pl.ds(pl.multiple_of(jnp.minimum(row + size, rows - 8), 8), 8), :]
        rn = jnp.concatenate([r[1:], after[0:1]], axis=0)
        planes, last_v = sweep_tile(
            row, size, r, rn, du, dv, base, coef, m, turned, ws, last_v, top if at + size == half else None
        )
        for c, p in pairs(kdev):
            eta[c, p, at : at + size, :] = planes[c, p][0] - planes[c, p][1]
        put(eta.at[:, :, at : at + size, :], eta_out.at[:, :, pl.ds(row, size), :])
    for copy in copies:
        copy.wait()


def other_half(*args):
    du, d = args[0], args[4]
    kdev, _, rows, width = du.shape
    return pl.pallas_call(
        other_kernel,
        out_shape=(jax.ShapeDtypeStruct(du.shape, F32), jax.ShapeDtypeStruct(d.shape, F32)),
        in_specs=[pl.BlockSpec(memory_space=pltpu.VMEM)] * len(args),
        out_specs=[pl.BlockSpec(memory_space=pltpu.HBM)] * 2,
        scratch_shapes=[
            pltpu.VMEM((kdev, 2, rows // 2, width), F32),
            pltpu.VMEM(d.shape, F32),
            pltpu.VMEM((kdev, 2, 8, width), F32),
            pltpu.SemaphoreType.DMA((4 + rows // 2 // 24,)),
        ],
        compiler_params=PARAMS,
        name="other_half",
    )(*map(vmem, args))


def swapped(x, axis, bit):
    return lax.ppermute(x, axis, [(i, i ^ bit) for i in range(lax.axis_size(axis))])


def body(elevation, equilibrium, depth, land_mask, friction_prev):
    rows = depth.shape[0]
    ntx, nty, ncons = (lax.axis_size(a) for a in ("tx", "ty", "cons"))
    fields = (elevation, equilibrium, depth, land_mask, friction_prev)
    m2, m1 = pack_columns(*fields)
    elev, equil, depth, mask, fric = elevation, equilibrium, depth, land_mask, friction_prev
    mask, mn, ms = pack(*fields, m1)
    f2 = lax.ppermute(m2, "tx", [(i, (i - 1 if i % 2 == 0 else i + 1) % ntx) for i in range(ntx)])
    f1 = swapped(m1, "tx", 1)
    e1, send, keep, coef = first_sweep(elev, equil, depth, mask, fric, m1)
    mn, ms, my, send = merge(rows, f1, f2, mn, ms, send)
    recv = swapped(send, "cons", 1)
    if nty == 2:
        fn = fs = swapped(my, "ty", 1)
    else:
        fn = lax.ppermute(ms, "ty", [(i, i - 1) for i in range(1, nty)])
        fs = lax.ppermute(mn, "ty", [(i, i + 1) for i in range(nty - 1)])
    first, second, late = cut_sum(recv, keep, my)
    messages = (m2, m1, f2, f1, mn, ms, fn, fs)
    rims = jnp.concatenate(rim(rows, late, *messages), axis=0)
    tail = stacked(late, rims)
    ss, sn, sw, se = held_strips(rows, *messages)
    prepared = prepare(e1, equil, mask, ss, sn, sw, se)
    partner = [swapped(x, "cons", 2) for x in (first, second, tail)]
    others = [swapped(rims, "cons", k) for k in range(1, ncons) if k != 2]
    both = added(rims, others[0], prepared[2])
    mine = early_sums((first, second), partner[:2], both)
    bit = 4
    while bit < ncons:
        mine = [added(x, swapped(x, "cons", bit)) for x in mine]
        tail, partner[2] = added(tail, partner[2]), swapped(added(tail, partner[2]), "cons", bit)
        bit *= 2
    other = [swapped(x, "cons", 1) for x in mine]
    late, rims = joined(tail, partner[2], both, other[0], *others[1:])
    fields = (*prepared, coef, depth, mask, late, rims)
    first_part, update, *own = own_half(*fields, ss, sn, sw, se, *mine)
    return other_half(*fields, first_part - update, *own, *other)


def solution(mesh):
    return jax.shard_map(
        body,
        mesh=mesh,
        in_specs=(
            P("cons", None, "ty", "tx"),
            P("cons", None, "ty", "tx"),
            P("ty", "tx"),
            P("ty", "tx"),
            P("ty", "tx"),
        ),
        out_specs=(P("cons", None, "ty", "tx"), P("ty", "tx")),
        check_vma=False,
    )
```

```python
import functools
import math

import jax
import jax.numpy as jnp
from jax import lax
from jax.experimental import pallas as pl
from jax.experimental.pallas import tpu as pltpu
from jax.sharding import PartitionSpec as P

OMEGA_TABLE = (1.0, 1.0351, 0.9582, 1.0379, 0.5181, 0.4816, 0.5164, 0.4454)
AY = 0.5
THETA = 0.05
DRAG = 0.5
BACKGROUND = 0.01
F32 = jnp.float32
LANES = 128
MSG = 16
TINY_DEPTH = 1e-6
PARAMS = pltpu.CompilerParams(vmem_limit_bytes=16 * 1024 * 1024)


def vmem(x):
    return pltpu.with_memory_space_constraint(x, pltpu.VMEM)


def hbm(x):
    return pltpu.with_memory_space_constraint(x, pltpu.HBM)


def recip(x):
    return pl.reciprocal(x, approx=True) if jnp.ndim(x) else 1.0 / x


def metric(rows, total):
    lat = (rows + 0.5) * (120.0 / total * math.pi / 180.0) - math.pi / 3.0
    s = lat * lat
    acc = jnp.full_like(s, 1.0 / math.factorial(16))
    for n in (14, 12, 10, 8, 6, 4, 2, 0):
        acc = ((-1.0) ** (n // 2)) / math.factorial(n) + s * acc
    return 0.5 / acc


def omegas(kdev):
    index = lax.axis_index("cons")
    out = []
    for c in range(kdev):
        w = jnp.float32(OMEGA_TABLE[c])
        for i in range(1, len(OMEGA_TABLE) // kdev):
            w = jnp.where(index == i, jnp.float32(OMEGA_TABLE[i * kdev + c]), w)
        out.append(w)
    return out


def rolled(x, shift, axis):
    return pltpu.roll(x, shift % x.shape[axis], axis)


def face(zr, zi, zr_next, zi_next, r2, coef, w2):
    g = coef * recip(r2 * r2 + w2 * w2)
    a = g * r2
    b = g * w2
    dr = zr - zr_next
    di = zi - zi_next
    return a * dr + b * di, a * di - b * dr


def flux(dr, di, g, a, w2):
    b = g * w2
    return a * dr + b * di, a * di - b * dr


def pack_columns_kernel(e_in, q_in, d_in, m_in, r_in, m2, m1, e, q, d, m, r, turned, behind, sems):
    rows, width = d_in.shape
    copies = []
    for s, side in enumerate((slice(0, LANES), slice(width - LANES, width))):
        for src, dst in ((e_in, e), (q_in, q)):
            copies.append((src.at[:, :, :, side], dst.at[s]))
        for src, dst in ((d_in, d), (m_in, m), (r_in, r)):
            copies.append((src.at[:, side], dst.at[s]))
    copies = [pltpu.make_async_copy(src, dst, sems.at[k]) for k, (src, dst) in enumerate(copies)]
    for copy in copies:
        copy.start()
    for copy in copies:
        copy.wait()
    lane = lax.broadcasted_iota(jnp.int32, (rows, LANES), 1)

    def edges(plane):
        return jnp.where(lane < LANES // 2, plane(0), plane(1))

    elev = [edges(lambda s: e[s, c, p]) for p in range(2) for c in range(2)]
    equil = [edges(lambda s: q[s, c, p]) for p in range(2) for c in range(2)]
    planes = [x - y for x, y in zip(elev, equil)]
    planes += [edges(lambda s: r[s]), edges(lambda s: d[s]), edges(lambda s: m[s]).astype(F32)]
    both = jnp.zeros((rows, LANES), F32)
    for k, plane in enumerate(planes + elev):
        both = jnp.where((lane >= 4 * k) & (lane < 4 * k + 4), rolled(plane, 4 * k + 2, 1), both)
    pad = turned.shape[1]
    turned[...] = jnp.concatenate([both, jnp.zeros((pad - rows, LANES), F32)], axis=0).T
    odd = lax.rem(lax.axis_index("tx"), 2)
    first = (lax.axis_index("ty") * rows).astype(F32)
    lat_row = jnp.minimum(lax.broadcasted_iota(jnp.int32, (8, pad), 1), rows).astype(F32) + first
    ax = metric(lat_row, rows * lax.axis_size("ty"))
    w0, w1 = omegas(2)
    w2 = 2.0 * jnp.where(lax.broadcasted_iota(jnp.int32, (8, pad), 0) < 4, w0, w1)
    up = lambda x: rolled(x, -1, 0)
    zr, zi = turned[0:8, :], turned[8:16, :]
    r8, d8, m8 = (jnp.concatenate([turned[at : at + 4, :]] * 2, axis=0) for at in (16, 20, 24))
    coef = (THETA * ax * ax) * (m8 * up(m8) * (d8 + up(d8)))
    behind[0:8, :], behind[8:16, :] = face(zr, zi, up(zr), up(zi), r8 + up(r8), coef, w2)
    for out, west in ((m1, odd), (m2, 1 - odd)):
        lanes = slice(0, out.shape[1])
        for k in range(4):
            out[k : k + 1, :] = turned[pl.ds(4 * k + 1 + west, 1), lanes]
            out[4 + k : 5 + k, :] = behind[pl.ds(4 * k + 2 * west, 1), lanes]
            out[8 + k : 9 + k, :] = turned[pl.ds(4 * (7 + k) + 1 + west, 1), lanes]
        for k in range(3):
            out[12 + k : 13 + k, :] = turned[pl.ds(4 * (4 + k) + 1 + west, 1), lanes]
        out[MSG - 1 :, :] = jnp.zeros((1, out.shape[1]), F32)


def pack_columns(elevation, equilibrium, depth, land_mask, friction):
    kdev, _, rows, width = elevation.shape
    pad = -(-rows // LANES) * LANES
    cut, plane = pltpu.VMEM((2, kdev, 2, rows, LANES), F32), pltpu.VMEM((2, rows, LANES), F32)
    return pl.pallas_call(
        pack_columns_kernel,
        out_shape=(pltpu.VMEM((MSG, rows), F32), pltpu.VMEM((MSG, pad), F32)),
        in_specs=[pl.BlockSpec(memory_space=pltpu.HBM)] * 5,
        out_specs=[pl.BlockSpec(memory_space=pltpu.VMEM)] * 2,
        scratch_shapes=[
            cut,
            cut,
            plane,
            pltpu.VMEM((2, rows, LANES), jnp.int32),
            plane,
            pltpu.VMEM((LANES, pad), F32),
            pltpu.VMEM((16, pad), F32),
            pltpu.SemaphoreType.DMA((10,)),
        ],
        compiler_params=PARAMS,
        name="pack_columns",
    )(*map(hbm, (elevation, equilibrium, depth, land_mask, friction)))


def pack_kernel(e, q, d, ints, r, after, m, mn, ms):
    del after
    kdev, _, rows, width = e.shape
    m[...] = ints[...].astype(F32)
    ws = omegas(kdev)
    for out, end, near, low in ((ms, slice(0, 8), 0, 0), (mn, slice(rows - 8, rows), 7, 6)):
        out[:, width:] = jnp.zeros((MSG, LANES), F32)
        r8, d8, m8 = r[end, :], d[end, :], m[end, :]
        up = lambda x: rolled(x, -1, 0)
        coef = (THETA * AY * AY) * (m8 * up(m8) * (d8 + up(d8)))
        r2 = r8 + up(r8)
        for c in range(kdev):
            elev = [e[c, p, end, :] for p in range(2)]
            z = [elev[p] - q[c, p, end, :] for p in range(2)]
            v = face(z[0], z[1], up(z[0]), up(z[1]), r2, coef, 2.0 * ws[c])
            for p in range(2):
                out[2 * p + c, :width] = z[p][near, :]
                out[4 + 2 * p + c, :width] = v[p][low, :]
                out[8 + 2 * p + c, :width] = elev[p][near, :]
        for k, plane in enumerate((r8, d8, m8)):
            out[12 + k, :width] = plane[near, :]
        out[MSG - 1, :width] = jnp.zeros((width,), F32)


def pack(elevation, equilibrium, depth, land_mask, friction, after):
    kdev, _, rows, width = elevation.shape
    plane = pltpu.VMEM(depth.shape, F32)
    row = pltpu.VMEM((MSG, width + LANES), F32)
    return pl.pallas_call(
        pack_kernel,
        out_shape=(plane, row, row),
        in_specs=[pl.BlockSpec(memory_space=pltpu.VMEM)] * 6,
        out_specs=[pl.BlockSpec(memory_space=pltpu.VMEM)] * 3,
        compiler_params=PARAMS,
        name="pack",
    )(*map(vmem, (elevation, equilibrium, depth, land_mask, friction, after)))


def tile_rows(ref, at, size, nxt):
    here = ref[at : at + size, :]
    after = ref[nxt : nxt + 8, :]
    return here, jnp.concatenate([here[1:], after[0:1]], axis=0)


def east(x):
    return rolled(x, -1, 1)


def row_metric(at, size, width, rows):
    first = lax.axis_index("ty") * rows
    index = lax.broadcasted_iota(jnp.int32, (size, LANES), 0) + (first + at)
    ax = metric(index.astype(F32), rows * lax.axis_size("ty"))
    return ax, jnp.concatenate([ax] * (width // LANES), axis=1)


def first_kernel(e, q, d, mask, r, after, e1, send, keep, coef, var):
    del after
    kdev, _, rows, width = e.shape
    size = 24
    ws = omegas(kdev)
    last_v = [jnp.zeros((1, width), F32)] * (2 * kdev)
    for at in range(0, rows, size):
        nxt = min(at + size, rows - 8)
        _, ax = row_metric(at, size, width, rows)
        md, mn = tile_rows(mask, at, size, nxt)
        dd, dn = tile_rows(d, at, size, nxt)
        rd, rn = tile_rows(r, at, size, nxt)
        coef_u = (THETA * ax * ax) * (md * east(md) * (dd + east(dd)))
        coef_v = (THETA * AY * AY) * (md * mn * (dd + dn))
        coef[0, at : at + size, :], coef[1, at : at + size, :] = coef_u, coef_v
        r2u = rd + east(rd)
        r2v = rd + rn
        squ, sqv = r2u * r2u, r2v * r2v
        sum_u = sum_v = None
        for c in range(kdev):
            w2 = 2.0 * ws[c]
            wt = THETA * ws[c]
            er, ern = tile_rows(e.at[c, 0], at, size, nxt)
            ei, ein = tile_rows(e.at[c, 1], at, size, nxt)
            qr, qrn = tile_rows(q.at[c, 0], at, size, nxt)
            qi, qin = tile_rows(q.at[c, 1], at, size, nxt)
            zr, zi = er - qr, ei - qi
            gu = coef_u * recip(squ + w2 * w2)
            gv = coef_v * recip(sqv + w2 * w2)
            ur, ui = flux(zr - east(zr), zi - east(zi), gu, gu * r2u, w2)
            vr, vi = flux(zr - (ern - qrn), zi - (ein - qin), gv, gv * r2v, w2)
            uwr, uwi = rolled(ur, 1, 1), rolled(ui, 1, 1)
            vsr = jnp.concatenate([last_v[2 * c], vr[:-1]], axis=0)
            vsi = jnp.concatenate([last_v[2 * c + 1], vi[:-1]], axis=0)
            last_v[2 * c], last_v[2 * c + 1] = vr[-1:], vi[-1:]
            e1[c, 0, at : at + size, :] = md * (er + wt * ei - (ur - uwr) - (vr - vsr))
            e1[c, 1, at : at + size, :] = md * (ei - wt * er - (ui - uwi) - (vi - vsi))
            su = (ur + uwr) * (ur + uwr) + (ui + uwi) * (ui + uwi)
            sv = (vr + vsr) * (vr + vsr) + (vi + vsi) * (vi + vsi)
            sum_u = su if sum_u is None else sum_u + su
            sum_v = sv if sum_v is None else sum_v + sv
        inv = recip(dd)
        ia = recip(THETA * ax)
        total = (0.125 * ia * ia) * sum_u + (0.125 / (THETA * AY) ** 2) * sum_v
        var[at : at + size, :] = total * (inv * inv)
    half = rows // 2
    core = lax.rem(lax.axis_index("cons"), 2)
    send[:half, :] = var[pl.ds(pl.multiple_of((1 - core) * half, 8), half), :]
    keep[:half, :] = var[pl.ds(pl.multiple_of(core * half, 8), half), :]
    send[half:, :] = keep[half - 8 : half, :]
    keep[half:, :] = send[half - 8 : half, :]


def first_sweep(e, q, d, m, r, after):
    kdev, _, rows, width = e.shape
    half = pltpu.VMEM((rows // 2 + 8, width), F32)
    return pl.pallas_call(
        first_kernel,
        out_shape=(pltpu.VMEM(e.shape, F32), half, half, pltpu.VMEM((2, *d.shape), F32)),
        in_specs=[pl.BlockSpec(memory_space=pltpu.VMEM)] * 6,
        out_specs=[pl.BlockSpec(memory_space=pltpu.VMEM)] * 4,
        scratch_shapes=[pltpu.VMEM(d.shape, F32)],
        compiler_params=PARAMS,
        cost_estimate=pl.CostEstimate(flops=80 * e.size, bytes_accessed=160 * e.size, transcendentals=0),
        name="first_sweep",
    )(*map(vmem, (e, q, d, m, r, after)))


def add_kernel(a, b, *refs):
    refs[-1][...] = a[...] + b[...]


def added(a, b, *after):
    return pl.pallas_call(
        add_kernel,
        out_shape=pltpu.VMEM(a.shape, F32),
        in_specs=[pl.BlockSpec(memory_space=pltpu.VMEM)] * (2 + len(after)),
        out_specs=pl.BlockSpec(memory_space=pltpu.VMEM),
        compiler_params=PARAMS,
        name="added",
    )(vmem(a), vmem(b), *map(vmem, after))


def cut_kernel(a, b, after, *outs):
    del after
    at = 0
    for out in outs:
        here = slice(at, at + out.shape[0])
        out[...] = a[here, :] + b[here, :]
        at += out.shape[0]


def cut_sum(a, b, after):
    rows, width = a.shape
    large = pltpu.VMEM(((rows - 16) // 2, width), F32)
    return pl.pallas_call(
        cut_kernel,
        out_shape=(large, large, pltpu.VMEM((16, width), F32)),
        in_specs=[pl.BlockSpec(memory_space=pltpu.VMEM)] * 3,
        out_specs=[pl.BlockSpec(memory_space=pltpu.VMEM)] * 3,
        compiler_params=PARAMS,
        name="cut_sum",
    )(vmem(a), vmem(b), vmem(after))


def tree_sum(terms):
    while len(terms) > 1:
        terms = [a + b for a, b in zip(terms[::2], terms[1::2])]
    return terms[0]


def early_kernel(after, *refs):
    del after
    pieces, partner, outs = refs[:2], refs[2:4], refs[4:]
    thin = outs[0].shape[0]
    for k, out in enumerate(outs):
        part, at = divmod(k * thin, pieces[0].shape[0])
        out[...] = pieces[part][at : at + thin, :] + partner[part][at : at + thin, :]


def early_sums(pieces, partner, after):
    rows, width = pieces[0].shape
    count = 2 * rows // 16
    return pl.pallas_call(
        early_kernel,
        out_shape=(pltpu.VMEM((16, width), F32),) * count,
        in_specs=[pl.BlockSpec(memory_space=pltpu.VMEM)] * 5,
        out_specs=[pl.BlockSpec(memory_space=pltpu.VMEM)] * count,
        compiler_params=PARAMS,
        name="early_sums",
    )(*map(vmem, (after, *pieces, *partner)))


def join_kernel(tail, partner, both, after, *refs):
    del after
    *others, late, rims = refs
    late[...] = tail[:16, :] + partner[:16, :]
    terms = [x[...] for x in others]
    rims[...] = tree_sum([both[...], partner[16:, :] + terms[0], *[a + b for a, b in zip(terms[1::2], terms[2::2])]])


def joined(*args):
    width = args[0].shape[1]
    return pl.pallas_call(
        join_kernel,
        out_shape=(pltpu.VMEM((16, width), F32), pltpu.VMEM((8, width), F32)),
        in_specs=[pl.BlockSpec(memory_space=pltpu.VMEM)] * len(args),
        out_specs=[pl.BlockSpec(memory_space=pltpu.VMEM)] * 2,
        compiler_params=PARAMS,
        name="joined",
    )(*map(vmem, args))


def roles(a, b):
    even = lax.rem(lax.axis_index("tx"), 2) == 0
    return jnp.where(even, b, a), jnp.where(even, a, b)


def padded(x, pad):
    return jnp.concatenate([x, jnp.zeros((x.shape[0], pad - x.shape[1]), F32)], axis=1)


def merge_kernel(rows, f2, f1, mn, ms, send, mn_out, ms_out, my_out, send_out):
    width = mn.shape[1] - LANES
    fw, fe = roles(f1[...], padded(f2[...], f1.shape[1]))
    lane = lax.broadcasted_iota(jnp.int32, (MSG, LANES), 1)
    last = LANES - 1

    def ends(at):
        east_, west = fe[:, at // LANES * LANES :][:, :LANES], fw[:, at // LANES * LANES :][:, :LANES]
        east_, west = rolled(east_, -(at % LANES), 1), rolled(west, last - at % LANES, 1)
        return jnp.where(lane == 0, east_, jnp.where(lane == last, west, 0.0))

    mn_out[:, :width] = mn[:, :width]
    ms_out[:, :width] = ms[:, :width]
    mn_out[:, width:] = ends(rows - 1)
    ms_out[:, width:] = ends(0)
    low = lax.axis_index("ty") == 0
    my_out[...] = jnp.where(low, mn_out[...], ms_out[...])
    send_out[...] = send[...]


def merge(rows, f1, f2, mn, ms, send):
    out = pltpu.VMEM(mn.shape, F32)
    return pl.pallas_call(
        functools.partial(merge_kernel, rows),
        out_shape=(out, out, out, pltpu.VMEM(send.shape, F32)),
        in_specs=[pl.BlockSpec(memory_space=pltpu.VMEM)] * 5,
        out_specs=[pl.BlockSpec(memory_space=pltpu.VMEM)] * 4,
        compiler_params=PARAMS,
        name="merge",
    )(*map(vmem, (f2, f1, mn, ms, send)))


def strip_omega(shape, ws):
    odd = lax.rem(lax.broadcasted_iota(jnp.int32, shape, 0), 2)
    return jnp.where(odd == 0, ws[0], ws[1])


def strip_sweep(low, high, ws, g_across, g_along):
    none = jnp.zeros((2, low.shape[1]), F32)

    def field(at):
        return jnp.concatenate([none, low[at : at + 2], high[at : at + 2], none], axis=0)

    def single(at):
        a, b = low[at : at + 1], high[at : at + 1]
        return jnp.concatenate([none, a, a, b, b, none], axis=0)

    def given(at):
        return jnp.concatenate([low[at : at + 2], none, high[at : at + 2], none], axis=0)

    zr, zi, er, ei = field(0), field(2), field(8), field(10)
    r, d, m = single(12), single(13), single(14)
    w = strip_omega(zr.shape, ws)
    w2 = 2.0 * w
    wt = THETA * w
    up = lambda x: rolled(x, -2, 0)
    nx = lambda x: rolled(x, -1, 1)
    coef_a = (THETA * g_across * g_across) * (m * up(m) * (d + up(d)))
    coef_l = (THETA * g_along * g_along) * (m * nx(m) * (d + nx(d)))
    ar, ai = face(zr, zi, up(zr), up(zi), r + up(r), coef_a, w2)
    middle = lax.broadcasted_iota(jnp.int32, zr.shape, 0) // 2 == 1
    ar, ai = jnp.where(middle, ar, given(4)), jnp.where(middle, ai, given(6))
    lr, li = face(zr, zi, nx(zr), nx(zi), r + nx(r), coef_l, w2)
    abr, abi = rolled(ar, 2, 0), rolled(ai, 2, 0)
    lbr, lbi = rolled(lr, 1, 1), rolled(li, 1, 1)
    e1r = m * (er + wt * ei - (ar - abr) - (lr - lbr))
    e1i = m * (ei - wt * er - (ai - abi) - (li - lbi))
    sa = (ar + abr) * (ar + abr) + (ai + abi) * (ai + abi)
    sl = (lr + lbr) * (lr + lbr) + (li + lbi) * (li + lbi)
    inv = recip(jnp.maximum(d, TINY_DEPTH))
    ia = recip(THETA * g_across)
    il = recip(THETA * g_along)
    var = 0.125 * (ia * ia * sa + il * il * sl) * (inv * inv)
    var = var + rolled(var, -1, 0)
    z1r = e1r - (er - zr)
    z1i = e1i - (ei - zi)
    return (z1r, z1i, d, coef_a, e1r, e1i), var


def strip_lines(rows, m2, m1, f2, f1, mn, ms, fn_ref, fs_ref):
    width = mn.shape[1] - LANES
    pad = m1.shape[1]
    ty, count = lax.axis_index("ty"), lax.axis_size("ty")
    fn = jnp.where(ty < count - 1, fn_ref[...], 0.0)
    fs = jnp.where(ty > 0, fs_ref[...], 0.0)
    mw, me = roles(m1[...], padded(m2[...], pad))
    fw, fe = roles(f1[...], padded(f2[...], pad))
    hi = rows - (pad - LANES)
    last = LANES - 1
    lane = lax.broadcasted_iota(jnp.int32, (MSG, LANES), 1)

    def ended(msg, block, at):
        end = msg[:, pad - LANES :]
        end = jnp.where(lane == hi, rolled(fn[:, block : block + LANES], hi - at, 1), end)
        end = jnp.where(lane == last, rolled(fs[:, block : block + LANES], last - at, 1), end)
        return jnp.concatenate([msg[:, : pad - LANES], end], axis=1)

    low_w, high_w = ended(fw, width, last), ended(mw, 0, 0)
    low_e, high_e = ended(me, width - LANES, last), ended(fe, width, 0)
    return (fs, ms[...]), (mn[...], fn), (low_w, high_w), (low_e, high_e)


def line_metric(lines, rows, width):
    ax = metric((lines + lax.axis_index("ty") * rows).astype(F32), rows * lax.axis_size("ty"))
    return jnp.concatenate([ax] * (width // LANES), axis=1)


def column_metric(rows, pad):
    first = (lax.axis_index("ty") * rows).astype(F32)
    row = lax.broadcasted_iota(jnp.int32, (8, pad), 1).astype(F32) + first
    return metric(jnp.minimum(row, first + rows), rows * lax.axis_size("ty"))


def strips(rows, *refs):
    ws = omegas(2)
    line = lax.broadcasted_iota(jnp.int32, (8, LANES), 0) // 2
    south, north, west, east_ = strip_lines(rows, *refs)
    width, pad = south[0].shape[1], west[0].shape[1]
    out = [
        strip_sweep(*pair, ws, AY, line_metric(line + start, rows, width))
        for pair, start in ((south, -2), (north, rows - 2))
    ]
    ax = column_metric(rows, pad)
    return out + [strip_sweep(*pair, ws, ax, AY) for pair in (west, east_)]


def pair_variance(a, b, ws, g_across, g_along):
    sides = (*a, *b)

    def field(at):
        return jnp.concatenate([x[at : at + 2] for x in sides], axis=0)

    def single(at):
        return jnp.concatenate([x[at : at + 1] for x in sides for _ in range(2)], axis=0)

    zr, zi = field(0), field(2)
    r, d, m = single(12), single(13), single(14)
    w2 = 2.0 * strip_omega(zr.shape, ws)
    up = lambda x: rolled(x, -2, 0)
    nx = lambda x: rolled(x, -1, 1)
    coef_a = (THETA * g_across * g_across) * (m * up(m) * (d + up(d)))
    coef_l = (THETA * g_along * g_along) * (m * nx(m) * (d + nx(d)))
    inner = face(zr, zi, up(zr), up(zi), r + up(r), coef_a, w2)
    low_line = lax.rem(lax.broadcasted_iota(jnp.int32, zr.shape, 0) // 2, 2) == 0
    sa = sl = None
    along = face(zr, zi, nx(zr), nx(zi), r + nx(r), coef_l, w2)
    for p in range(2):
        outer = field(4 + 2 * p)
        both = jnp.where(low_line, inner[p], outer) + jnp.where(low_line, outer, rolled(inner[p], 2, 0))
        other = along[p] + rolled(along[p], 1, 1)
        sa = both * both if sa is None else sa + both * both
        sl = other * other if sl is None else sl + other * other
    inv = recip(jnp.maximum(d, TINY_DEPTH))
    ia = recip(THETA * g_across)
    il = recip(THETA * g_along)
    var = 0.125 * (ia * ia * sa + il * il * sl) * (inv * inv)
    return var + rolled(var, -1, 0)


def rim_kernel(rows, after, *refs):
    del after
    *refs, row_sums, col_sums = refs
    ws = omegas(2)
    south, north, west, east_ = strip_lines(rows, *refs)
    width, pad = row_sums.shape[1], west[0].shape[1]
    index = lax.broadcasted_iota(jnp.int32, (8, LANES), 0)
    line = lax.rem(index // 2, 2) - 1 + index // 4 * rows
    var = pair_variance(south, north, ws, AY, line_metric(line, rows, south[0].shape[1]))
    for k in range(4):
        row_sums[k, :] = var[2 * k, :width]
    var = pair_variance(west, east_, ws, column_metric(rows, pad), AY)
    for k in range(4):
        col_sums[k // 2, k % 2 * pad : (k % 2 + 1) * pad] = var[2 * k, :]
    col_sums[2:, :] = jnp.zeros((2, width), F32)


def strips_kernel(rows, *refs):
    for out, (held, _) in zip(refs[-4:], strips(rows, *refs[:-4])):
        for k, x in enumerate(held):
            out[8 * k : 8 * k + 8, :] = x


def rim(rows, late, *messages):
    width = late.shape[1]
    return pl.pallas_call(
        functools.partial(rim_kernel, rows),
        out_shape=(pltpu.VMEM((4, width), F32),) * 2,
        in_specs=[pl.BlockSpec(memory_space=pltpu.VMEM)] * 9,
        out_specs=[pl.BlockSpec(memory_space=pltpu.VMEM)] * 2,
        compiler_params=PARAMS,
        name="rim",
    )(*map(vmem, (late, *messages)))


def stack_kernel(a, b, out):
    out[: a.shape[0], :] = a[...]
    out[a.shape[0] :, :] = b[...]


def stacked(a, b):
    return pl.pallas_call(
        stack_kernel,
        out_shape=pltpu.VMEM((a.shape[0] + b.shape[0], a.shape[1]), F32),
        in_specs=[pl.BlockSpec(memory_space=pltpu.VMEM)] * 2,
        out_specs=pl.BlockSpec(memory_space=pltpu.VMEM),
        compiler_params=PARAMS,
        name="stacked",
    )(vmem(a), vmem(b))


def held_strips(rows, *messages):
    row = pltpu.VMEM((48, messages[4].shape[1]), F32)
    col = pltpu.VMEM((48, messages[1].shape[1]), F32)
    return pl.pallas_call(
        functools.partial(strips_kernel, rows),
        out_shape=(row, row, col, col),
        in_specs=[pl.BlockSpec(memory_space=pltpu.VMEM)] * 8,
        out_specs=[pl.BlockSpec(memory_space=pltpu.VMEM)] * 4,
        compiler_params=PARAMS,
        name="held_strips",
    )(*map(vmem, messages))


def prepare_kernel(e1_in, q, m, ss, sn, sw, se, du, dv, base, e1, cols):
    kdev, _, rows, width = e1_in.shape
    size = 24
    ws = omegas(kdev)
    e1[...] = e1_in[...]
    for p in range(2):
        cols[2 * p : 2 * p + 2, :] = sw[8 * (4 + p) + 4 : 8 * (4 + p) + 6, :]
        cols[4 + 2 * p : 6 + 2 * p, :] = se[8 * (4 + p) + 2 : 8 * (4 + p) + 4, :]
    turned = cols[...].T
    lane = lax.broadcasted_iota(jnp.int32, (rows, LANES), 1)
    left, right = slice(0, LANES), slice(width - LANES, width)
    last = LANES - 1
    for p in range(2):
        for c in range(kdev):
            e1[c, p, 0:1, :] = ss[8 * (4 + p) + 4 + c : 8 * (4 + p) + 5 + c, :width]
            e1[c, p, rows - 1 : rows, :] = sn[8 * (4 + p) + 2 + c : 8 * (4 + p) + 3 + c, :width]
            k = 2 * p + c
            e1[c, p, :, left] = jnp.where(lane == 0, rolled(turned[:rows], -k, 1), e1[c, p, :, left])
            k = 4 + 2 * p + c
            e1[c, p, :, right] = jnp.where(lane == last, rolled(turned[:rows], last - k, 1), e1[c, p, :, right])
    for at in range(0, rows, size):
        nxt = min(at + size, rows - 8)
        here = slice(at, at + size)
        md = m[here, :]
        for c in range(kdev):
            wt = THETA * ws[c]
            er, ern = tile_rows(e1.at[c, 0], at, size, nxt)
            ei, ein = tile_rows(e1.at[c, 1], at, size, nxt)
            qr, qrn = tile_rows(q.at[c, 0], at, size, nxt)
            qi, qin = tile_rows(q.at[c, 1], at, size, nxt)
            zr, zi = er - qr, ei - qi
            du[c, 0, here, :] = zr - east(zr)
            du[c, 1, here, :] = zi - east(zi)
            dv[c, 0, here, :] = zr - (ern - qrn)
            dv[c, 1, here, :] = zi - (ein - qin)
            base[c, 0, here, :] = md * (er + wt * ei)
            base[c, 1, here, :] = md * (ei - wt * er)


def prepare(e1, q, m, ss, sn, sw, se):
    plane = pltpu.VMEM(e1.shape, F32)
    return pl.pallas_call(
        prepare_kernel,
        out_shape=(plane, plane, plane),
        in_specs=[pl.BlockSpec(memory_space=pltpu.VMEM)] * 7,
        out_specs=[pl.BlockSpec(memory_space=pltpu.VMEM)] * 3,
        scratch_shapes=[pltpu.VMEM(e1.shape, F32), pltpu.VMEM((LANES, sw.shape[1]), F32)],
        compiler_params=PARAMS,
        cost_estimate=pl.CostEstimate(flops=40 * e1.size, bytes_accessed=160 * e1.size, transcendentals=0),
        name="prepare",
    )(*map(vmem, (e1, q, m, ss, sn, sw, se)))


def rate(var, d):
    s = var + BACKGROUND
    return (DRAG * (s * lax.rsqrt(s))) * recip(d)


def sweep_tile(row, size, r, r_north, du, dv, base, coef, m, turned, ws, last_v, top):
    kdev, width = du.shape[0], du.shape[3]
    here = pl.ds(row, size)
    edges = turned[here, :]
    md = m[here, :]
    coef_u, coef_v = coef[0, here, :], coef[1, here, :]
    r2u = r + east(r)
    r2v = r + r_north
    squ, sqv = r2u * r2u, r2v * r2v
    lane = lax.broadcasted_iota(jnp.int32, (size, LANES), 1)
    last = LANES - 1

    def with_east(u, k):
        block = jnp.where(lane == last, rolled(edges, last - k, 1), u[:, width - LANES :])
        return jnp.concatenate([u[:, : width - LANES], block], axis=1)

    def from_west(u, k):
        u = rolled(u, 1, 1)
        block = jnp.where(lane == 0, rolled(edges, -k, 1), u[:, :LANES])
        return jnp.concatenate([block, u[:, LANES:]], axis=1)

    planes, out_v = {}, {}
    for c in range(kdev):
        w2 = 2.0 * ws[c]
        gu = coef_u * recip(squ + w2 * w2)
        gv = coef_v * recip(sqv + w2 * w2)
        u = flux(du[c, 0, here, :], du[c, 1, here, :], gu, gu * r2u, w2)
        v = flux(dv[c, 0, here, :], dv[c, 1, here, :], gv, gv * r2v, w2)
        for p in range(2):
            up, vp = with_east(u[p], 4 + 2 * p + c), v[p]
            if top is not None:
                vp = jnp.concatenate([vp[:-1], top(c, p, vp[-1:])], axis=0)
            uw = from_west(up, 2 * p + c)
            vs = jnp.concatenate([last_v[c, p], vp[:-1]], axis=0)
            out_v[c, p] = vp[-1:]
            planes[c, p] = base[c, p, here, :], md * ((up - uw) + (vp - vs))
    return planes, out_v


def pairs(kdev):
    return [(c, p) for c in range(kdev) for p in range(2)]


def half_rate(var, rims, turned, d, row, low, half):
    here = pl.ds(row, half)
    edges = turned[here, :]
    width = var.shape[1]
    index = lax.broadcasted_iota(jnp.int32, (8, width), 0)
    first = jnp.where(low & (index == 0), rims[1:2], var[:8])
    final = jnp.where(jnp.logical_not(low) & (index == 7), rims[2:3], var[half - 8 :])
    var = jnp.concatenate([first, var[8 : half - 8], final], axis=0)
    lane = lax.broadcasted_iota(jnp.int32, (half, LANES), 1)
    left = jnp.where(lane == 0, rolled(edges, -8, 1), var[:, :LANES])
    right = jnp.where(lane == LANES - 1, rolled(edges, LANES - 1 - 9, 1), var[:, width - LANES :])
    return rate(jnp.concatenate([left, var[:, LANES : width - LANES], right], axis=1), d[here, :])


def own_kernel(du, dv, base, coef, d, m, late, rims_ref, ss, sn, sw, se, *refs):
    *mine, first_part, update, fric, vs_out, vn_out, turned, cols = refs
    kdev, _, half, width = update.shape
    pad = sw.shape[1]
    ws = omegas(kdev)
    core = lax.rem(lax.axis_index("cons"), 2)
    low = core == 0
    rims = rims_ref[...]

    def edge(strip, var_a, var_b):
        zr, zi, dep, ca = (strip[8 * k : 8 * k + 8, :] for k in range(4))
        var = jnp.concatenate([var_a, var_a, var_a, var_a, var_b, var_b, var_b, var_b], axis=0)
        f = rate(var, jnp.maximum(dep, TINY_DEPTH))
        up = lambda x: rolled(x, -2, 0)
        w2 = 2.0 * strip_omega(zr.shape, ws)
        return face(zr, zi, up(zr), up(zi), f + up(f), ca, w2)

    none = jnp.zeros((1, LANES), F32)
    wide = lambda x: jnp.concatenate([x, none], axis=1)
    south = edge(ss, wide(rims[0:1]), wide(rims[1:2]))
    north = edge(sn, wide(rims[2:3]), wide(rims[3:4]))
    west = edge(sw, rims[4:5, :pad], rims[4:5, pad : 2 * pad])
    east_ = edge(se, rims[5:6, :pad], rims[5:6, pad : 2 * pad])
    for p in range(2):
        cols[2 * p : 2 * p + 2, :] = west[p][2:4]
        cols[4 + 2 * p : 6 + 2 * p, :] = east_[p][2:4]
        for c in range(kdev):
            vs_out[2 * c + p : 2 * c + p + 1, :] = south[p][2 + c : 3 + c, :width]
            vn_out[2 * c + p : 2 * c + p + 1, :] = north[p][2 + c : 3 + c, :width]
    cols[8:9, :] = rims[4:5, pad : 2 * pad]
    cols[9:10, :] = rims[5:6, :pad]
    turned[...] = cols[...].T

    first = pl.multiple_of(core * half, 8)
    var = jnp.concatenate([x[...] for x in mine] + [late[:8, :]], axis=0)
    fric[...] = half_rate(var, rims, turned, d, first, low, half)
    size = half
    last_v = {(c, p): jnp.where(low, vs_out[2 * c + p : 2 * c + p + 1, :], 0.0) for c, p in pairs(kdev)}

    def top(c, p, own):
        return jnp.where(low, 0.0, vn_out[2 * c + p : 2 * c + p + 1, :])

    for at in range(0, half, size):
        r, rn = tile_rows(fric, at, size, min(at + size, half - 8))
        planes, last_v = sweep_tile(
            pl.multiple_of(first + at, 8), size, r, rn, du, dv, base, coef, m, turned, ws, last_v,
            top if at + size == half else None,
        )
        for c, p in pairs(kdev):
            first_part[c, p, at : at + size, :], update[c, p, at : at + size, :] = planes[c, p]


def own_half(*args):
    kdev, _, rows, width = args[0].shape
    pad = args[10].shape[1]
    line = pltpu.VMEM((8, width), F32)
    return pl.pallas_call(
        own_kernel,
        out_shape=(
            pltpu.VMEM((kdev, 2, rows // 2, width), F32),
            pltpu.VMEM((kdev, 2, rows // 2, width), F32),
            pltpu.VMEM((rows // 2, width), F32),
            line,
            line,
            pltpu.VMEM((pad, LANES), F32),
        ),
        in_specs=[pl.BlockSpec(memory_space=pltpu.VMEM)] * len(args),
        out_specs=[pl.BlockSpec(memory_space=pltpu.VMEM)] * 6,
        scratch_shapes=[pltpu.VMEM((LANES, pad), F32)],
        compiler_params=PARAMS,
        name="own_half",
    )(*map(vmem, args))


def other_kernel(du, dv, base, coef, d, m, late, rims, eta_own, fric_own, vs, vn, turned, *refs):
    *other, eta_out, fric_out, eta, fric, fixed, sems = refs
    kdev, _, half, width = eta.shape
    ws = omegas(kdev)
    core = lax.rem(lax.axis_index("cons"), 2)
    own_low = core == 0
    own, first = pl.multiple_of(core * half, 8), pl.multiple_of((1 - core) * half, 8)
    copies = []

    def put(src, dst):
        copy = pltpu.make_async_copy(src, dst, sems.at[len(copies)])
        copy.start()
        copies.append(copy)

    skip = pl.multiple_of(core * 8, 8)
    put(
        eta_own.at[:, :, pl.ds(skip, half - 8), :],
        eta_out.at[:, :, pl.ds(pl.multiple_of(own + skip, 8), half - 8), :],
    )
    fric[pl.ds(own, half), :] = fric_own[...]
    fric[pl.ds(first, half), :] = half_rate(
        jnp.concatenate([x[...] for x in other] + [late[8:, :]], axis=0),
        rims[...], turned, d, first, jnp.logical_not(own_low), half,
    )
    put(fric, fric_out)

    r, rn = tile_rows(fric, half - 8, 8, half)
    r2 = r + rn
    between = {}
    for c in range(kdev):
        w2 = 2.0 * ws[c]
        g = coef[1, half - 8 : half, :] * recip(r2 * r2 + w2 * w2)
        v = flux(dv[c, 0, half - 8 : half, :], dv[c, 1, half - 8 : half, :], g, g * r2, w2)
        for p in range(2):
            between[c, p] = v[p][7:8]
    index = lax.broadcasted_iota(jnp.int32, (8, width), 0)
    at_face = index == jnp.where(own_low, 7, 0)
    sign = jnp.where(own_low, -1.0, 1.0)
    local = pl.ds(pl.multiple_of((1 - core) * (half - 8), 8), 8)
    border = pl.ds(pl.multiple_of(half - 8 + 8 * core, 8), 8)
    md = m[border, :]
    for c, p in pairs(kdev):
        fixed[c, p] = eta_own[c, p, local, :] + jnp.where(at_face, sign * (md * between[c, p]), 0.0)
    put(fixed, eta_out.at[:, :, border, :])

    size = 24
    rows = 2 * half
    last_v = {(c, p): jnp.where(own_low, between[c, p], vs[2 * c + p : 2 * c + p + 1, :]) for c, p in pairs(kdev)}

    def top(c, p, own_v):
        return jnp.where(own_low, vn[2 * c + p : 2 * c + p + 1, :], own_v)

    for at in range(0, half, size):
        row = pl.multiple_of(first + at, 8)
        r = fric[pl.ds(row, size), :]
        after = fric[pl.ds(pl.multiple_of(jnp.minimum(row + size, rows - 8), 8), 8), :]
        rn = jnp.concatenate([r[1:], after[0:1]], axis=0)
        planes, last_v = sweep_tile(
            row, size, r, rn, du, dv, base, coef, m, turned, ws, last_v, top if at + size == half else None
        )
        for c, p in pairs(kdev):
            eta[c, p, at : at + size, :] = planes[c, p][0] - planes[c, p][1]
        put(eta.at[:, :, at : at + size, :], eta_out.at[:, :, pl.ds(row, size), :])
    for copy in copies:
        copy.wait()


def other_half(*args):
    du, d = args[0], args[4]
    kdev, _, rows, width = du.shape
    return pl.pallas_call(
        other_kernel,
        out_shape=(jax.ShapeDtypeStruct(du.shape, F32), jax.ShapeDtypeStruct(d.shape, F32)),
        in_specs=[pl.BlockSpec(memory_space=pltpu.VMEM)] * len(args),
        out_specs=[pl.BlockSpec(memory_space=pltpu.HBM)] * 2,
        scratch_shapes=[
            pltpu.VMEM((kdev, 2, rows // 2, width), F32),
            pltpu.VMEM(d.shape, F32),
            pltpu.VMEM((kdev, 2, 8, width), F32),
            pltpu.SemaphoreType.DMA((3 + rows // 2 // 24,)),
        ],
        compiler_params=PARAMS,
        name="other_half",
    )(*map(vmem, args))


def swapped(x, axis, bit):
    return lax.ppermute(x, axis, [(i, i ^ bit) for i in range(lax.axis_size(axis))])


def body(elevation, equilibrium, depth, land_mask, friction_prev):
    rows = depth.shape[0]
    ntx, nty, ncons = (lax.axis_size(a) for a in ("tx", "ty", "cons"))
    fields = (elevation, equilibrium, depth, land_mask, friction_prev)
    m2, m1 = pack_columns(*fields)
    elev, equil, depth, mask, fric = elevation, equilibrium, depth, land_mask, friction_prev
    mask, mn, ms = pack(*fields, m1)
    f2 = lax.ppermute(m2, "tx", [(i, (i - 1 if i % 2 == 0 else i + 1) % ntx) for i in range(ntx)])
    f1 = swapped(m1, "tx", 1)
    e1, send, keep, coef = first_sweep(elev, equil, depth, mask, fric, m1)
    mn, ms, my, send = merge(rows, f1, f2, mn, ms, send)
    recv = swapped(send, "cons", 1)
    if nty == 2:
        fn = fs = swapped(my, "ty", 1)
    else:
        fn = lax.ppermute(ms, "ty", [(i, i - 1) for i in range(1, nty)])
        fs = lax.ppermute(mn, "ty", [(i, i + 1) for i in range(nty - 1)])
    first, second, late = cut_sum(recv, keep, my)
    messages = (m2, m1, f2, f1, mn, ms, fn, fs)
    rims = jnp.concatenate(rim(rows, late, *messages), axis=0)
    tail = stacked(late, rims)
    ss, sn, sw, se = held_strips(rows, *messages)
    prepared = prepare(e1, equil, mask, ss, sn, sw, se)
    partner = [swapped(x, "cons", 2) for x in (first, second, tail)]
    others = [swapped(rims, "cons", k) for k in range(1, ncons) if k != 2]
    both = added(rims, others[0], prepared[2])
    mine = early_sums((first, second), partner[:2], both)
    bit = 4
    while bit < ncons:
        mine = [added(x, swapped(x, "cons", bit)) for x in mine]
        tail, partner[2] = added(tail, partner[2]), swapped(added(tail, partner[2]), "cons", bit)
        bit *= 2
    other = [swapped(x, "cons", 1) for x in mine]
    late, rims = joined(tail, partner[2], both, other[0], *others[1:])
    fields = (*prepared, coef, depth, mask, late, rims)
    first_part, update, *own = own_half(*fields, ss, sn, sw, se, *mine)
    return other_half(*fields, first_part - update, *own, *other)


def solution(mesh):
    return jax.shard_map(
        body,
        mesh=mesh,
        in_specs=(
            P("cons", None, "ty", "tx"),
            P("cons", None, "ty", "tx"),
            P("ty", "tx"),
            P("ty", "tx"),
            P("ty", "tx"),
        ),
        out_specs=(P("cons", None, "ty", "tx"), P("ty", "tx")),
        check_vma=False,
    )
```
